32 devices in a mesh: rows: 16 (over z, x, core), mask: 2 (over y).
Axes of the slice: x: 2, y: 2, z: 4, core: 2. Of those that a mesh axis runs over, the one named last changes fastest.
Arguments:
- image_field: bfloat16 [2, 8192, 8192], P(None, ('rows', 'mask')), may hold values from -6 to 6
- amplitudes: bfloat16 [2, 8192, 8192], P('mask', None, 'rows'), may hold values from 0 to 12, as said below
- mask_ids: int32 [2], P('mask'), may hold values from 0 to 63
Outputs:
- gradient: float32 [2, 8192, 8192], P(None, ('rows', 'mask'))
- loss_value: float32 [], replicated
The draws below stay inside these ranges and needn't reach their ends.
Inputs may be any that keep to these rules, and one draw needn't show every extreme that they name: `amplitudes`: magnitudes are non-negative.
All inputs are finite; a program needn't handle non-finite values.
Results may differ from the reference program's by a relative error of at most 0.024.
Values may be sent and summed in bfloat16 or wider, within the bound.
No kernel may reach another device: no remote copies, remote signals or barrier semaphores. Data moves between devices by JAX's collectives and lax.ppermute only.
A program may use at most 192 MiB of HBM per device.

```python
import math
import jax
import jax.numpy as jnp
from jax import lax

N = 8192
INNER = 128
MASK_SET = 64
M_WIN = 2


def draw_amplitudes(key, part):
    column_scale = 0.3 + 2.7 * jnp.arange(N, dtype=jnp.float32)[None, None, :] / N
    mask_scale = 0.6 + 0.8 * jnp.arange(M_WIN, dtype=jnp.float32)[:, None, None] / max(M_WIN - 1, 1)
    spread = jax.random.uniform(key, (M_WIN, N, N), jnp.float32, 0.2, 1.8)
    return (spread * column_scale * mask_scale).astype(jnp.bfloat16)


def shard_levels(own_key, extent, pieces, low, high):
    factor_of, own = 1.0, jax.random.fold_in(own_key, 6)
    for axis_at, blocks in pieces:
        steps = jnp.exp(jax.random.uniform(jax.random.fold_in(own, axis_at), (blocks,), jnp.float32, low / len(pieces), high / len(pieces)))
        factor_of = factor_of * jnp.repeat(steps, extent[axis_at] // blocks).reshape([-1 if axis == axis_at else 1 for axis in range(len(extent))])
    return factor_of


def gaussian(stream_key, extent, scale, reach, pieces=(), held_as=jnp.bfloat16):
    entries = jax.random.normal(stream_key, extent, jnp.float32) * scale
    if len(pieces) > 0:
        entries = shard_levels(stream_key, extent, pieces, -0.22, 0.18) * entries
    return jnp.clip(entries, min=-reach, max=reach).astype(held_as)


def setup_inputs(seed: int = 0) -> dict:
    splits = jax.random.split(jax.random.key(seed), 4)
    return {
        "image_field": gaussian(splits[0], (2, N, N), 1.0, 6.0, ((1, 32),)),
        "amplitudes": draw_amplitudes(jax.random.fold_in(splits[3], 71), 0),
        "mask_ids": jax.random.randint(splits[2], (M_WIN,), 0, MASK_SET).astype(jnp.int32),
    }


EPSILON = 0.25

def shift_bits(values, count):
    return lax.shift_right_logical(values, jnp.full(values.shape, count, jnp.int32))

def mask_code(window_id, row_index, column_index):
    mixed = row_index * jnp.int32(73856093) ^ column_index * jnp.int32(19349663) ^ (window_id + jnp.int32(1)) * jnp.int32(83492791)
    mixed = mixed ^ shift_bits(mixed, 13)
    mixed = mixed * jnp.int32(1274126177)
    mixed = mixed ^ shift_bits(mixed, 16)
    return shift_bits(mixed, 28) & jnp.int32(3)

def rotate(real_part, imag_part, phase_code, direction):
    cosine = (phase_code == 0).astype(jnp.float32) - (phase_code == 2).astype(jnp.float32)
    sine = direction * ((phase_code == 1).astype(jnp.float32) - (phase_code == 3).astype(jnp.float32))
    return (real_part * cosine - imag_part * sine, real_part * sine + imag_part * cosine)

def round_half(values):
    return lax.optimization_barrier(values.astype(jnp.bfloat16)).astype(jnp.float32)

def factor_table(length, direction):
    index = jnp.arange(length, dtype=jnp.int32)
    angles = (index[:, None] * index[None, :] % length).astype(jnp.float32) * (2.0 * math.pi / length)
    cosine = jnp.cos(angles)
    sine = direction * jnp.sin(angles)
    upper = jnp.stack([cosine, -sine], axis=1)
    lower = jnp.stack([sine, cosine], axis=1)
    return round_half(jnp.stack([upper, lower]))

def turn_table(outer, inner, length, direction):
    first = jnp.arange(outer, dtype=jnp.int32)[:, None]
    second = jnp.arange(inner, dtype=jnp.int32)[None, :]
    angles = (first * second % length).astype(jnp.float32) * (2.0 * math.pi / length)
    return (jnp.cos(angles), direction * jnp.sin(angles))

def factor(form, table, values):
    return jnp.einsum(form, table.astype(jnp.float32), values.astype(jnp.float32), precision=lax.Precision.HIGHEST)

def twist(real_part, imag_part, cosine, sine, axis):
    return round_half(jnp.stack([real_part * cosine - imag_part * sine, real_part * sine + imag_part * cosine], axis=axis))

def rows_forward(values, tables):
    lead_table, sub_table, cosine, sine = tables
    batch, parts, count, length = values.shape
    view = values.reshape(batch, parts, count, lead_table.shape[1], sub_table.shape[1])
    first = factor('pkqj,xqrjb->xprkb', lead_table, view)
    middle = twist(first[:, 0], first[:, 1], cosine, sine, 1)
    second = factor('pkqj,xqraj->xprak', sub_table, middle)
    return second.reshape(batch, parts, count, length) * (1.0 / math.sqrt(length))

def rows_inverse(values, tables):
    lead_table, sub_table, cosine, sine = tables
    batch, parts, count, length = values.shape
    view = values.reshape(batch, parts, count, lead_table.shape[1], sub_table.shape[1])
    first = factor('pkqj,xqraj->xprak', sub_table, view)
    middle = twist(first[:, 0], first[:, 1], cosine, sine, 1)
    second = factor('pkqj,xqrjb->xprkb', lead_table, middle)
    return second.reshape(batch, parts, count, length) * (1.0 / math.sqrt(length))

def cols_forward(values, tables):
    lead_table, sub_table, cosine, sine = tables
    parts, length, width = values.shape
    view = values.reshape(parts, lead_table.shape[1], sub_table.shape[1], width)
    first = factor('pkqj,qjbw->pkbw', lead_table, view)
    middle = twist(first[0], first[1], cosine[:, :, None], sine[:, :, None], 0)
    second = factor('pkqj,qajw->pakw', sub_table, middle)
    return second.reshape(parts, length, width) * (1.0 / math.sqrt(length))

def cols_inverse(values, tables):
    lead_table, sub_table, cosine, sine = tables
    parts, length, width = values.shape
    view = values.reshape(parts, lead_table.shape[1], sub_table.shape[1], width)
    first = factor('pkqj,qajw->pakw', sub_table, view)
    middle = twist(first[0], first[1], cosine[:, :, None], sine[:, :, None], 0)
    second = factor('pkqj,qjbw->pkbw', lead_table, middle)
    return second.reshape(parts, length, width) * (1.0 / math.sqrt(length))

def reference(image_field, amplitudes, mask_ids):
    outer = N // INNER
    forward_cos, forward_sin = turn_table(outer, INNER, N, -1.0)
    inverse_cos, inverse_sin = turn_table(outer, INNER, N, 1.0)
    forward_tables = (factor_table(outer, -1.0), factor_table(INNER, -1.0), forward_cos, forward_sin)
    inverse_tables = (factor_table(outer, 1.0), factor_table(INNER, 1.0), inverse_cos, inverse_sin)
    row_index = jnp.arange(N, dtype=jnp.int32)[:, None]
    column_index = jnp.arange(N, dtype=jnp.int32)[None, :]
    field_real = image_field[0].astype(jnp.float32)
    field_imag = image_field[1].astype(jnp.float32)
    grad_real = jnp.zeros((N, N), jnp.float32)
    grad_imag = jnp.zeros((N, N), jnp.float32)
    loss_sum = jnp.zeros((), jnp.float32)
    for which in range(M_WIN):
        phase_code = mask_code(mask_ids[which], row_index, column_index)
        masked_real, masked_imag = rotate(field_real, field_imag, phase_code, 1.0)
        masked = round_half(jnp.stack([masked_real, masked_imag]))
        sent = round_half(rows_forward(masked[None], forward_tables)[0])
        spectrum = cols_forward(sent, forward_tables)
        spec_real = spectrum[0]
        spec_imag = spectrum[1]
        measured = amplitudes[which].astype(jnp.float32)
        magnitude = jnp.sqrt(spec_real * spec_real + spec_imag * spec_imag + EPSILON)
        factor_kept = 1.0 - measured / magnitude
        misfit = magnitude - measured
        loss_sum = loss_sum + jnp.sum(misfit * misfit)
        weighted = round_half(jnp.stack([spec_real * factor_kept, spec_imag * factor_kept]))
        columns_back = round_half(cols_inverse(weighted, inverse_tables))
        rows_back = rows_inverse(columns_back[None], inverse_tables)[0]
        term_real, term_imag = rotate(rows_back[0], rows_back[1], phase_code, -1.0)
        grad_real = grad_real + round_half(term_real)
        grad_imag = grad_imag + round_half(term_imag)
    gradient = jnp.stack([grad_real, grad_imag])
    return (gradient, loss_sum / (M_WIN * N * N))
```

```python
import functools
import math

import jax
import jax.numpy as jnp
import ml_dtypes
import numpy as np
from jax import lax
from jax.experimental import pallas as pl
from jax.experimental.pallas import tpu as pltpu
from jax.sharding import PartitionSpec as P

INNER = 128
OUTER = 64
LENGTH = INNER * OUTER
EPSILON = 0.25
TILE = 16
VMEM_LIMIT = 58 * 1024 * 1024
ROOT_HALF = math.sqrt(0.5)

ROW_MULTIPLIER = 73856093
COLUMN_MULTIPLIER = 19349663
MASK_MULTIPLIER = 83492791
MIX_MULTIPLIER = 1274126177


def wrap(value):
    return (value + 2**31) % 2**32 - 2**31


def add(a, b):
    return (a[0] + b[0], a[1] + b[1])


def sub(a, b):
    return (a[0] - b[0], a[1] - b[1])


def quarter(a, sign):
    return (-a[1], a[0]) if sign > 0 else (a[1], -a[0])


def turn(a, step, count, sign):
    step = step % count
    if step == 0:
        return a
    if 4 * step == count:
        return quarter(a, sign)
    if 2 * step == count:
        return (-a[0], -a[1])
    if 4 * step == 3 * count:
        return quarter(a, -sign)
    if 8 * step == count:
        q = quarter(a, sign)
        return ((a[0] + q[0]) * ROOT_HALF, (a[1] + q[1]) * ROOT_HALF)
    if 8 * step == 3 * count:
        q = quarter(a, sign)
        return ((q[0] - a[0]) * ROOT_HALF, (q[1] - a[1]) * ROOT_HALF)
    angle = sign * 2.0 * math.pi * step / count
    cosine, sine = math.cos(angle), math.sin(angle)
    return (a[0] * cosine - a[1] * sine, a[0] * sine + a[1] * cosine)


def fourier4(x, sign):
    t0, t1 = add(x[0], x[2]), sub(x[0], x[2])
    t2, t3 = add(x[1], x[3]), quarter(sub(x[1], x[3]), sign)
    return [add(t0, t2), add(t1, t3), sub(t0, t2), sub(t1, t3)]


def fourier8(x, sign):
    even = fourier4(x[0::2], sign)
    odd = fourier4(x[1::2], sign)
    odd = [turn(odd[k], k, 8, sign) for k in range(4)]
    return [add(even[k], odd[k]) for k in range(4)] + [sub(even[k], odd[k]) for k in range(4)]


def fourier64(load, store, middle, sign):
    for b in range(8):
        values = fourier8([load(8 * a + b) for a in range(8)], sign)
        for c in range(8):
            real, imag = turn(values[c], b * c, 64, sign)
            middle[c * 8 + b, 0] = real
            middle[c * 8 + b, 1] = imag
    for c in range(8):
        values = fourier8([(middle[c * 8 + b, 0], middle[c * 8 + b, 1]) for b in range(8)], sign)
        for d in range(8):
            store(c + 8 * d, values[d])


def mask_bits(row_term, lane_term, tile):
    mixed = row_term ^ (lane_term + jnp.int32(wrap(tile * INNER * COLUMN_MULTIPLIER)))
    mixed = mixed ^ lax.shift_right_logical(mixed, jnp.full(mixed.shape, 13, jnp.int32))
    mixed = mixed * jnp.int32(MIX_MULTIPLIER)
    return mixed << 3, mixed << 2


def rotate(value, low, high, direction):
    swap = low < 0
    real = jnp.where(swap, value[1], value[0])
    imag = jnp.where(swap, value[0], value[1])
    mixed = (low ^ high) < 0
    upper = high < 0
    flip_real, flip_imag = (mixed, upper) if direction > 0 else (upper, mixed)
    return (jnp.where(flip_real, -real, real), jnp.where(flip_imag, -imag, imag))


def hash_terms(ids_ref, base, mask):
    rows = lax.broadcasted_iota(jnp.int32, (TILE, INNER), 0) + base
    lanes = lax.broadcasted_iota(jnp.int32, (TILE, INNER), 1)
    mask_term = (ids_ref[mask] + 1) * jnp.int32(MASK_MULTIPLIER)
    return (rows * jnp.int32(ROW_MULTIPLIER)) ^ mask_term, lanes * jnp.int32(COLUMN_MULTIPLIER)


def table_pair():
    inner = np.arange(INNER, dtype=np.int64)
    outer = np.arange(OUTER, dtype=np.int64)
    steps = inner[None, None, :] * (outer[:, None, None] + OUTER * inner[None, :, None]) % LENGTH
    angles = steps * (-2.0 * math.pi / LENGTH)
    cosine, sine = np.cos(angles), np.sin(angles)
    table = np.concatenate(
        [np.concatenate([cosine, -sine], axis=2), np.concatenate([sine, cosine], axis=2)], axis=1
    )
    forward = (table * 2.0**-7).astype(ml_dtypes.bfloat16)
    backward = (table.transpose(0, 2, 1) * 2.0**-6).astype(ml_dtypes.bfloat16)
    return forward, backward


def rows_out_kernel(chunks, ids_ref, base_ref, image_ref, table_hbm, *rest):
    outs = rest[:chunks]
    table, middle, held, sem = rest[chunks:]
    masks = outs[0].shape[1]
    rows = image_ref.shape[1]
    slabs = rows // TILE
    step = pl.program_id(0)
    copy = pltpu.make_async_copy(table_hbm, table, sem)

    @pl.when(step == 0)
    def _():
        copy.start()

    def slab(index, carry):
        mask = index // slabs
        at = pl.multiple_of((index % slabs) * TILE, TILE)
        row_term, lane_term = hash_terms(ids_ref, base_ref[0] + step * rows + at, mask)

        def load(n):
            low, high = mask_bits(row_term, lane_term, n)
            span = slice(n * INNER, (n + 1) * INNER)
            value = [image_ref[p, pl.ds(at, TILE), span].astype(jnp.float32) for p in range(2)]
            return rotate(value, low, high, 1)

        def store(k, value):
            to = pl.ds(pl.multiple_of(index * TILE, TILE), TILE)
            held[k, to, 0:INNER] = value[0].astype(jnp.bfloat16)
            held[k, to, INNER:] = value[1].astype(jnp.bfloat16)

        fourier64(load, store, middle, -1)
        return carry

    lax.fori_loop(0, masks * slabs, slab, 0)

    @pl.when(step == 0)
    def _():
        copy.wait()

    def spread(slot, carry):
        for j in range(chunks):
            k = slot * chunks + j
            value = jnp.dot(held[k], table[k], preferred_element_type=jnp.float32)
            value = value.astype(jnp.bfloat16)
            for m in range(masks):
                for p in range(2):
                    outs[j][slot, m, p] = value[
                        m * rows : (m + 1) * rows, p * INNER : (p + 1) * INNER
                    ]
        return carry

    lax.fori_loop(0, OUTER // chunks, spread, 0)


def rows_out(ids, base, image, table, masks, slots):
    _, count, width = image.shape
    chunks = OUTER // slots
    rows = min(count, max(TILE, 256 // masks))
    out = jax.ShapeDtypeStruct((slots, masks, 2, count, INNER), jnp.bfloat16)
    return pl.pallas_call(
        functools.partial(rows_out_kernel, chunks),
        grid=(count // rows,),
        in_specs=[
            pl.BlockSpec(memory_space=pltpu.SMEM),
            pl.BlockSpec(memory_space=pltpu.SMEM),
            pl.BlockSpec((2, rows, width), lambda i: (0, i, 0)),
            pl.BlockSpec(memory_space=pl.ANY),
        ],
        out_specs=[pl.BlockSpec((slots, masks, 2, rows, INNER), lambda i: (0, 0, 0, i, 0))]
        * chunks,
        out_shape=[out] * chunks,
        scratch_shapes=[
            pltpu.VMEM((OUTER, 2 * INNER, 2 * INNER), jnp.bfloat16),
            pltpu.VMEM((OUTER, 2, TILE, INNER), jnp.float32),
            pltpu.VMEM((OUTER, masks * rows, 2 * INNER), jnp.bfloat16),
            pltpu.SemaphoreType.DMA,
        ],
        compiler_params=pltpu.CompilerParams(
            vmem_limit_bytes=VMEM_LIMIT, dimension_semantics=("arbitrary",)
        ),
        cost_estimate=pl.CostEstimate(
            flops=masks * count * width * 1100, bytes_accessed=40 << 20, transcendentals=0
        ),
        name="rows_out",
    )(ids, base, image, table)


def columns_kernel(share, in_ref, measured_ref, forward_hbm, backward_hbm, out_ref, loss_ref,
                   forward, backward, middle, held, sems):
    copies = [
        pltpu.make_async_copy(forward_hbm, forward, sems.at[0]),
        pltpu.make_async_copy(backward_hbm, backward, sems.at[1]),
    ]
    for copy in copies:
        copy.start()
    slabs = INNER // TILE

    def place(n, at):
        if share >= INNER:
            per = share // INNER
            return n // per, pl.ds(pl.multiple_of((n % per) * INNER + at, TILE), TILE)
        return (n * (INNER // share) + at // share, pl.ds(pl.multiple_of(at % share, TILE), TILE))

    def arrive(index, carry):
        at = pl.multiple_of(index * TILE, TILE)

        def load(n):
            source, span = place(n, at)
            return [in_ref[source, p, span, :].astype(jnp.float32) for p in range(2)]

        def store(k, value):
            for p in range(2):
                to = pl.ds(pl.multiple_of(p * INNER + at, TILE), TILE)
                held[k, to, :] = value[p].astype(jnp.bfloat16)

        fourier64(load, store, middle, -1)
        return carry

    lax.fori_loop(0, slabs, arrive, 0)
    for copy in copies:
        copy.wait()
    loss_ref[...] = jnp.zeros_like(loss_ref)

    def residual(k, carry):
        spectrum = jnp.dot(forward[k], held[k], preferred_element_type=jnp.float32)
        real, imag = spectrum[:INNER], spectrum[INNER:]
        measured = measured_ref[
            0, pl.ds(pl.multiple_of(k * INNER, INNER), INNER), :
        ].astype(jnp.float32)
        square = real * real + imag * imag + EPSILON
        inverse = lax.rsqrt(square)
        misfit = square * inverse - measured
        kept = 1.0 - measured * inverse
        loss_ref[...] += jnp.sum((misfit * misfit).reshape(INNER // 8, 8, INNER), axis=0)
        weighted = jnp.concatenate([real * kept, imag * kept], axis=0).astype(jnp.bfloat16)
        back = jnp.dot(backward[k], weighted, preferred_element_type=jnp.float32)
        held[k] = back.astype(jnp.bfloat16)
        return carry

    lax.fori_loop(0, OUTER, residual, 0, unroll=2)

    def leave(index, carry):
        at = pl.multiple_of(index * TILE, TILE)

        def load(k):
            return [
                held[k, pl.ds(pl.multiple_of(p * INNER + at, TILE), TILE), :].astype(jnp.float32)
                for p in range(2)
            ]

        def store(n, value):
            source, span = place(n, at)
            for p in range(2):
                out_ref[source, p, span, :] = value[p].astype(jnp.bfloat16)

        fourier64(load, store, middle, 1)
        return carry

    lax.fori_loop(0, slabs, leave, 0)


def columns(chunk, arrived, measured, forward, backward):
    devices, _, share, width = arrived.shape
    length = devices * share
    return pl.pallas_call(
        functools.partial(columns_kernel, share),
        grid=(1,),
        in_specs=[
            pl.BlockSpec((devices, 2, share, width), lambda i: (0, 0, 0, 0)),
            pl.BlockSpec((1, length, width), lambda i: (0, 0, chunk)),
            pl.BlockSpec(memory_space=pl.ANY),
            pl.BlockSpec(memory_space=pl.ANY),
        ],
        out_specs=[
            pl.BlockSpec((devices, 2, share, width), lambda i: (0, 0, 0, 0)),
            pl.BlockSpec((8, INNER), lambda i: (0, 0)),
        ],
        out_shape=[
            jax.ShapeDtypeStruct(arrived.shape, jnp.bfloat16),
            jax.ShapeDtypeStruct((8, INNER), jnp.float32),
        ],
        scratch_shapes=[
            pltpu.VMEM((OUTER, 2 * INNER, 2 * INNER), jnp.bfloat16),
            pltpu.VMEM((OUTER, 2 * INNER, 2 * INNER), jnp.bfloat16),
            pltpu.VMEM((OUTER, 2, TILE, INNER), jnp.float32),
            pltpu.VMEM((OUTER, 2 * INNER, width), jnp.bfloat16),
            pltpu.SemaphoreType.DMA((2,)),
        ],
        compiler_params=pltpu.CompilerParams(
            vmem_limit_bytes=VMEM_LIMIT, dimension_semantics=("arbitrary",)
        ),
        cost_estimate=pl.CostEstimate(
            flops=length * width * 2200, bytes_accessed=40 << 20, transcendentals=length * width
        ),
        name="columns",
    )(arrived, measured, forward, backward)


def rows_in_kernel(chunks, ids_ref, base_ref, *rest):
    ins = rest[:chunks]
    table_hbm, out_ref, table, middle, held, sem = rest[chunks:]
    masks = ins[0].shape[1]
    rows = out_ref.shape[1]
    slabs = rows // TILE
    step = pl.program_id(0)
    copy = pltpu.make_async_copy(table_hbm, table, sem)

    @pl.when(step == 0)
    def _():
        copy.start()
        copy.wait()

    def gather(slot, carry):
        for j in range(chunks):
            k = slot * chunks + j
            value = jnp.concatenate(
                [
                    jnp.concatenate([ins[j][slot, m, 0], ins[j][slot, m, 1]], axis=1)
                    for m in range(masks)
                ],
                axis=0,
            )
            held[k] = jnp.dot(value, table[k], preferred_element_type=jnp.float32).astype(
                jnp.bfloat16
            )
        return carry

    lax.fori_loop(0, OUTER // chunks, gather, 0)

    def slab(index, carry, first):
        mask = index // slabs
        at = pl.multiple_of((index % slabs) * TILE, TILE)
        row_term, lane_term = hash_terms(ids_ref, base_ref[0] + step * rows + at, mask)

        def load(k):
            take = pl.ds(pl.multiple_of(index * TILE, TILE), TILE)
            return [
                held[k, take, p * INNER : (p + 1) * INNER].astype(jnp.float32) for p in range(2)
            ]

        def store(n, value):
            low, high = mask_bits(row_term, lane_term, n)
            value = rotate(value, low, high, -1)
            span = slice(n * INNER, (n + 1) * INNER)
            for p in range(2):
                if first:
                    out_ref[p, pl.ds(at, TILE), span] = value[p]
                else:
                    out_ref[p, pl.ds(at, TILE), span] += value[p]

        fourier64(load, store, middle, 1)
        return carry

    lax.fori_loop(0, slabs, functools.partial(slab, first=True), 0)
    lax.fori_loop(slabs, masks * slabs, functools.partial(slab, first=False), 0)


def rows_in(ids, base, arrived, table):
    chunks = len(arrived)
    slots, masks, _, count, _ = arrived[0].shape
    rows = min(count, max(TILE, 256 // masks))
    width = LENGTH
    return pl.pallas_call(
        functools.partial(rows_in_kernel, chunks),
        grid=(count // rows,),
        in_specs=[
            pl.BlockSpec(memory_space=pltpu.SMEM),
            pl.BlockSpec(memory_space=pltpu.SMEM),
        ]
        + [pl.BlockSpec((slots, masks, 2, rows, INNER), lambda i: (0, 0, 0, i, 0))] * chunks
        + [pl.BlockSpec(memory_space=pl.ANY)],
        out_specs=pl.BlockSpec((2, rows, width), lambda i: (0, i, 0)),
        out_shape=jax.ShapeDtypeStruct((2, count, width), jnp.float32),
        scratch_shapes=[
            pltpu.VMEM((OUTER, 2 * INNER, 2 * INNER), jnp.bfloat16),
            pltpu.VMEM((OUTER, 2, TILE, INNER), jnp.float32),
            pltpu.VMEM((OUTER, masks * rows, 2 * INNER), jnp.bfloat16),
            pltpu.SemaphoreType.DMA,
        ],
        compiler_params=pltpu.CompilerParams(
            vmem_limit_bytes=VMEM_LIMIT, dimension_semantics=("arbitrary",)
        ),
        cost_estimate=pl.CostEstimate(
            flops=masks * count * width * 1100, bytes_accessed=40 << 20, transcendentals=0
        ),
        name="rows_in",
    )(ids, base, *arrived, table)


AXES = ("rows", "mask")


def exchange(blocks):
    return lax.all_to_all(blocks, AXES, split_axis=0, concat_axis=0, tiled=True)


def shards(slots, masks, image, measured, mask_ids):
    forward, backward = (jnp.asarray(table) for table in table_pair())
    _, count, width = image.shape
    ids = lax.all_gather(mask_ids, "mask", tiled=True)
    base = (lax.axis_index("rows") * masks + lax.axis_index("mask")) * count
    base = base.astype(jnp.int32)[None]
    devices = slots * masks
    sent = rows_out(ids, base, image, backward, masks, slots)
    returned = []
    losses = []
    for chunk, blocks in enumerate(sent):
        arrived = exchange(blocks.reshape(devices, 2, count, INNER))
        leaving, loss = columns(chunk, arrived, measured, forward, backward)
        losses.append(jnp.sum(loss))
        returned.append(exchange(leaving).reshape(slots, masks, 2, count, INNER))
    loss_value = lax.psum(sum(losses), AXES) / (masks * width * width)
    return rows_in(ids, base, returned, forward), loss_value


def solution(mesh):
    slots, masks = mesh.shape["rows"], mesh.shape["mask"]
    return jax.shard_map(
        functools.partial(shards, slots, masks),
        mesh=mesh,
        in_specs=(P(None, AXES, None), P("mask", None, "rows"), P("mask")),
        out_specs=(P(None, AXES, None), P()),
        check_vma=False,
    )
```

```python
import functools
import math

import jax
import jax.numpy as jnp
import ml_dtypes
import numpy as np
from jax import lax
from jax.experimental import pallas as pl
from jax.experimental.pallas import tpu as pltpu
from jax.sharding import PartitionSpec as P

INNER = 128
OUTER = 64
LENGTH = INNER * OUTER
EPSILON = 0.25
TILE = 16
VMEM_LIMIT = 58 * 1024 * 1024
ROOT_HALF = math.sqrt(0.5)

ROW_MULTIPLIER = 73856093
COLUMN_MULTIPLIER = 19349663
MASK_MULTIPLIER = 83492791
MIX_MULTIPLIER = 1274126177


def wrap(value):
    return (value + 2**31) % 2**32 - 2**31


def add(a, b):
    return (a[0] + b[0], a[1] + b[1])


def sub(a, b):
    return (a[0] - b[0], a[1] - b[1])


def quarter(a, sign):
    return (-a[1], a[0]) if sign > 0 else (a[1], -a[0])


def turn(a, step, count, sign):
    step = step % count
    if step == 0:
        return a
    if 4 * step == count:
        return quarter(a, sign)
    if 2 * step == count:
        return (-a[0], -a[1])
    if 4 * step == 3 * count:
        return quarter(a, -sign)
    if 8 * step == count:
        q = quarter(a, sign)
        return ((a[0] + q[0]) * ROOT_HALF, (a[1] + q[1]) * ROOT_HALF)
    if 8 * step == 3 * count:
        q = quarter(a, sign)
        return ((q[0] - a[0]) * ROOT_HALF, (q[1] - a[1]) * ROOT_HALF)
    angle = sign * 2.0 * math.pi * step / count
    cosine, sine = math.cos(angle), math.sin(angle)
    return (a[0] * cosine - a[1] * sine, a[0] * sine + a[1] * cosine)


def fourier4(x, sign):
    t0, t1 = add(x[0], x[2]), sub(x[0], x[2])
    t2, t3 = add(x[1], x[3]), quarter(sub(x[1], x[3]), sign)
    return [add(t0, t2), add(t1, t3), sub(t0, t2), sub(t1, t3)]


def fourier8(x, sign):
    even = fourier4(x[0::2], sign)
    odd = fourier4(x[1::2], sign)
    odd = [turn(odd[k], k, 8, sign) for k in range(4)]
    return [add(even[k], odd[k]) for k in range(4)] + [sub(even[k], odd[k]) for k in range(4)]


def fourier(x, sign):
    if len(x) == 1:
        return x
    if len(x) == 2:
        return [add(x[0], x[1]), sub(x[0], x[1])]
    return fourier4(x, sign) if len(x) == 4 else fourier8(x, sign)


def fourier64(load, store, middle, sign):
    for b in range(8):
        values = fourier8([load(8 * a + b) for a in range(8)], sign)
        for c in range(8):
            real, imag = turn(values[c], b * c, 64, sign)
            middle[c * 8 + b, 0] = real
            middle[c * 8 + b, 1] = imag
    for c in range(8):
        values = fourier8([(middle[c * 8 + b, 0], middle[c * 8 + b, 1]) for b in range(8)], sign)
        for d in range(8):
            store(c + 8 * d, values[d])


def fourier_part(load, store, middle, kept, radix):
    size = OUTER // radix
    first = size // 4
    for b in range(4):
        groups = [[] for _ in kept]
        for a in range(first):
            n = 4 * a + b
            values = fourier([load(n + size * t) for t in range(radix)], -1)
            for at, j in enumerate(kept):
                groups[at].append(turn(values[j], n * j, OUTER, -1))
        for at in range(len(kept)):
            values = fourier(groups[at], -1)
            for c in range(first):
                real, imag = turn(values[c], b * c, size, -1)
                middle[(at * first + c) * 4 + b, 0] = real
                middle[(at * first + c) * 4 + b, 1] = imag
    for at in range(len(kept)):
        for c in range(first):
            slot = (at * first + c) * 4
            values = fourier4([(middle[slot + b, 0], middle[slot + b, 1]) for b in range(4)], -1)
            for d in range(4):
                store(c + first * d, at, values[d])


def inverse_part(load, store, middle, kept, radix):
    size = OUTER // radix
    first = size // 4
    for at in range(len(kept)):
        for b in range(4):
            values = fourier([load(4 * a + b, at) for a in range(first)], 1)
            for c in range(first):
                real, imag = turn(values[c], b * c, size, 1)
                middle[(at * first + c) * 4 + b, 0] = real
                middle[(at * first + c) * 4 + b, 1] = imag
    for c in range(first):
        sums = []
        for at in range(len(kept)):
            slot = (at * first + c) * 4
            sums.append(
                fourier4([(middle[slot + b, 0], middle[slot + b, 1]) for b in range(4)], 1)
            )
        for d in range(4):
            n = c + first * d
            store(n, [turn(sums[at][d], n * j, OUTER, 1) for at, j in enumerate(kept)])


def mask_bits(row_term, lane_term, tile):
    mixed = row_term ^ (lane_term + jnp.int32(wrap(tile * INNER * COLUMN_MULTIPLIER)))
    mixed = mixed ^ lax.shift_right_logical(mixed, jnp.full(mixed.shape, 13, jnp.int32))
    mixed = mixed * jnp.int32(MIX_MULTIPLIER)
    return mixed << 3, mixed << 2


def rotate(value, low, high, direction):
    swap = low < 0
    real = jnp.where(swap, value[1], value[0])
    imag = jnp.where(swap, value[0], value[1])
    mixed = (low ^ high) < 0
    upper = high < 0
    flip_real, flip_imag = (mixed, upper) if direction > 0 else (upper, mixed)
    return (jnp.where(flip_real, -real, real), jnp.where(flip_imag, -imag, imag))


def hash_terms(ids_ref, base, mask):
    rows = lax.broadcasted_iota(jnp.int32, (TILE, INNER), 0) + base
    lanes = lax.broadcasted_iota(jnp.int32, (TILE, INNER), 1)
    mask_term = (ids_ref[mask] + 1) * jnp.int32(MASK_MULTIPLIER)
    return (rows * jnp.int32(ROW_MULTIPLIER)) ^ mask_term, lanes * jnp.int32(COLUMN_MULTIPLIER)


def table_pair():
    inner = np.arange(INNER, dtype=np.int64)
    outer = np.arange(OUTER, dtype=np.int64)
    steps = inner[None, None, :] * (outer[:, None, None] + OUTER * inner[None, :, None]) % LENGTH
    angles = steps * (-2.0 * math.pi / LENGTH)
    cosine, sine = np.cos(angles), np.sin(angles)
    table = np.concatenate(
        [np.concatenate([cosine, -sine], axis=2), np.concatenate([sine, cosine], axis=2)], axis=1
    )
    forward = (table * 2.0**-7).astype(ml_dtypes.bfloat16)
    backward = (table.transpose(0, 2, 1) * 2.0**-6).astype(ml_dtypes.bfloat16)
    return forward, backward


def rows_out_kernel(kept, ids_ref, base_ref, image_ref, table_hbm, out_ref, table, middle, held,
                    sem):
    slots, masks, _, rows, _ = out_ref.shape
    radix = OUTER // slots
    slabs = rows // TILE
    step = pl.program_id(0)
    copy = pltpu.make_async_copy(table_hbm.at[:, pl.ds(kept[0], len(kept))], table, sem)

    @pl.when(step == 0)
    def _():
        copy.start()

    def slab(index, carry):
        mask = index // slabs
        at = pl.multiple_of((index % slabs) * TILE, TILE)
        row_term, lane_term = hash_terms(ids_ref, base_ref[0] + step * rows + at, mask)

        def load(n):
            low, high = mask_bits(row_term, lane_term, n)
            span = slice(n * INNER, (n + 1) * INNER)
            value = [image_ref[p, pl.ds(at, TILE), span].astype(jnp.float32) for p in range(2)]
            return rotate(value, low, high, 1)

        def store(r, j, value):
            to = pl.ds(pl.multiple_of(index * TILE, TILE), TILE)
            held[r, j, to, 0:INNER] = value[0].astype(jnp.bfloat16)
            held[r, j, to, INNER:] = value[1].astype(jnp.bfloat16)

        fourier_part(load, store, middle, kept, radix)
        return carry

    lax.fori_loop(0, masks * slabs, slab, 0)

    @pl.when(step == 0)
    def _():
        copy.wait()

    def spread(r, carry):
        for j in range(len(kept)):
            value = jnp.dot(held[r, j], table[r, j], preferred_element_type=jnp.float32)
            value = value.astype(jnp.bfloat16)
            for m in range(masks):
                for p in range(2):
                    out_ref[r, m, p, :, j * INNER : (j + 1) * INNER] = value[
                        m * rows : (m + 1) * rows, p * INNER : (p + 1) * INNER
                    ]
        return carry

    lax.fori_loop(0, slots, spread, 0)


def row_step(count, masks):
    return min(count, max(TILE, 256 // masks))


def row_scratch(slots, kept, masks, rows):
    return [
        pltpu.VMEM((slots, kept, 2 * INNER, 2 * INNER), jnp.bfloat16),
        pltpu.VMEM((slots * kept, 2, TILE, INNER), jnp.float32),
        pltpu.VMEM((slots, kept, masks * rows, 2 * INNER), jnp.bfloat16),
        pltpu.SemaphoreType.DMA,
    ]


def parameters(flops):
    return {
        "compiler_params": pltpu.CompilerParams(
            vmem_limit_bytes=VMEM_LIMIT, dimension_semantics=("arbitrary",)
        ),
        "cost_estimate": pl.CostEstimate(
            flops=flops, bytes_accessed=40 << 20, transcendentals=0
        ),
    }


def rows_out(kept, ids, base, image, table, masks):
    _, count, width = image.shape
    slots = table.shape[0]
    rows = row_step(count, masks)
    span = len(kept) * INNER
    return pl.pallas_call(
        functools.partial(rows_out_kernel, kept),
        grid=(count // rows,),
        in_specs=[
            pl.BlockSpec(memory_space=pltpu.SMEM),
            pl.BlockSpec(memory_space=pltpu.SMEM),
            pl.BlockSpec((2, rows, width), lambda i: (0, i, 0)),
            pl.BlockSpec(memory_space=pl.ANY),
        ],
        out_specs=pl.BlockSpec((slots, masks, 2, rows, span), lambda i: (0, 0, 0, i, 0)),
        out_shape=jax.ShapeDtypeStruct((slots, masks, 2, count, span), jnp.bfloat16),
        scratch_shapes=row_scratch(slots, len(kept), masks, rows),
        name="rows_out",
        **parameters(masks * count * width * 1000),
    )(ids, base, image, table)


def columns_kernel(share, in_ref, measured_ref, forward_hbm, backward_hbm, out_ref, loss_ref,
                   forward, backward, middle, held, sems):
    copies = [
        pltpu.make_async_copy(forward_hbm, forward, sems.at[0]),
        pltpu.make_async_copy(backward_hbm, backward, sems.at[1]),
    ]

    @pl.when(pl.program_id(0) == 0)
    def _():
        for copy in copies:
            copy.start()
        loss_ref[...] = jnp.zeros_like(loss_ref)

    slabs = INNER // TILE

    def place(n, at):
        if share >= INNER:
            per = share // INNER
            return n // per, pl.ds(pl.multiple_of((n % per) * INNER + at, TILE), TILE)
        return (n * (INNER // share) + at // share, pl.ds(pl.multiple_of(at % share, TILE), TILE))

    def arrive(index, carry):
        at = pl.multiple_of(index * TILE, TILE)

        def load(n):
            source, span = place(n, at)
            return [in_ref[source, p, span, :].astype(jnp.float32) for p in range(2)]

        def store(k, value):
            for p in range(2):
                to = pl.ds(pl.multiple_of(p * INNER + at, TILE), TILE)
                held[k, to, :] = value[p].astype(jnp.bfloat16)

        fourier64(load, store, middle, -1)
        return carry

    lax.fori_loop(0, slabs, arrive, 0)

    @pl.when(pl.program_id(0) == 0)
    def _():
        for copy in copies:
            copy.wait()

    def residual(k, carry):
        spectrum = jnp.dot(forward[k], held[k], preferred_element_type=jnp.float32)
        real, imag = spectrum[:INNER], spectrum[INNER:]
        measured = measured_ref[
            0, pl.ds(pl.multiple_of(k * INNER, INNER), INNER), :
        ].astype(jnp.float32)
        square = real * real + imag * imag + EPSILON
        inverse = lax.rsqrt(square)
        misfit = square * inverse - measured
        kept = 1.0 - measured * inverse
        loss_ref[...] += jnp.sum((misfit * misfit).reshape(INNER // 8, 8, INNER), axis=0)
        weighted = jnp.concatenate([real * kept, imag * kept], axis=0).astype(jnp.bfloat16)
        back = jnp.dot(backward[k], weighted, preferred_element_type=jnp.float32)
        held[k] = back.astype(jnp.bfloat16)
        return carry

    lax.fori_loop(0, OUTER, residual, 0, unroll=2)

    def leave(index, carry):
        at = pl.multiple_of(index * TILE, TILE)

        def load(k):
            return [
                held[k, pl.ds(pl.multiple_of(p * INNER + at, TILE), TILE), :].astype(jnp.float32)
                for p in range(2)
            ]

        def store(n, value):
            source, span = place(n, at)
            for p in range(2):
                out_ref[source, p, span, :] = value[p].astype(jnp.bfloat16)

        fourier64(load, store, middle, 1)
        return carry

    lax.fori_loop(0, slabs, leave, 0)


def columns(chunk, arrived, measured, forward, backward):
    devices, _, share, width = arrived.shape
    length = devices * share
    steps = width // INNER
    return pl.pallas_call(
        functools.partial(columns_kernel, share),
        grid=(steps,),
        in_specs=[
            pl.BlockSpec((devices, 2, share, INNER), lambda i: (0, 0, 0, i)),
            pl.BlockSpec((1, length, INNER), lambda i: (0, 0, chunk * steps + i)),
            pl.BlockSpec(memory_space=pl.ANY),
            pl.BlockSpec(memory_space=pl.ANY),
        ],
        out_specs=[
            pl.BlockSpec((devices, 2, share, INNER), lambda i: (0, 0, 0, i)),
            pl.BlockSpec((8, INNER), lambda i: (0, 0)),
        ],
        out_shape=[
            jax.ShapeDtypeStruct(arrived.shape, jnp.bfloat16),
            jax.ShapeDtypeStruct((8, INNER), jnp.float32),
        ],
        scratch_shapes=[
            pltpu.VMEM((OUTER, 2 * INNER, 2 * INNER), jnp.bfloat16),
            pltpu.VMEM((OUTER, 2 * INNER, 2 * INNER), jnp.bfloat16),
            pltpu.VMEM((OUTER, 2, TILE, INNER), jnp.float32),
            pltpu.VMEM((OUTER, 2 * INNER, INNER), jnp.bfloat16),
            pltpu.SemaphoreType.DMA((2,)),
        ],
        name="columns",
        **parameters(length * width * 2200),
    )(arrived, measured, forward, backward)


def gather_kept(kept, in_ref, table_hbm, table, held, sem):
    slots, masks = in_ref.shape[:2]
    copy = pltpu.make_async_copy(table_hbm.at[:, pl.ds(kept[0], len(kept))], table, sem)

    @pl.when(pl.program_id(0) == 0)
    def _():
        copy.start()
        copy.wait()

    def gather(r, carry):
        for j in range(len(kept)):
            span = slice(j * INNER, (j + 1) * INNER)
            value = jnp.concatenate(
                [
                    jnp.concatenate([in_ref[r, m, p, :, span] for p in range(2)], axis=1)
                    for m in range(masks)
                ],
                axis=0,
            )
            held[r, j] = jnp.dot(value, table[r, j], preferred_element_type=jnp.float32).astype(
                jnp.bfloat16
            )
        return carry

    lax.fori_loop(0, slots, gather, 0)


def held_tile(held, r, j, index):
    take = pl.ds(pl.multiple_of(index * TILE, TILE), TILE)
    return [
        held[r, j, take, p * INNER : (p + 1) * INNER].astype(jnp.float32) for p in range(2)
    ]


def rows_part_kernel(kept, in_ref, table_hbm, out_ref, table, middle, held, sem):
    slots, masks, _, rows, _ = in_ref.shape
    slabs = rows // TILE
    gather_kept(kept, in_ref, table_hbm, table, held, sem)

    def slab(index, carry):
        mask = index // slabs
        at = pl.multiple_of((index % slabs) * TILE, TILE)

        def load(r, j):
            return held_tile(held, r, j, index)

        def store(n, values):
            for j, value in enumerate(values):
                for p in range(2):
                    out_ref[n, j, mask, p, pl.ds(at, TILE), :] = value[p].astype(jnp.bfloat16)

        inverse_part(load, store, middle, kept, OUTER // slots)
        return carry

    lax.fori_loop(0, masks * slabs, slab, 0)


def rows_part(kept, arrived, table):
    slots, masks, _, count, span = arrived.shape
    rows = row_step(count, masks)
    return pl.pallas_call(
        functools.partial(rows_part_kernel, kept),
        grid=(count // rows,),
        in_specs=[
            pl.BlockSpec((slots, masks, 2, rows, span), lambda i: (0, 0, 0, i, 0)),
            pl.BlockSpec(memory_space=pl.ANY),
        ],
        out_specs=pl.BlockSpec(
            (slots, len(kept), masks, 2, rows, INNER), lambda i: (0, 0, 0, 0, i, 0)
        ),
        out_shape=jax.ShapeDtypeStruct(
            (slots, len(kept), masks, 2, count, INNER), jnp.bfloat16
        ),
        scratch_shapes=row_scratch(slots, len(kept), masks, rows),
        name="rows_part",
        **parameters(masks * count * LENGTH * 600),
    )(arrived, table)


def rows_in_kernel(kept, ids_ref, base_ref, in_ref, part_ref, table_hbm, out_ref, table, middle,
                   held, sem):
    slots, masks, _, rows, _ = in_ref.shape
    radix = OUTER // slots
    slabs = rows // TILE
    step = pl.program_id(0)
    gather_kept(kept, in_ref, table_hbm, table, held, sem)

    def slab(index, carry, first):
        mask = index // slabs
        at = pl.multiple_of((index % slabs) * TILE, TILE)
        row_term, lane_term = hash_terms(ids_ref, base_ref[0] + step * rows + at, mask)

        def load(r, j):
            return held_tile(held, r, j, index)

        def store(n, values):
            early = [
                [part_ref[n, j, mask, p, pl.ds(at, TILE), :].astype(jnp.float32) for p in range(2)]
                for j in range(radix - len(kept))
            ]
            for t, value in enumerate(fourier(early + values, 1)):
                tile = n + slots * t
                low, high = mask_bits(row_term, lane_term, tile)
                value = rotate(value, low, high, -1)
                span = slice(tile * INNER, (tile + 1) * INNER)
                for p in range(2):
                    if first:
                        out_ref[p, pl.ds(at, TILE), span] = value[p]
                    else:
                        out_ref[p, pl.ds(at, TILE), span] += value[p]

        inverse_part(load, store, middle, kept, radix)
        return carry

    lax.fori_loop(0, slabs, functools.partial(slab, first=True), 0)
    lax.fori_loop(slabs, masks * slabs, functools.partial(slab, first=False), 0)


def rows_in(kept, ids, base, arrived, part, table):
    slots, masks, _, count, span = arrived.shape
    rows = row_step(count, masks)
    return pl.pallas_call(
        functools.partial(rows_in_kernel, kept),
        grid=(count // rows,),
        in_specs=[
            pl.BlockSpec(memory_space=pltpu.SMEM),
            pl.BlockSpec(memory_space=pltpu.SMEM),
            pl.BlockSpec((slots, masks, 2, rows, span), lambda i: (0, 0, 0, i, 0)),
            pl.BlockSpec((slots,) + part.shape[1:4] + (rows, INNER), lambda i: (0, 0, 0, 0, i, 0)),
            pl.BlockSpec(memory_space=pl.ANY),
        ],
        out_specs=pl.BlockSpec((2, rows, LENGTH), lambda i: (0, i, 0)),
        out_shape=jax.ShapeDtypeStruct((2, count, LENGTH), jnp.float32),
        scratch_shapes=row_scratch(slots, len(kept), masks, rows),
        name="rows_in",
        **parameters(masks * count * LENGTH * 1000),
    )(ids, base, arrived, part, table)


AXES = ("rows", "mask")
CHUNKS = 2


def exchange(blocks):
    flat = blocks.reshape((-1,) + blocks.shape[-3:])
    flat = lax.all_to_all(flat, AXES, split_axis=0, concat_axis=0, tiled=True)
    return flat.reshape(blocks.shape)


def shards(slots, masks, image, measured, mask_ids):
    forward, backward = (jnp.asarray(table) for table in table_pair())
    _, count, width = image.shape
    radix = OUTER // slots
    each = radix // CHUNKS
    kept = [tuple(range(c * each, (c + 1) * each)) for c in range(CHUNKS)]
    by_slot = (slots, radix, 2 * INNER, 2 * INNER)
    out_table, in_table = backward.reshape(by_slot), forward.reshape(by_slot)
    ids = lax.all_gather(mask_ids, "mask", tiled=True)
    base = (lax.axis_index("rows") * masks + lax.axis_index("mask")) * count
    base = base.astype(jnp.int32)[None]
    losses = []
    leaving = []
    for c in range(CHUNKS):
        sent = rows_out(kept[c], ids, base, image, out_table, masks)
        arrived = exchange(sent.reshape((-1,) + sent.shape[2:]))
        left, loss = columns(c, arrived, measured, forward, backward)
        leaving.append(left.reshape(sent.shape))
        losses.append(jnp.sum(loss))
    returned, loss_part = lax.optimization_barrier((exchange(leaving[0]), losses[0] + losses[1]))
    loss_sum = lax.psum(loss_part, AXES)
    last, loss_sum = lax.optimization_barrier((leaving[1], loss_sum))
    part = rows_part(kept[0], returned, in_table)
    gradient = rows_in(kept[1], ids, base, exchange(last), part, in_table)
    return gradient, loss_sum / (masks * width * width)


def solution(mesh):
    slots, masks = mesh.shape["rows"], mesh.shape["mask"]
    return jax.shard_map(
        functools.partial(shards, slots, masks),
        mesh=mesh,
        in_specs=(P(None, AXES, None), P("mask", None, "rows"), P("mask")),
        out_specs=(P(None, AXES, None), P()),
        check_vma=False,
    )
```

```python
import functools
import math

import jax
import jax.numpy as jnp
import ml_dtypes
import numpy as np
from jax import lax
from jax.experimental import pallas as pl
from jax.experimental.pallas import tpu as pltpu
from jax.sharding import PartitionSpec as P

INNER = 128
OUTER = 64
LENGTH = INNER * OUTER
EPSILON = 0.25
TILE = 16
VMEM_LIMIT = 58 * 1024 * 1024
ROOT_HALF = math.sqrt(0.5)

ROW_MULTIPLIER = 73856093
COLUMN_MULTIPLIER = 19349663
MASK_MULTIPLIER = 83492791
MIX_MULTIPLIER = 1274126177


def wrap(value):
    return (value + 2**31) % 2**32 - 2**31


def add(a, b):
    return (a[0] + b[0], a[1] + b[1])


def sub(a, b):
    return (a[0] - b[0], a[1] - b[1])


def quarter(a, sign):
    return (-a[1], a[0]) if sign > 0 else (a[1], -a[0])


def turn(a, step, count, sign):
    step = step % count
    if step == 0:
        return a
    if 4 * step == count:
        return quarter(a, sign)
    if 2 * step == count:
        return (-a[0], -a[1])
    if 4 * step == 3 * count:
        return quarter(a, -sign)
    if 8 * step == count:
        q = quarter(a, sign)
        return ((a[0] + q[0]) * ROOT_HALF, (a[1] + q[1]) * ROOT_HALF)
    if 8 * step == 3 * count:
        q = quarter(a, sign)
        return ((q[0] - a[0]) * ROOT_HALF, (q[1] - a[1]) * ROOT_HALF)
    angle = sign * 2.0 * math.pi * step / count
    cosine, sine = math.cos(angle), math.sin(angle)
    return (a[0] * cosine - a[1] * sine, a[0] * sine + a[1] * cosine)


def fourier4(x, sign):
    t0, t1 = add(x[0], x[2]), sub(x[0], x[2])
    t2, t3 = add(x[1], x[3]), quarter(sub(x[1], x[3]), sign)
    return [add(t0, t2), add(t1, t3), sub(t0, t2), sub(t1, t3)]


def fourier8(x, sign):
    even = fourier4(x[0::2], sign)
    odd = fourier4(x[1::2], sign)
    odd = [turn(odd[k], k, 8, sign) for k in range(4)]
    return [add(even[k], odd[k]) for k in range(4)] + [sub(even[k], odd[k]) for k in range(4)]


def fourier(x, sign):
    if len(x) == 1:
        return x
    if len(x) == 2:
        return [add(x[0], x[1]), sub(x[0], x[1])]
    return fourier4(x, sign) if len(x) == 4 else fourier8(x, sign)


def fourier64(load, store, middle, sign):
    for b in range(8):
        values = fourier8([load(8 * a + b) for a in range(8)], sign)
        for c in range(8):
            real, imag = turn(values[c], b * c, 64, sign)
            middle[c * 8 + b, 0] = real
            middle[c * 8 + b, 1] = imag
    for c in range(8):
        values = fourier8([(middle[c * 8 + b, 0], middle[c * 8 + b, 1]) for b in range(8)], sign)
        for d in range(8):
            store(c + 8 * d, values[d])


def fourier_part(load, store, middle, kept, radix):
    size = OUTER // radix
    first = size // 4
    for b in range(4):
        groups = [[] for _ in kept]
        for a in range(first):
            n = 4 * a + b
            values = fourier([load(n + size * t) for t in range(radix)], -1)
            for at, j in enumerate(kept):
                groups[at].append(turn(values[j], n * j, OUTER, -1))
        for at in range(len(kept)):
            values = fourier(groups[at], -1)
            for c in range(first):
                real, imag = turn(values[c], b * c, size, -1)
                middle[(at * first + c) * 4 + b, 0] = real
                middle[(at * first + c) * 4 + b, 1] = imag
    for at in range(len(kept)):
        for c in range(first):
            slot = (at * first + c) * 4
            values = fourier4([(middle[slot + b, 0], middle[slot + b, 1]) for b in range(4)], -1)
            for d in range(4):
                store(c + first * d, at, values[d])


def inverse_part(load, store, middle, kept, radix):
    size = OUTER // radix
    first = size // 4
    for at in range(len(kept)):
        for b in range(4):
            values = fourier([load(4 * a + b, at) for a in range(first)], 1)
            for c in range(first):
                real, imag = turn(values[c], b * c, size, 1)
                middle[(at * first + c) * 4 + b, 0] = real
                middle[(at * first + c) * 4 + b, 1] = imag
    for c in range(first):
        sums = []
        for at in range(len(kept)):
            slot = (at * first + c) * 4
            sums.append(
                fourier4([(middle[slot + b, 0], middle[slot + b, 1]) for b in range(4)], 1)
            )
        for d in range(4):
            n = c + first * d
            store(n, [turn(sums[at][d], n * j, OUTER, 1) for at, j in enumerate(kept)])


def phase_code(row_term, lane_term, tile):
    mixed = row_term ^ (lane_term + jnp.int32(wrap(tile * INNER * COLUMN_MULTIPLIER)))
    mixed = mixed ^ lax.shift_right_logical(mixed, jnp.full(mixed.shape, 13, jnp.int32))
    mixed = mixed * jnp.int32(MIX_MULTIPLIER)
    code = lax.shift_right_arithmetic(mixed << 2, jnp.full(mixed.shape, 30, jnp.int32))
    return code.astype(jnp.float32).astype(jnp.bfloat16)


def rotate(value, code, direction):
    size = jnp.abs(code)
    cosine = 1 - size
    sine = code * (2 - size)
    left, right = value[0] * sine, value[1] * sine
    if direction > 0:
        return (value[0] * cosine - right, left + value[1] * cosine)
    return (value[0] * cosine + right, value[1] * cosine - left)


def hash_terms(id_refs, base, mask):
    masks = len(id_refs)
    rows = lax.broadcasted_iota(jnp.int32, (TILE, INNER), 0) + base
    lanes = lax.broadcasted_iota(jnp.int32, (TILE, INNER), 1)
    ahead = lax.rem(mask - lax.axis_index("mask") + masks, masks)
    mask_id = id_refs[0][0]
    for d in range(1, masks):
        mask_id = jnp.where(ahead == d, id_refs[d][0], mask_id)
    mask_term = (mask_id + 1) * jnp.int32(MASK_MULTIPLIER)
    return (rows * jnp.int32(ROW_MULTIPLIER)) ^ mask_term, lanes * jnp.int32(COLUMN_MULTIPLIER)


def table_pair():
    inner = np.arange(INNER, dtype=np.int64)
    outer = np.arange(OUTER, dtype=np.int64)
    steps = inner[None, None, :] * (outer[:, None, None] + OUTER * inner[None, :, None]) % LENGTH
    angles = steps * (-2.0 * math.pi / LENGTH)
    cosine, sine = np.cos(angles), np.sin(angles)
    table = np.concatenate(
        [np.concatenate([cosine, -sine], axis=2), np.concatenate([sine, cosine], axis=2)], axis=1
    )
    forward = (table * 2.0**-7).astype(ml_dtypes.bfloat16)
    backward = (table.transpose(0, 2, 1) * 2.0**-6).astype(ml_dtypes.bfloat16)
    return forward, backward


def rows_out_kernel(kept, masks, *refs):
    id_refs = refs[:masks]
    image_ref, table_hbm, out_ref, *rest = refs[masks:]
    code_ref = rest[0] if len(rest) == 5 else None
    table, middle, held, sem = rest[-4:]
    slots, _, _, rows, _ = out_ref.shape
    steps = pl.num_programs(0)
    device = lax.axis_index("rows") * masks + lax.axis_index("mask")
    radix = OUTER // slots
    slabs = rows // TILE
    step = pl.program_id(0)
    copy = pltpu.make_async_copy(table_hbm.at[:, pl.ds(kept[0], len(kept))], table, sem)

    @pl.when(step == 0)
    def _():
        copy.start()

    def slab(index, carry):
        mask = index // slabs
        at = pl.multiple_of((index % slabs) * TILE, TILE)
        base = (device * steps + step) * rows + at
        row_term, lane_term = hash_terms(id_refs, base, mask)

        def load(n):
            code = phase_code(row_term, lane_term, n)
            span = slice(n * INNER, (n + 1) * INNER)
            if code_ref is not None:
                code_ref[mask, pl.ds(at, TILE), span] = code
            return rotate([image_ref[p, pl.ds(at, TILE), span] for p in range(2)], code, 1)

        def store(r, j, value):
            to = pl.ds(pl.multiple_of(index * TILE, TILE), TILE)
            held[r, j, to, 0:INNER] = value[0]
            held[r, j, to, INNER:] = value[1]

        fourier_part(load, store, middle, kept, radix)
        return carry

    lax.fori_loop(0, masks * slabs, slab, 0)

    @pl.when(step == 0)
    def _():
        copy.wait()

    def spread(r, carry):
        for j in range(len(kept)):
            value = jnp.dot(held[r, j], table[r, j], preferred_element_type=jnp.float32)
            value = value.astype(jnp.bfloat16)
            for m in range(masks):
                for p in range(2):
                    out_ref[r, m, p, :, j * INNER : (j + 1) * INNER] = value[
                        m * rows : (m + 1) * rows, p * INNER : (p + 1) * INNER
                    ]
        return carry

    lax.fori_loop(0, slots, spread, 0)


def row_step(count, masks):
    return min(count, max(TILE, 256 // masks))


def row_scratch(slots, kept, masks, rows):
    return [
        pltpu.VMEM((slots, kept, 2 * INNER, 2 * INNER), jnp.bfloat16),
        pltpu.VMEM((slots * kept, 2, TILE, INNER), jnp.bfloat16),
        pltpu.VMEM((slots, kept, masks * rows, 2 * INNER), jnp.bfloat16),
        pltpu.SemaphoreType.DMA,
    ]


def parameters(flops):
    return {
        "compiler_params": pltpu.CompilerParams(
            vmem_limit_bytes=VMEM_LIMIT, dimension_semantics=("arbitrary",)
        ),
        "cost_estimate": pl.CostEstimate(
            flops=flops, bytes_accessed=40 << 20, transcendentals=0
        ),
    }


def rows_out(kept, ids, image, table, with_code):
    masks = len(ids)
    _, count, width = image.shape
    slots = table.shape[0]
    rows = row_step(count, masks)
    span = len(kept) * INNER
    return pl.pallas_call(
        functools.partial(rows_out_kernel, kept, masks),
        grid=(count // rows,),
        in_specs=[pl.BlockSpec(memory_space=pltpu.SMEM)] * masks
        + [
            pl.BlockSpec((2, rows, width), lambda i: (0, i, 0)),
            pl.BlockSpec(memory_space=pl.ANY),
        ],
        out_specs=[
            pl.BlockSpec((slots, masks, 2, rows, span), lambda i: (0, 0, 0, i, 0)),
            pl.BlockSpec((masks, rows, width), lambda i: (0, i, 0)),
        ][: 1 + with_code],
        out_shape=[
            jax.ShapeDtypeStruct((slots, masks, 2, count, span), jnp.bfloat16),
            jax.ShapeDtypeStruct((masks, count, width), jnp.bfloat16),
        ][: 1 + with_code],
        scratch_shapes=row_scratch(slots, len(kept), masks, rows),
        name="rows_out",
        **parameters(masks * count * width * 1000),
    )(*ids, image, table)


def columns_kernel(share, in_ref, measured_ref, forward_hbm, backward_hbm, out_ref, loss_ref,
                   forward, backward, middle, held, sems):
    copies = [
        pltpu.make_async_copy(forward_hbm, forward, sems.at[0]),
        pltpu.make_async_copy(backward_hbm, backward, sems.at[1]),
    ]

    @pl.when(pl.program_id(0) == 0)
    def _():
        for copy in copies:
            copy.start()
        loss_ref[...] = jnp.zeros_like(loss_ref)

    slabs = INNER // TILE

    def place(n, at):
        if share >= INNER:
            per = share // INNER
            return n // per, pl.ds(pl.multiple_of((n % per) * INNER + at, TILE), TILE)
        return (n * (INNER // share) + at // share, pl.ds(pl.multiple_of(at % share, TILE), TILE))

    def arrive(index, carry):
        at = pl.multiple_of(index * TILE, TILE)

        def load(n):
            source, span = place(n, at)
            return [in_ref[source, p, span, :].astype(jnp.float32) for p in range(2)]

        def store(k, value):
            for p in range(2):
                to = pl.ds(pl.multiple_of(p * INNER + at, TILE), TILE)
                held[k, to, :] = value[p].astype(jnp.bfloat16)

        fourier64(load, store, middle, -1)
        return carry

    lax.fori_loop(0, slabs, arrive, 0)

    @pl.when(pl.program_id(0) == 0)
    def _():
        for copy in copies:
            copy.wait()

    def residual(k, carry):
        spectrum = jnp.dot(forward[k], held[k], preferred_element_type=jnp.float32)
        real, imag = spectrum[:INNER], spectrum[INNER:]
        measured = measured_ref[
            0, pl.ds(pl.multiple_of(k * INNER, INNER), INNER), :
        ].astype(jnp.float32)
        square = real * real + imag * imag + EPSILON
        inverse = lax.rsqrt(square)
        misfit = square * inverse - measured
        kept = 1.0 - measured * inverse
        loss_ref[...] += jnp.sum((misfit * misfit).reshape(INNER // 8, 8, INNER), axis=0)
        weighted = jnp.concatenate([real * kept, imag * kept], axis=0).astype(jnp.bfloat16)
        back = jnp.dot(backward[k], weighted, preferred_element_type=jnp.float32)
        held[k] = back.astype(jnp.bfloat16)
        return carry

    lax.fori_loop(0, OUTER, residual, 0, unroll=2)

    def leave(index, carry):
        at = pl.multiple_of(index * TILE, TILE)

        def load(k):
            return [
                held[k, pl.ds(pl.multiple_of(p * INNER + at, TILE), TILE), :].astype(jnp.float32)
                for p in range(2)
            ]

        def store(n, value):
            source, span = place(n, at)
            for p in range(2):
                out_ref[source, p, span, :] = value[p].astype(jnp.bfloat16)

        fourier64(load, store, middle, 1)
        return carry

    lax.fori_loop(0, slabs, leave, 0)


def columns(chunk, arrived, measured, forward, backward):
    devices, _, share, width = arrived.shape
    length = devices * share
    steps = width // INNER
    return pl.pallas_call(
        functools.partial(columns_kernel, share),
        grid=(steps,),
        in_specs=[
            pl.BlockSpec((devices, 2, share, INNER), lambda i: (0, 0, 0, i)),
            pl.BlockSpec((1, length, INNER), lambda i: (0, 0, chunk * steps + i)),
            pl.BlockSpec(memory_space=pl.ANY),
            pl.BlockSpec(memory_space=pl.ANY),
        ],
        out_specs=[
            pl.BlockSpec((devices, 2, share, INNER), lambda i: (0, 0, 0, i)),
            pl.BlockSpec((8, INNER), lambda i: (0, 0)),
        ],
        out_shape=[
            jax.ShapeDtypeStruct(arrived.shape, jnp.bfloat16),
            jax.ShapeDtypeStruct((8, INNER), jnp.float32),
        ],
        scratch_shapes=[
            pltpu.VMEM((OUTER, 2 * INNER, 2 * INNER), jnp.bfloat16),
            pltpu.VMEM((OUTER, 2 * INNER, 2 * INNER), jnp.bfloat16),
            pltpu.VMEM((OUTER, 2, TILE, INNER), jnp.float32),
            pltpu.VMEM((OUTER, 2 * INNER, INNER), jnp.bfloat16),
            pltpu.SemaphoreType.DMA((2,)),
        ],
        name="columns",
        **parameters(length * width * 2200),
    )(arrived, measured, forward, backward)


def gather_kept(kept, in_ref, table_hbm, table, held, sem):
    slots, masks = in_ref.shape[:2]
    copy = pltpu.make_async_copy(table_hbm.at[:, pl.ds(kept[0], len(kept))], table, sem)

    @pl.when(pl.program_id(0) == 0)
    def _():
        copy.start()
        copy.wait()

    def gather(r, carry):
        for j in range(len(kept)):
            span = slice(j * INNER, (j + 1) * INNER)
            value = jnp.concatenate(
                [
                    jnp.concatenate([in_ref[r, m, p, :, span] for p in range(2)], axis=1)
                    for m in range(masks)
                ],
                axis=0,
            )
            held[r, j] = jnp.dot(value, table[r, j], preferred_element_type=jnp.float32).astype(
                jnp.bfloat16
            )
        return carry

    lax.fori_loop(0, slots, gather, 0)


def held_tile(held, r, j, index):
    take = pl.ds(pl.multiple_of(index * TILE, TILE), TILE)
    return [
        held[r, j, take, p * INNER : (p + 1) * INNER] for p in range(2)
    ]


def rows_part_kernel(kept, in_ref, table_hbm, out_ref, table, middle, held, sem):
    slots, masks, _, rows, _ = in_ref.shape
    slabs = rows // TILE
    gather_kept(kept, in_ref, table_hbm, table, held, sem)

    def slab(index, carry):
        mask = index // slabs
        at = pl.multiple_of((index % slabs) * TILE, TILE)

        def load(r, j):
            return held_tile(held, r, j, index)

        def store(n, values):
            for j, value in enumerate(values):
                for p in range(2):
                    out_ref[n, j, mask, p, pl.ds(at, TILE), :] = value[p]

        inverse_part(load, store, middle, kept, OUTER // slots)
        return carry

    lax.fori_loop(0, masks * slabs, slab, 0)


def rows_part(kept, arrived, table):
    slots, masks, _, count, span = arrived.shape
    rows = row_step(count, masks)
    return pl.pallas_call(
        functools.partial(rows_part_kernel, kept),
        grid=(count // rows,),
        in_specs=[
            pl.BlockSpec((slots, masks, 2, rows, span), lambda i: (0, 0, 0, i, 0)),
            pl.BlockSpec(memory_space=pl.ANY),
        ],
        out_specs=pl.BlockSpec(
            (slots, len(kept), masks, 2, rows, INNER), lambda i: (0, 0, 0, 0, i, 0)
        ),
        out_shape=jax.ShapeDtypeStruct(
            (slots, len(kept), masks, 2, count, INNER), jnp.bfloat16
        ),
        scratch_shapes=row_scratch(slots, len(kept), masks, rows),
        name="rows_part",
        **parameters(masks * count * LENGTH * 600),
    )(arrived, table)


def rows_in_kernel(kept, code_ref, in_ref, part_ref, table_hbm, out_ref, table, middle, held,
                   sem):
    slots, masks, _, rows, _ = in_ref.shape
    radix = OUTER // slots
    slabs = rows // TILE
    gather_kept(kept, in_ref, table_hbm, table, held, sem)

    def slab(index, carry, first):
        mask = index // slabs
        at = pl.multiple_of((index % slabs) * TILE, TILE)

        def load(r, j):
            return held_tile(held, r, j, index)

        def store(n, values):
            early = [
                [part_ref[n, j, mask, p, pl.ds(at, TILE), :] for p in range(2)]
                for j in range(radix - len(kept))
            ]
            for t, value in enumerate(fourier(early + values, 1)):
                tile = n + slots * t
                span = slice(tile * INNER, (tile + 1) * INNER)
                value = rotate(value, code_ref[mask, pl.ds(at, TILE), span], -1)
                for p in range(2):
                    if first:
                        out_ref[p, pl.ds(at, TILE), span] = value[p].astype(jnp.float32)
                    else:
                        out_ref[p, pl.ds(at, TILE), span] += value[p].astype(jnp.float32)

        inverse_part(load, store, middle, kept, radix)
        return carry

    lax.fori_loop(0, slabs, functools.partial(slab, first=True), 0)
    lax.fori_loop(slabs, masks * slabs, functools.partial(slab, first=False), 0)


def rows_in(kept, code, arrived, part, table):
    slots, masks, _, count, span = arrived.shape
    rows = row_step(count, masks)
    return pl.pallas_call(
        functools.partial(rows_in_kernel, kept),
        grid=(count // rows,),
        in_specs=[
            pl.BlockSpec((masks, rows, LENGTH), lambda i: (0, i, 0)),
            pl.BlockSpec((slots, masks, 2, rows, span), lambda i: (0, 0, 0, i, 0)),
            pl.BlockSpec((slots,) + part.shape[1:4] + (rows, INNER), lambda i: (0, 0, 0, 0, i, 0)),
            pl.BlockSpec(memory_space=pl.ANY),
        ],
        out_specs=pl.BlockSpec((2, rows, LENGTH), lambda i: (0, i, 0)),
        out_shape=jax.ShapeDtypeStruct((2, count, LENGTH), jnp.float32),
        scratch_shapes=row_scratch(slots, len(kept), masks, rows),
        name="rows_in",
        **parameters(masks * count * LENGTH * 1000),
    )(code, arrived, part, table)


AXES = ("rows", "mask")
CHUNKS = 2


def exchange(blocks):
    flat = blocks.reshape((-1,) + blocks.shape[-3:])
    flat = lax.all_to_all(flat, AXES, split_axis=0, concat_axis=0, tiled=True)
    return flat.reshape(blocks.shape)


def shards(slots, masks, image, measured, mask_ids):
    forward, backward = (jnp.asarray(table) for table in table_pair())
    _, count, width = image.shape
    radix = OUTER // slots
    each = radix // CHUNKS
    kept = [tuple(range(c * each, (c + 1) * each)) for c in range(CHUNKS)]
    by_slot = (slots, radix, 2 * INNER, 2 * INNER)
    out_table, in_table = backward.reshape(by_slot), forward.reshape(by_slot)
    ids = [mask_ids] + [
        lax.ppermute(mask_ids, "mask", [((m + d) % masks, m) for m in range(masks)])
        for d in range(1, masks)
    ]
    losses = []
    leaving = []
    for c in range(CHUNKS):
        sent, *code = rows_out(kept[c], ids, image, out_table, c == CHUNKS - 1)
        sent, image = lax.optimization_barrier((sent, image))
        arrived = exchange(sent.reshape((-1,) + sent.shape[2:]))
        left, loss = columns(c, arrived, measured, forward, backward)
        leaving.append(left.reshape(sent.shape))
        losses.append(loss)
    every_loss = lax.all_gather(losses[0] + losses[1], AXES, tiled=True)
    part = rows_part(kept[0], exchange(leaving[0]), in_table)
    gradient = rows_in(kept[1], code[0], exchange(leaving[1]), part, in_table)
    return gradient, jnp.sum(every_loss) / (masks * width * width)


def solution(mesh):
    slots, masks = mesh.shape["rows"], mesh.shape["mask"]
    return jax.shard_map(
        functools.partial(shards, slots, masks),
        mesh=mesh,
        in_specs=(P(None, AXES, None), P("mask", None, "rows"), P("mask")),
        out_specs=(P(None, AXES, None), P()),
        check_vma=False,
    )
```

```python
import functools
import math

import jax
import jax.numpy as jnp
import ml_dtypes
import numpy as np
from jax import lax
from jax.experimental import pallas as pl
from jax.experimental.pallas import tpu as pltpu
from jax.sharding import PartitionSpec as P

INNER = 128
OUTER = 64
LENGTH = INNER * OUTER
EPSILON = 0.25
TILE = 16
VMEM_LIMIT = 58 * 1024 * 1024
ROOT_HALF = math.sqrt(0.5)

ROW_MULTIPLIER = 73856093
COLUMN_MULTIPLIER = 19349663
MASK_MULTIPLIER = 83492791
MIX_MULTIPLIER = 1274126177


def wrap(value):
    return (value + 2**31) % 2**32 - 2**31


def add(a, b):
    return (a[0] + b[0], a[1] + b[1])


def sub(a, b):
    return (a[0] - b[0], a[1] - b[1])


def quarter(a, sign):
    return (-a[1], a[0]) if sign > 0 else (a[1], -a[0])


def turn(a, step, count, sign):
    step = step % count
    if step == 0:
        return a
    if 4 * step == count:
        return quarter(a, sign)
    if 2 * step == count:
        return (-a[0], -a[1])
    if 4 * step == 3 * count:
        return quarter(a, -sign)
    if 8 * step == count:
        q = quarter(a, sign)
        return ((a[0] + q[0]) * ROOT_HALF, (a[1] + q[1]) * ROOT_HALF)
    if 8 * step == 3 * count:
        q = quarter(a, sign)
        return ((q[0] - a[0]) * ROOT_HALF, (q[1] - a[1]) * ROOT_HALF)
    angle = sign * 2.0 * math.pi * step / count
    cosine, sine = math.cos(angle), math.sin(angle)
    return (a[0] * cosine - a[1] * sine, a[0] * sine + a[1] * cosine)


def fourier4(x, sign):
    t0, t1 = add(x[0], x[2]), sub(x[0], x[2])
    t2, t3 = add(x[1], x[3]), quarter(sub(x[1], x[3]), sign)
    return [add(t0, t2), add(t1, t3), sub(t0, t2), sub(t1, t3)]


def fourier8(x, sign):
    even = fourier4(x[0::2], sign)
    odd = fourier4(x[1::2], sign)
    odd = [turn(odd[k], k, 8, sign) for k in range(4)]
    return [add(even[k], odd[k]) for k in range(4)] + [sub(even[k], odd[k]) for k in range(4)]


def fourier(x, sign):
    if len(x) == 1:
        return x
    if len(x) == 2:
        return [add(x[0], x[1]), sub(x[0], x[1])]
    return fourier4(x, sign) if len(x) == 4 else fourier8(x, sign)


def fourier64(load, store, middle, sign):
    for b in range(8):
        values = fourier8([load(8 * a + b) for a in range(8)], sign)
        for c in range(8):
            real, imag = turn(values[c], b * c, 64, sign)
            middle[c * 8 + b, 0] = real
            middle[c * 8 + b, 1] = imag
    for c in range(8):
        values = fourier8([(middle[c * 8 + b, 0], middle[c * 8 + b, 1]) for b in range(8)], sign)
        for d in range(8):
            store(c + 8 * d, values[d])


def fourier_part(load, store, middle, kept, radix):
    size = OUTER // radix
    first = size // 4
    for b in range(4):
        groups = [[] for _ in kept]
        for a in range(first):
            n = 4 * a + b
            values = fourier([load(n + size * t) for t in range(radix)], -1)
            for at, j in enumerate(kept):
                groups[at].append(turn(values[j], n * j, OUTER, -1))
        for at in range(len(kept)):
            values = fourier(groups[at], -1)
            for c in range(first):
                real, imag = turn(values[c], b * c, size, -1)
                middle[(at * first + c) * 4 + b, 0] = real
                middle[(at * first + c) * 4 + b, 1] = imag
    for at in range(len(kept)):
        for c in range(first):
            slot = (at * first + c) * 4
            values = fourier4([(middle[slot + b, 0], middle[slot + b, 1]) for b in range(4)], -1)
            for d in range(4):
                store(c + first * d, at, values[d])


def inverse_part(load, store, middle, kept, radix):
    size = OUTER // radix
    first = size // 4
    for at in range(len(kept)):
        for b in range(4):
            values = fourier([load(4 * a + b, at) for a in range(first)], 1)
            for c in range(first):
                real, imag = turn(values[c], b * c, size, 1)
                middle[(at * first + c) * 4 + b, 0] = real
                middle[(at * first + c) * 4 + b, 1] = imag
    for c in range(first):
        sums = []
        for at in range(len(kept)):
            slot = (at * first + c) * 4
            sums.append(
                fourier4([(middle[slot + b, 0], middle[slot + b, 1]) for b in range(4)], 1)
            )
        for d in range(4):
            n = c + first * d
            store(n, [turn(sums[at][d], n * j, OUTER, 1) for at, j in enumerate(kept)])


def phase_code(row_term, lane_term, tile):
    mixed = row_term ^ (lane_term + jnp.int32(wrap(tile * INNER * COLUMN_MULTIPLIER)))
    mixed = mixed ^ lax.shift_right_logical(mixed, jnp.full(mixed.shape, 13, jnp.int32))
    mixed = mixed * jnp.int32(MIX_MULTIPLIER)
    code = lax.shift_right_arithmetic(mixed << 2, jnp.full(mixed.shape, 30, jnp.int32))
    return code.astype(jnp.float32)


def rotate(value, code, direction):
    size = jnp.abs(code)
    cosine = 1 - size
    sine = code * (2 - size)
    left, right = value[0] * sine, value[1] * sine
    if direction > 0:
        return (value[0] * cosine - right, left + value[1] * cosine)
    return (value[0] * cosine + right, value[1] * cosine - left)


def hash_terms(id_refs, base, mask):
    masks = len(id_refs)
    rows = lax.broadcasted_iota(jnp.int32, (TILE, INNER), 0) + base
    lanes = lax.broadcasted_iota(jnp.int32, (TILE, INNER), 1)
    ahead = lax.rem(mask - lax.axis_index("mask") + masks, masks)
    mask_id = id_refs[0][0]
    for d in range(1, masks):
        mask_id = jnp.where(ahead == d, id_refs[d][0], mask_id)
    mask_term = (mask_id + 1) * jnp.int32(MASK_MULTIPLIER)
    return (rows * jnp.int32(ROW_MULTIPLIER)) ^ mask_term, lanes * jnp.int32(COLUMN_MULTIPLIER)


def table_pair():
    inner = np.arange(INNER, dtype=np.int64)
    outer = np.arange(OUTER, dtype=np.int64)
    steps = inner[None, None, :] * (outer[:, None, None] + OUTER * inner[None, :, None]) % LENGTH
    angles = steps * (-2.0 * math.pi / LENGTH)
    cosine, sine = np.cos(angles), np.sin(angles)
    table = np.concatenate(
        [np.concatenate([cosine, -sine], axis=2), np.concatenate([sine, cosine], axis=2)], axis=1
    )
    forward = (table * 2.0**-7).astype(ml_dtypes.bfloat16)
    backward = (table.transpose(0, 2, 1) * 2.0**-6).astype(ml_dtypes.bfloat16)
    return forward, backward


def rows_out_kernel(kept, masks, *refs):
    id_refs = refs[:masks]
    image_ref, table_hbm, out_ref, *rest = refs[masks:]
    code_ref = rest[0] if len(rest) == 5 else None
    table, middle, held, sem = rest[-4:]
    slots, _, _, rows, _ = out_ref.shape
    steps = pl.num_programs(0)
    device = lax.axis_index("rows") * masks + lax.axis_index("mask")
    radix = OUTER // slots
    slabs = rows // TILE
    step = pl.program_id(0)
    copy = pltpu.make_async_copy(table_hbm.at[:, pl.ds(kept[0], len(kept))], table, sem)

    @pl.when(step == 0)
    def _():
        copy.start()

    def slab(index, carry):
        mask = index // slabs
        at = pl.multiple_of((index % slabs) * TILE, TILE)
        base = (device * steps + step) * rows + at
        row_term, lane_term = hash_terms(id_refs, base, mask)

        def load(n):
            code = phase_code(row_term, lane_term, n)
            span = slice(n * INNER, (n + 1) * INNER)
            if code_ref is not None:
                code_ref[mask, pl.ds(at, TILE), span] = code.astype(jnp.bfloat16)
            value = [image_ref[p, pl.ds(at, TILE), span].astype(jnp.float32) for p in range(2)]
            return rotate(value, code, 1)

        def store(r, j, value):
            to = pl.ds(pl.multiple_of(index * TILE, TILE), TILE)
            held[r, j, to, 0:INNER] = value[0].astype(jnp.bfloat16)
            held[r, j, to, INNER:] = value[1].astype(jnp.bfloat16)

        fourier_part(load, store, middle, kept, radix)
        return carry

    lax.fori_loop(0, masks * slabs, slab, 0)

    @pl.when(step == 0)
    def _():
        copy.wait()

    def spread(r, carry):
        for j in range(len(kept)):
            value = jnp.dot(held[r, j], table[r, j], preferred_element_type=jnp.float32)
            value = value.astype(jnp.bfloat16)
            for m in range(masks):
                for p in range(2):
                    out_ref[r, m, p, :, j * INNER : (j + 1) * INNER] = value[
                        m * rows : (m + 1) * rows, p * INNER : (p + 1) * INNER
                    ]
        return carry

    lax.fori_loop(0, slots, spread, 0, unroll=4)


def row_step(count, masks):
    return min(count, max(TILE, 256 // masks))


def row_scratch(slots, kept, masks, rows):
    return [
        pltpu.VMEM((slots, kept, 2 * INNER, 2 * INNER), jnp.bfloat16),
        pltpu.VMEM((slots * kept, 2, TILE, INNER), jnp.float32),
        pltpu.VMEM((slots, kept, masks * rows, 2 * INNER), jnp.bfloat16),
        pltpu.SemaphoreType.DMA,
    ]


def parameters(flops):
    return {
        "compiler_params": pltpu.CompilerParams(
            vmem_limit_bytes=VMEM_LIMIT, dimension_semantics=("arbitrary",)
        ),
        "cost_estimate": pl.CostEstimate(
            flops=flops, bytes_accessed=40 << 20, transcendentals=0
        ),
    }


def rows_out(kept, ids, image, table, with_code):
    masks = len(ids)
    _, count, width = image.shape
    slots = table.shape[0]
    rows = row_step(count, masks)
    span = len(kept) * INNER
    return pl.pallas_call(
        functools.partial(rows_out_kernel, kept, masks),
        grid=(count // rows,),
        in_specs=[pl.BlockSpec(memory_space=pltpu.SMEM)] * masks
        + [
            pl.BlockSpec((2, rows, width), lambda i: (0, i, 0)),
            pl.BlockSpec(memory_space=pl.ANY),
        ],
        out_specs=[
            pl.BlockSpec((slots, masks, 2, rows, span), lambda i: (0, 0, 0, i, 0)),
            pl.BlockSpec((masks, rows, width), lambda i: (0, i, 0)),
        ][: 1 + with_code],
        out_shape=[
            jax.ShapeDtypeStruct((slots, masks, 2, count, span), jnp.bfloat16),
            jax.ShapeDtypeStruct((masks, count, width), jnp.bfloat16),
        ][: 1 + with_code],
        scratch_shapes=row_scratch(slots, len(kept), masks, rows),
        name="rows_out",
        **parameters(masks * count * width * 1000),
    )(*ids, image, table)


def columns_kernel(share, in_ref, measured_ref, forward_hbm, backward_hbm, out_ref, loss_ref,
                   forward, backward, middle, held, sems):
    copies = [
        pltpu.make_async_copy(forward_hbm, forward, sems.at[0]),
        pltpu.make_async_copy(backward_hbm, backward, sems.at[1]),
    ]

    @pl.when(pl.program_id(0) == 0)
    def _():
        for copy in copies:
            copy.start()
        loss_ref[...] = jnp.zeros_like(loss_ref)

    slabs = INNER // TILE

    def place(n, at):
        if share >= INNER:
            per = share // INNER
            return n // per, pl.ds(pl.multiple_of((n % per) * INNER + at, TILE), TILE)
        return (n * (INNER // share) + at // share, pl.ds(pl.multiple_of(at % share, TILE), TILE))

    def arrive(index, carry):
        at = pl.multiple_of(index * TILE, TILE)

        def load(n):
            source, span = place(n, at)
            return [in_ref[source, p, span, :].astype(jnp.float32) for p in range(2)]

        def store(k, value):
            for p in range(2):
                to = pl.ds(pl.multiple_of(p * INNER + at, TILE), TILE)
                held[k, to, :] = value[p].astype(jnp.bfloat16)

        fourier64(load, store, middle, -1)
        return carry

    lax.fori_loop(0, slabs, arrive, 0)

    @pl.when(pl.program_id(0) == 0)
    def _():
        for copy in copies:
            copy.wait()

    def residual(k, carry):
        spectrum = jnp.dot(forward[k], held[k], preferred_element_type=jnp.float32)
        real, imag = spectrum[:INNER], spectrum[INNER:]
        measured = measured_ref[
            0, pl.ds(pl.multiple_of(k * INNER, INNER), INNER), :
        ].astype(jnp.float32)
        square = real * real + imag * imag + EPSILON
        inverse = lax.rsqrt(square)
        misfit = square * inverse - measured
        kept = 1.0 - measured * inverse
        loss_ref[...] += jnp.sum((misfit * misfit).reshape(INNER // 8, 8, INNER), axis=0)
        weighted = jnp.concatenate([real * kept, imag * kept], axis=0).astype(jnp.bfloat16)
        back = jnp.dot(backward[k], weighted, preferred_element_type=jnp.float32)
        held[k] = back.astype(jnp.bfloat16)
        return carry

    lax.fori_loop(0, OUTER, residual, 0, unroll=2)

    def leave(index, carry):
        at = pl.multiple_of(index * TILE, TILE)

        def load(k):
            return [
                held[k, pl.ds(pl.multiple_of(p * INNER + at, TILE), TILE), :].astype(jnp.float32)
                for p in range(2)
            ]

        def store(n, value):
            source, span = place(n, at)
            for p in range(2):
                out_ref[source, p, span, :] = value[p].astype(jnp.bfloat16)

        fourier64(load, store, middle, 1)
        return carry

    lax.fori_loop(0, slabs, leave, 0)


def columns(chunk, arrived, measured, forward, backward):
    devices, _, share, width = arrived.shape
    length = devices * share
    steps = width // INNER
    return pl.pallas_call(
        functools.partial(columns_kernel, share),
        grid=(steps,),
        in_specs=[
            pl.BlockSpec((devices, 2, share, INNER), lambda i: (0, 0, 0, i)),
            pl.BlockSpec((1, length, INNER), lambda i: (0, 0, chunk * steps + i)),
            pl.BlockSpec(memory_space=pl.ANY),
            pl.BlockSpec(memory_space=pl.ANY),
        ],
        out_specs=[
            pl.BlockSpec((devices, 2, share, INNER), lambda i: (0, 0, 0, i)),
            pl.BlockSpec((8, INNER), lambda i: (0, 0)),
        ],
        out_shape=[
            jax.ShapeDtypeStruct(arrived.shape, jnp.bfloat16),
            jax.ShapeDtypeStruct((8, INNER), jnp.float32),
        ],
        scratch_shapes=[
            pltpu.VMEM((OUTER, 2 * INNER, 2 * INNER), jnp.bfloat16),
            pltpu.VMEM((OUTER, 2 * INNER, 2 * INNER), jnp.bfloat16),
            pltpu.VMEM((OUTER, 2, TILE, INNER), jnp.float32),
            pltpu.VMEM((OUTER, 2 * INNER, INNER), jnp.bfloat16),
            pltpu.SemaphoreType.DMA((2,)),
        ],
        name="columns",
        **parameters(length * width * 2200),
    )(arrived, measured, forward, backward)


def gather_kept(kept, in_ref, table_hbm, table, held, sem):
    slots, masks = in_ref.shape[:2]
    copy = pltpu.make_async_copy(table_hbm.at[:, pl.ds(kept[0], len(kept))], table, sem)

    @pl.when(pl.program_id(0) == 0)
    def _():
        copy.start()
        copy.wait()

    def gather(r, carry):
        for j in range(len(kept)):
            span = slice(j * INNER, (j + 1) * INNER)
            value = jnp.concatenate(
                [
                    jnp.concatenate([in_ref[r, m, p, :, span] for p in range(2)], axis=1)
                    for m in range(masks)
                ],
                axis=0,
            )
            held[r, j] = jnp.dot(value, table[r, j], preferred_element_type=jnp.float32).astype(
                jnp.bfloat16
            )
        return carry

    lax.fori_loop(0, slots, gather, 0, unroll=4)


def held_tile(held, r, j, index):
    take = pl.ds(pl.multiple_of(index * TILE, TILE), TILE)
    return [
        held[r, j, take, p * INNER : (p + 1) * INNER].astype(jnp.float32) for p in range(2)
    ]


def rows_part_kernel(kept, in_ref, table_hbm, out_ref, table, middle, held, sem):
    slots, masks, _, rows, _ = in_ref.shape
    slabs = rows // TILE
    gather_kept(kept, in_ref, table_hbm, table, held, sem)

    def slab(index, carry):
        mask = index // slabs
        at = pl.multiple_of((index % slabs) * TILE, TILE)

        def load(r, j):
            return held_tile(held, r, j, index)

        def store(n, values):
            for j, value in enumerate(values):
                for p in range(2):
                    out_ref[n, j, mask, p, pl.ds(at, TILE), :] = value[p].astype(jnp.bfloat16)

        inverse_part(load, store, middle, kept, OUTER // slots)
        return carry

    lax.fori_loop(0, masks * slabs, slab, 0)


def rows_part(kept, arrived, table):
    slots, masks, _, count, span = arrived.shape
    rows = row_step(count, masks)
    return pl.pallas_call(
        functools.partial(rows_part_kernel, kept),
        grid=(count // rows,),
        in_specs=[
            pl.BlockSpec((slots, masks, 2, rows, span), lambda i: (0, 0, 0, i, 0)),
            pl.BlockSpec(memory_space=pl.ANY),
        ],
        out_specs=pl.BlockSpec(
            (slots, len(kept), masks, 2, rows, INNER), lambda i: (0, 0, 0, 0, i, 0)
        ),
        out_shape=jax.ShapeDtypeStruct(
            (slots, len(kept), masks, 2, count, INNER), jnp.bfloat16
        ),
        scratch_shapes=row_scratch(slots, len(kept), masks, rows),
        name="rows_part",
        **parameters(masks * count * LENGTH * 600),
    )(arrived, table)


def rows_in_kernel(kept, code_ref, in_ref, part_ref, table_hbm, out_ref, table, middle, held,
                   sem):
    slots, masks, _, rows, _ = in_ref.shape
    radix = OUTER // slots
    slabs = rows // TILE
    gather_kept(kept, in_ref, table_hbm, table, held, sem)

    def slab(index, carry, first):
        mask = index // slabs
        at = pl.multiple_of((index % slabs) * TILE, TILE)

        def load(r, j):
            return held_tile(held, r, j, index)

        def store(n, values):
            early = [
                [part_ref[n, j, mask, p, pl.ds(at, TILE), :].astype(jnp.float32) for p in range(2)]
                for j in range(radix - len(kept))
            ]
            for t, value in enumerate(fourier(early + values, 1)):
                tile = n + slots * t
                span = slice(tile * INNER, (tile + 1) * INNER)
                code = code_ref[mask, pl.ds(at, TILE), span].astype(jnp.float32)
                value = rotate(value, code, -1)
                for p in range(2):
                    if first:
                        out_ref[p, pl.ds(at, TILE), span] = value[p]
                    else:
                        out_ref[p, pl.ds(at, TILE), span] += value[p]

        inverse_part(load, store, middle, kept, radix)
        return carry

    lax.fori_loop(0, slabs, functools.partial(slab, first=True), 0)
    lax.fori_loop(slabs, masks * slabs, functools.partial(slab, first=False), 0)


def rows_in(kept, code, arrived, part, table):
    slots, masks, _, count, span = arrived.shape
    rows = row_step(count, masks)
    return pl.pallas_call(
        functools.partial(rows_in_kernel, kept),
        grid=(count // rows,),
        in_specs=[
            pl.BlockSpec((masks, rows, LENGTH), lambda i: (0, i, 0)),
            pl.BlockSpec((slots, masks, 2, rows, span), lambda i: (0, 0, 0, i, 0)),
            pl.BlockSpec((slots,) + part.shape[1:4] + (rows, INNER), lambda i: (0, 0, 0, 0, i, 0)),
            pl.BlockSpec(memory_space=pl.ANY),
        ],
        out_specs=pl.BlockSpec((2, rows, LENGTH), lambda i: (0, i, 0)),
        out_shape=jax.ShapeDtypeStruct((2, count, LENGTH), jnp.float32),
        scratch_shapes=row_scratch(slots, len(kept), masks, rows),
        name="rows_in",
        **parameters(masks * count * LENGTH * 1000),
    )(code, arrived, part, table)


AXES = ("rows", "mask")
CHUNKS = 2


def exchange(blocks):
    flat = blocks.reshape((-1,) + blocks.shape[-3:])
    flat = lax.all_to_all(flat, AXES, split_axis=0, concat_axis=0, tiled=True)
    return flat.reshape(blocks.shape)


def stages(devices):
    bits = devices.bit_length() - 1
    first = -(-bits // 3)
    second = -(-(bits - first) // 2)
    return [2**first, 2**second, 2 ** (bits - first - second)]


def add_over(value, devices, factor, stride):
    total = value
    for d in range(1, factor):
        pairs = []
        for i in range(devices):
            digit = i // stride % factor
            pairs.append((i, i + ((digit + d) % factor - digit) * stride))
        total = total + lax.ppermute(value, AXES, pairs)
    return total


def shards(slots, masks, image, measured, mask_ids):
    forward, backward = (jnp.asarray(table) for table in table_pair())
    _, count, width = image.shape
    devices = slots * masks
    radix = OUTER // slots
    each = radix // CHUNKS
    kept = [tuple(range(c * each, (c + 1) * each)) for c in range(CHUNKS)]
    by_slot = (slots, radix, 2 * INNER, 2 * INNER)
    out_table, in_table = backward.reshape(by_slot), forward.reshape(by_slot)
    ids = [mask_ids] + [
        lax.ppermute(mask_ids, "mask", [((m + d) % masks, m) for m in range(masks)])
        for d in range(1, masks)
    ]
    loss = jnp.zeros((1,), jnp.float32)
    leaving = []
    for c in range(CHUNKS):
        sent, *code = rows_out(kept[c], ids, image, out_table, c == CHUNKS - 1)
        sent, image = lax.optimization_barrier((sent, image))
        arrived = exchange(sent.reshape((-1,) + sent.shape[2:]))
        left, part_loss = columns(c, arrived, measured, forward, backward)
        leaving.append(left.reshape(sent.shape))
        loss = loss + jnp.sum(part_loss)
    first, second, third = stages(devices)
    loss = add_over(loss, devices, first, 1)
    returned = exchange(leaving[0])
    returned, loss = lax.optimization_barrier((returned, loss))
    loss = add_over(loss, devices, second, first)
    part = rows_part(kept[0], returned, in_table)
    last, part, loss = lax.optimization_barrier((exchange(leaving[1]), part, loss))
    loss = add_over(loss, devices, third, first * second)
    gradient = rows_in(kept[1], code[0], last, part, in_table)
    return gradient, loss[0] / (masks * width * width)


def solution(mesh):
    slots, masks = mesh.shape["rows"], mesh.shape["mask"]
    return jax.shard_map(
        functools.partial(shards, slots, masks),
        mesh=mesh,
        in_specs=(P(None, AXES, None), P("mask", None, "rows"), P("mask")),
        out_specs=(P(None, AXES, None), P()),
        check_vma=False,
    )
```

```python
import functools
import math

import jax
import jax.numpy as jnp
import ml_dtypes
import numpy as np
from jax import lax
from jax.experimental import pallas as pl
from jax.experimental.pallas import tpu as pltpu
from jax.sharding import PartitionSpec as P

INNER = 128
OUTER = 64
LENGTH = INNER * OUTER
EPSILON = 0.25
TILE = 16
VMEM_LIMIT = 58 * 1024 * 1024
ROOT_HALF = math.sqrt(0.5)

ROW_MULTIPLIER = 73856093
COLUMN_MULTIPLIER = 19349663
MASK_MULTIPLIER = 83492791
MIX_MULTIPLIER = 1274126177


def wrap(value):
    return (value + 2**31) % 2**32 - 2**31


def add(a, b):
    return (a[0] + b[0], a[1] + b[1])


def sub(a, b):
    return (a[0] - b[0], a[1] - b[1])


def quarter(a, sign):
    return (-a[1], a[0]) if sign > 0 else (a[1], -a[0])


def turn(a, step, count, sign):
    step = step % count
    if step == 0:
        return a
    if 4 * step == count:
        return quarter(a, sign)
    if 2 * step == count:
        return (-a[0], -a[1])
    if 4 * step == 3 * count:
        return quarter(a, -sign)
    if 8 * step == count:
        q = quarter(a, sign)
        return ((a[0] + q[0]) * ROOT_HALF, (a[1] + q[1]) * ROOT_HALF)
    if 8 * step == 3 * count:
        q = quarter(a, sign)
        return ((q[0] - a[0]) * ROOT_HALF, (q[1] - a[1]) * ROOT_HALF)
    angle = sign * 2.0 * math.pi * step / count
    cosine, sine = math.cos(angle), math.sin(angle)
    return (a[0] * cosine - a[1] * sine, a[0] * sine + a[1] * cosine)


def fourier4(x, sign):
    t0, t1 = add(x[0], x[2]), sub(x[0], x[2])
    t2, t3 = add(x[1], x[3]), quarter(sub(x[1], x[3]), sign)
    return [add(t0, t2), add(t1, t3), sub(t0, t2), sub(t1, t3)]


def fourier8(x, sign):
    even = fourier4(x[0::2], sign)
    odd = fourier4(x[1::2], sign)
    odd = [turn(odd[k], k, 8, sign) for k in range(4)]
    return [add(even[k], odd[k]) for k in range(4)] + [sub(even[k], odd[k]) for k in range(4)]


def fourier(x, sign):
    if len(x) == 1:
        return x
    if len(x) == 2:
        return [add(x[0], x[1]), sub(x[0], x[1])]
    return fourier4(x, sign) if len(x) == 4 else fourier8(x, sign)


def fourier64(load, store, middle, sign):
    for b in range(8):
        values = fourier8([load(8 * a + b) for a in range(8)], sign)
        for c in range(8):
            real, imag = turn(values[c], b * c, 64, sign)
            middle[c * 8 + b, 0] = real
            middle[c * 8 + b, 1] = imag
    for c in range(8):
        values = fourier8([(middle[c * 8 + b, 0], middle[c * 8 + b, 1]) for b in range(8)], sign)
        for d in range(8):
            store(c + 8 * d, values[d])


def fourier_part(load, store, middle, kept, radix):
    size = OUTER // radix
    first = size // 4
    for b in range(4):
        groups = [[] for _ in kept]
        for a in range(first):
            n = 4 * a + b
            values = fourier([load(n + size * t) for t in range(radix)], -1)
            for at, j in enumerate(kept):
                groups[at].append(turn(values[j], n * j, OUTER, -1))
        for at in range(len(kept)):
            values = fourier(groups[at], -1)
            for c in range(first):
                real, imag = turn(values[c], b * c, size, -1)
                middle[(at * first + c) * 4 + b, 0] = real
                middle[(at * first + c) * 4 + b, 1] = imag
    for at in range(len(kept)):
        for c in range(first):
            slot = (at * first + c) * 4
            values = fourier4([(middle[slot + b, 0], middle[slot + b, 1]) for b in range(4)], -1)
            for d in range(4):
                store(c + first * d, at, values[d])


def inverse_part(load, store, middle, kept, radix):
    size = OUTER // radix
    first = size // 4
    for at in range(len(kept)):
        for b in range(4):
            values = fourier([load(4 * a + b, at) for a in range(first)], 1)
            for c in range(first):
                real, imag = turn(values[c], b * c, size, 1)
                middle[(at * first + c) * 4 + b, 0] = real
                middle[(at * first + c) * 4 + b, 1] = imag
    for c in range(first):
        sums = []
        for at in range(len(kept)):
            slot = (at * first + c) * 4
            sums.append(
                fourier4([(middle[slot + b, 0], middle[slot + b, 1]) for b in range(4)], 1)
            )
        for d in range(4):
            n = c + first * d
            store(n, [turn(sums[at][d], n * j, OUTER, 1) for at, j in enumerate(kept)])


def fold(mixed):
    return mixed ^ lax.shift_right_logical(mixed, jnp.full(mixed.shape, 13, jnp.int32))


def phase_code(row_term, column_term):
    product = (row_term ^ column_term) * jnp.int32(wrap(4 * MIX_MULTIPLIER))
    code = lax.shift_right_arithmetic(product, jnp.full(product.shape, 30, jnp.int32))
    return code.astype(jnp.float32)


def rotate(value, code, direction):
    size = jnp.abs(code)
    cosine = 1 - size
    sine = code * (2 - size)
    left, right = value[0] * sine, value[1] * sine
    if direction > 0:
        return (value[0] * cosine - right, left + value[1] * cosine)
    return (value[0] * cosine + right, value[1] * cosine - left)


def row_hash(id_refs, base, mask):
    masks = len(id_refs)
    rows = lax.broadcasted_iota(jnp.int32, (TILE, INNER), 0) + base
    ahead = lax.rem(mask - lax.axis_index("mask") + masks, masks)
    mask_id = id_refs[0][0]
    for d in range(1, masks):
        mask_id = jnp.where(ahead == d, id_refs[d][0], mask_id)
    mask_term = (mask_id + 1) * jnp.int32(MASK_MULTIPLIER)
    return fold((rows * jnp.int32(ROW_MULTIPLIER)) ^ mask_term)


def column_hash(tile):
    lanes = lax.broadcasted_iota(jnp.int32, (TILE, INNER), 1)
    shift = jnp.int32(wrap(tile * INNER * COLUMN_MULTIPLIER))
    return fold(lanes * jnp.int32(COLUMN_MULTIPLIER) + shift)


def table_pair():
    inner = np.arange(INNER, dtype=np.int64)
    outer = np.arange(OUTER, dtype=np.int64)
    steps = inner[None, None, :] * (outer[:, None, None] + OUTER * inner[None, :, None]) % LENGTH
    angles = steps * (-2.0 * math.pi / LENGTH)
    cosine, sine = np.cos(angles), np.sin(angles)
    table = np.concatenate(
        [np.concatenate([cosine, -sine], axis=2), np.concatenate([sine, cosine], axis=2)], axis=1
    )
    forward = (table * 2.0**-7).astype(ml_dtypes.bfloat16)
    backward = (table.transpose(0, 2, 1) * 2.0**-6).astype(ml_dtypes.bfloat16)
    return forward, backward


def by_parity(step, last, early, both, late):
    @pl.when(step == 0)
    def _():
        early(0)

    for parity in range(2):

        @pl.when((step > 0) & (step < last) & (step % 2 == parity))
        def _():
            both(1 - parity, parity)

    @pl.when(step == last)
    def _():
        late((last - 1) % 2)


def rows_out_kernel(kept, masks, blocks, *refs):
    id_refs = refs[:masks]
    image_ref, table_hbm, out_ref, *rest = refs[masks:]
    code_ref = rest[0] if len(rest) == 7 else None
    table, middle, held_even, held_odd, column_terms, sem = rest[-6:]
    held = (held_even, held_odd)
    slots, _, _, rows, _ = out_ref.shape
    radix = OUTER // slots
    slabs = rows // TILE
    step = pl.program_id(0)
    device = lax.axis_index("rows") * masks + lax.axis_index("mask")
    copy = pltpu.make_async_copy(table_hbm.at[:, pl.ds(kept[0], len(kept))], table, sem)
    count = masks * slabs
    share = slots // count

    @pl.when(step == 0)
    def _():
        copy.start()
        for n in range(OUTER):
            column_terms[n] = column_hash(n)

    def spread(r, j, read):
        value = jnp.dot(held[read][r, j], table[r, j], preferred_element_type=jnp.float32)
        value = value.astype(jnp.bfloat16)
        for m in range(masks):
            for p in range(2):
                out_ref[r, m, p, :, j * INNER : (j + 1) * INNER] = value[
                    m * rows : (m + 1) * rows, p * INNER : (p + 1) * INNER
                ]

    def slab(index, carry, read, write):
        mask = index // slabs
        at = pl.multiple_of((index % slabs) * TILE, TILE)
        row_term = row_hash(id_refs, (device * blocks + step) * rows + at, mask)
        dots = [] if read is None else [(i, j) for i in range(share) for j in range(len(kept))]
        every = OUTER // max(len(dots), 1)
        calls = []

        def load(n):
            if dots and len(calls) % every == 0:
                i, j = dots[len(calls) // every]
                spread(index * share + i, j, read)
            calls.append(n)
            code = phase_code(row_term, column_terms[n])
            span = slice(n * INNER, (n + 1) * INNER)
            if code_ref is not None:
                code_ref[mask, pl.ds(at, TILE), span] = code.astype(jnp.bfloat16)
            value = [image_ref[p, pl.ds(at, TILE), span].astype(jnp.float32) for p in range(2)]
            return rotate(value, code, 1)

        def store(r, j, value):
            to = pl.ds(pl.multiple_of(index * TILE, TILE), TILE)
            held[write][r, j, to, 0:INNER] = value[0].astype(jnp.bfloat16)
            held[write][r, j, to, INNER:] = value[1].astype(jnp.bfloat16)

        fourier_part(load, store, middle, kept, radix)
        return carry

    def early(write):
        lax.fori_loop(0, count, functools.partial(slab, read=None, write=write), 0)
        copy.wait()

    def both(read, write):
        lax.fori_loop(0, count, functools.partial(slab, read=read, write=write), 0)

    def late(read):
        def some(index, carry):
            for i in range(share):
                for j in range(len(kept)):
                    spread(index * share + i, j, read)
            return carry

        lax.fori_loop(0, count, some, 0, unroll=2)

    by_parity(step, blocks, early, both, late)


def row_step(count, masks):
    return min(count, max(TILE, 128 // masks))


def row_scratch(slots, kept, masks, rows, buffers):
    held = pltpu.VMEM((slots, kept, masks * rows, 2 * INNER), jnp.bfloat16)
    return [
        pltpu.VMEM((slots, kept, 2 * INNER, 2 * INNER), jnp.bfloat16),
        pltpu.VMEM((slots * kept, 2, TILE, INNER), jnp.float32),
    ] + [held] * buffers


def parameters(flops):
    return {
        "compiler_params": pltpu.CompilerParams(
            vmem_limit_bytes=VMEM_LIMIT, dimension_semantics=("arbitrary",)
        ),
        "cost_estimate": pl.CostEstimate(
            flops=flops, bytes_accessed=40 << 20, transcendentals=0
        ),
    }


def rows_out(kept, ids, image, table, with_code):
    masks = len(ids)
    _, count, width = image.shape
    slots = table.shape[0]
    rows = row_step(count, masks)
    blocks = count // rows
    span = len(kept) * INNER

    def now(i):
        return jnp.minimum(i, blocks - 1)

    def before(i):
        return jnp.maximum(i - 1, 0)

    return pl.pallas_call(
        functools.partial(rows_out_kernel, kept, masks, blocks),
        grid=(blocks + 1,),
        in_specs=[pl.BlockSpec(memory_space=pltpu.SMEM)] * masks
        + [
            pl.BlockSpec((2, rows, width), lambda i: (0, now(i), 0)),
            pl.BlockSpec(memory_space=pl.ANY),
        ],
        out_specs=[
            pl.BlockSpec((slots, masks, 2, rows, span), lambda i: (0, 0, 0, before(i), 0)),
            pl.BlockSpec((masks, rows, width), lambda i: (0, now(i), 0)),
        ][: 1 + with_code],
        out_shape=[
            jax.ShapeDtypeStruct((slots, masks, 2, count, span), jnp.bfloat16),
            jax.ShapeDtypeStruct((masks, count, width), jnp.bfloat16),
        ][: 1 + with_code],
        scratch_shapes=row_scratch(slots, len(kept), masks, rows, 2)
        + [pltpu.VMEM((OUTER, TILE, INNER), jnp.int32), pltpu.SemaphoreType.DMA],
        name="rows_out",
        **parameters(masks * count * width * 1000),
    )(*ids, image, table)


def columns_kernel(share, in_ref, measured_ref, forward_hbm, backward_hbm, out_ref, loss_ref,
                   forward, backward, middle, held, sems):
    copies = [
        pltpu.make_async_copy(forward_hbm, forward, sems.at[0]),
        pltpu.make_async_copy(backward_hbm, backward, sems.at[1]),
    ]

    @pl.when(pl.program_id(0) == 0)
    def _():
        for copy in copies:
            copy.start()
        loss_ref[...] = jnp.zeros_like(loss_ref)

    slabs = INNER // TILE

    def place(n, at):
        if share >= INNER:
            per = share // INNER
            return n // per, pl.ds(pl.multiple_of((n % per) * INNER + at, TILE), TILE)
        return (n * (INNER // share) + at // share, pl.ds(pl.multiple_of(at % share, TILE), TILE))

    def arrive(index, carry):
        at = pl.multiple_of(index * TILE, TILE)

        def load(n):
            source, span = place(n, at)
            return [in_ref[source, p, span, :].astype(jnp.float32) for p in range(2)]

        def store(k, value):
            for p in range(2):
                to = pl.ds(pl.multiple_of(p * INNER + at, TILE), TILE)
                held[k, to, :] = value[p].astype(jnp.bfloat16)

        fourier64(load, store, middle, -1)
        return carry

    lax.fori_loop(0, slabs, arrive, 0)

    @pl.when(pl.program_id(0) == 0)
    def _():
        for copy in copies:
            copy.wait()

    def residual(k, carry):
        spectrum = jnp.dot(forward[k], held[k], preferred_element_type=jnp.float32)
        real, imag = spectrum[:INNER], spectrum[INNER:]
        measured = measured_ref[
            0, pl.ds(pl.multiple_of(k * INNER, INNER), INNER), :
        ].astype(jnp.float32)
        square = real * real + imag * imag + EPSILON
        inverse = lax.rsqrt(square)
        misfit = square * inverse - measured
        kept = 1.0 - measured * inverse
        loss_ref[...] += jnp.sum((misfit * misfit).reshape(INNER // 8, 8, INNER), axis=0)
        weighted = jnp.concatenate([real * kept, imag * kept], axis=0).astype(jnp.bfloat16)
        back = jnp.dot(backward[k], weighted, preferred_element_type=jnp.float32)
        held[k] = back.astype(jnp.bfloat16)
        return carry

    lax.fori_loop(0, OUTER, residual, 0, unroll=2)

    def leave(index, carry):
        at = pl.multiple_of(index * TILE, TILE)

        def load(k):
            return [
                held[k, pl.ds(pl.multiple_of(p * INNER + at, TILE), TILE), :].astype(jnp.float32)
                for p in range(2)
            ]

        def store(n, value):
            source, span = place(n, at)
            for p in range(2):
                out_ref[source, p, span, :] = value[p].astype(jnp.bfloat16)

        fourier64(load, store, middle, 1)
        return carry

    lax.fori_loop(0, slabs, leave, 0)


def columns(chunk, arrived, measured, forward, backward):
    devices, _, share, width = arrived.shape
    length = devices * share
    steps = width // INNER
    return pl.pallas_call(
        functools.partial(columns_kernel, share),
        grid=(steps,),
        in_specs=[
            pl.BlockSpec((devices, 2, share, INNER), lambda i: (0, 0, 0, i)),
            pl.BlockSpec((1, length, INNER), lambda i: (0, 0, chunk * steps + i)),
            pl.BlockSpec(memory_space=pl.ANY),
            pl.BlockSpec(memory_space=pl.ANY),
        ],
        out_specs=[
            pl.BlockSpec((devices, 2, share, INNER), lambda i: (0, 0, 0, i)),
            pl.BlockSpec((8, INNER), lambda i: (0, 0)),
        ],
        out_shape=[
            jax.ShapeDtypeStruct(arrived.shape, jnp.bfloat16),
            jax.ShapeDtypeStruct((8, INNER), jnp.float32),
        ],
        scratch_shapes=[
            pltpu.VMEM((OUTER, 2 * INNER, 2 * INNER), jnp.bfloat16),
            pltpu.VMEM((OUTER, 2 * INNER, 2 * INNER), jnp.bfloat16),
            pltpu.VMEM((OUTER, 2, TILE, INNER), jnp.float32),
            pltpu.VMEM((OUTER, 2 * INNER, INNER), jnp.bfloat16),
            pltpu.SemaphoreType.DMA((2,)),
        ],
        name="columns",
        **parameters(length * width * 2200),
    )(arrived, measured, forward, backward)


def gather_one(r, j, in_ref, table, held):
    masks = in_ref.shape[1]
    span = slice(j * INNER, (j + 1) * INNER)
    value = jnp.concatenate(
        [
            jnp.concatenate([in_ref[r, m, p, :, span] for p in range(2)], axis=1)
            for m in range(masks)
        ],
        axis=0,
    )
    held[r, j] = jnp.dot(value, table[r, j], preferred_element_type=jnp.float32).astype(
        jnp.bfloat16
    )


def gather_all(kept, in_ref, table, held):
    def some(r, carry):
        for j in range(len(kept)):
            gather_one(r, j, in_ref, table, held)
        return carry

    lax.fori_loop(0, in_ref.shape[0], some, 0, unroll=4)


def fetch_table(kept, table_hbm, table, sem):
    copy = pltpu.make_async_copy(table_hbm.at[:, pl.ds(kept[0], len(kept))], table, sem)

    @pl.when(pl.program_id(0) == 0)
    def _():
        copy.start()
        copy.wait()


def held_tile(held, r, j, index):
    take = pl.ds(pl.multiple_of(index * TILE, TILE), TILE)
    return [
        held[r, j, take, p * INNER : (p + 1) * INNER].astype(jnp.float32) for p in range(2)
    ]


def rows_part_kernel(kept, in_ref, table_hbm, out_ref, table, middle, held, sem):
    slots, masks, _, rows, _ = in_ref.shape
    slabs = rows // TILE
    fetch_table(kept, table_hbm, table, sem)
    gather_all(kept, in_ref, table, held)

    def slab(index, carry):
        mask = index // slabs
        at = pl.multiple_of((index % slabs) * TILE, TILE)

        def load(r, j):
            return held_tile(held, r, j, index)

        def store(n, values):
            for j, value in enumerate(values):
                for p in range(2):
                    out_ref[n, j, mask, p, pl.ds(at, TILE), :] = value[p].astype(jnp.bfloat16)

        inverse_part(load, store, middle, kept, OUTER // slots)
        return carry

    lax.fori_loop(0, masks * slabs, slab, 0)


def rows_part(kept, arrived, table):
    slots, masks, _, count, span = arrived.shape
    rows = row_step(count, masks)
    return pl.pallas_call(
        functools.partial(rows_part_kernel, kept),
        grid=(count // rows,),
        in_specs=[
            pl.BlockSpec((slots, masks, 2, rows, span), lambda i: (0, 0, 0, i, 0)),
            pl.BlockSpec(memory_space=pl.ANY),
        ],
        out_specs=pl.BlockSpec(
            (slots, len(kept), masks, 2, rows, INNER), lambda i: (0, 0, 0, 0, i, 0)
        ),
        out_shape=jax.ShapeDtypeStruct(
            (slots, len(kept), masks, 2, count, INNER), jnp.bfloat16
        ),
        scratch_shapes=row_scratch(slots, len(kept), masks, rows, 1)
        + [pltpu.SemaphoreType.DMA],
        name="rows_part",
        **parameters(masks * count * LENGTH * 600),
    )(arrived, table)


def rows_in_kernel(kept, blocks, code_ref, in_ref, part_ref, table_hbm, out_ref, table, middle,
                   held_even, held_odd, sem):
    held = (held_even, held_odd)
    slots, masks, _, rows, _ = in_ref.shape
    radix = OUTER // slots
    slabs = rows // TILE
    count = masks * slabs
    share = slots // count
    fetch_table(kept, table_hbm, table, sem)

    def slab(index, carry, first, read, write):
        mask = index // slabs
        at = pl.multiple_of((index % slabs) * TILE, TILE)
        dots = [] if write is None else [(i, j) for i in range(share) for j in range(len(kept))]
        every = slots * len(kept) // max(len(dots), 1)
        calls = []

        def load(r, j):
            if dots and len(calls) % every == 0:
                i, k = dots[len(calls) // every]
                gather_one(index * share + i, k, in_ref, table, held[write])
            calls.append(r)
            return held_tile(held[read], r, j, index)

        def store(n, values):
            early = [
                [part_ref[n, j, mask, p, pl.ds(at, TILE), :].astype(jnp.float32) for p in range(2)]
                for j in range(radix - len(kept))
            ]
            for t, value in enumerate(fourier(early + values, 1)):
                tile = n + slots * t
                span = slice(tile * INNER, (tile + 1) * INNER)
                code = code_ref[mask, pl.ds(at, TILE), span].astype(jnp.float32)
                value = rotate(value, code, -1)
                for p in range(2):
                    if first:
                        out_ref[p, pl.ds(at, TILE), span] = value[p]
                    else:
                        out_ref[p, pl.ds(at, TILE), span] += value[p]

        inverse_part(load, store, middle, kept, radix)
        return carry

    def early(write):
        gather_all(kept, in_ref, table, held[write])

    def both(read, write):
        pair = {"read": read, "write": write}
        lax.fori_loop(0, slabs, functools.partial(slab, first=True, **pair), 0)
        lax.fori_loop(slabs, count, functools.partial(slab, first=False, **pair), 0)

    def late(read):
        both(read, None)

    by_parity(pl.program_id(0), blocks, early, both, late)


def rows_in(kept, code, arrived, part, table):
    slots, masks, _, count, span = arrived.shape
    rows = row_step(count, masks)
    blocks = count // rows

    def now(i):
        return jnp.minimum(i, blocks - 1)

    def before(i):
        return jnp.maximum(i - 1, 0)

    return pl.pallas_call(
        functools.partial(rows_in_kernel, kept, blocks),
        grid=(blocks + 1,),
        in_specs=[
            pl.BlockSpec((masks, rows, LENGTH), lambda i: (0, before(i), 0)),
            pl.BlockSpec((slots, masks, 2, rows, span), lambda i: (0, 0, 0, now(i), 0)),
            pl.BlockSpec(
                (slots,) + part.shape[1:4] + (rows, INNER), lambda i: (0, 0, 0, 0, before(i), 0)
            ),
            pl.BlockSpec(memory_space=pl.ANY),
        ],
        out_specs=pl.BlockSpec((2, rows, LENGTH), lambda i: (0, before(i), 0)),
        out_shape=jax.ShapeDtypeStruct((2, count, LENGTH), jnp.float32),
        scratch_shapes=row_scratch(slots, len(kept), masks, rows, 2)
        + [pltpu.SemaphoreType.DMA],
        name="rows_in",
        **parameters(masks * count * LENGTH * 1000),
    )(code, arrived, part, table)


AXES = ("rows", "mask")
CHUNKS = 2


def exchange(blocks):
    flat = blocks.reshape((-1,) + blocks.shape[-3:])
    flat = lax.all_to_all(flat, AXES, split_axis=0, concat_axis=0, tiled=True)
    return flat.reshape(blocks.shape)


def stages(devices):
    bits = devices.bit_length() - 1
    first = -(-bits // 3)
    second = -(-(bits - first) // 2)
    return [2**first, 2**second, 2 ** (bits - first - second)]


def add_over(value, devices, factor, stride):
    total = value
    for d in range(1, factor):
        pairs = []
        for i in range(devices):
            digit = i // stride % factor
            pairs.append((i, i + ((digit + d) % factor - digit) * stride))
        total = total + lax.ppermute(value, AXES, pairs)
    return total


def shards(slots, masks, image, measured, mask_ids):
    forward, backward = (jnp.asarray(table) for table in table_pair())
    _, count, width = image.shape
    devices = slots * masks
    radix = OUTER // slots
    each = radix // CHUNKS
    kept = [tuple(range(c * each, (c + 1) * each)) for c in range(CHUNKS)]
    by_slot = (slots, radix, 2 * INNER, 2 * INNER)
    out_table, in_table = backward.reshape(by_slot), forward.reshape(by_slot)
    ids = [mask_ids] + [
        lax.ppermute(mask_ids, "mask", [((m + d) % masks, m) for m in range(masks)])
        for d in range(1, masks)
    ]
    loss = jnp.zeros((1,), jnp.float32)
    leaving = []
    for c in range(CHUNKS):
        sent, *code = rows_out(kept[c], ids, image, out_table, c == CHUNKS - 1)
        sent, image = lax.optimization_barrier((sent, image))
        arrived = exchange(sent.reshape((-1,) + sent.shape[2:]))
        left, part_loss = columns(c, arrived, measured, forward, backward)
        leaving.append(left.reshape(sent.shape))
        loss = loss + jnp.sum(part_loss)
    first, second, third = stages(devices)
    loss = add_over(loss, devices, first, 1)
    returned = exchange(leaving[0])
    returned, loss = lax.optimization_barrier((returned, loss))
    loss = add_over(loss, devices, second, first)
    part = rows_part(kept[0], returned, in_table)
    last, part, loss = lax.optimization_barrier((exchange(leaving[1]), part, loss))
    loss = add_over(loss, devices, third, first * second)
    gradient = rows_in(kept[1], code[0], last, part, in_table)
    return gradient, loss[0] / (masks * width * width)


def solution(mesh):
    slots, masks = mesh.shape["rows"], mesh.shape["mask"]
    return jax.shard_map(
        functools.partial(shards, slots, masks),
        mesh=mesh,
        in_specs=(P(None, AXES, None), P("mask", None, "rows"), P("mask")),
        out_specs=(P(None, AXES, None), P()),
        check_vma=False,
    )
```

```python
import functools
import math

import jax
import jax.numpy as jnp
import ml_dtypes
import numpy as np
from jax import lax
from jax.experimental import pallas as pl
from jax.experimental.pallas import tpu as pltpu
from jax.sharding import PartitionSpec as P

INNER = 128
OUTER = 64
LENGTH = INNER * OUTER
EPSILON = 0.25
TILE = 16
HALVES = 2
VMEM_LIMIT = 58 * 1024 * 1024
ROOT_HALF = math.sqrt(0.5)

ROW_MULTIPLIER = 73856093
COLUMN_MULTIPLIER = 19349663
MASK_MULTIPLIER = 83492791
MIX_MULTIPLIER = 1274126177


def wrap(value):
    return (value + 2**31) % 2**32 - 2**31


def add(a, b):
    return (a[0] + b[0], a[1] + b[1])


def sub(a, b):
    return (a[0] - b[0], a[1] - b[1])


def quarter(a, sign):
    return (-a[1], a[0]) if sign > 0 else (a[1], -a[0])


def turn(a, step, count, sign):
    step = step % count
    if step == 0:
        return a
    if 4 * step == count:
        return quarter(a, sign)
    if 2 * step == count:
        return (-a[0], -a[1])
    if 4 * step == 3 * count:
        return quarter(a, -sign)
    if 8 * step == count:
        q = quarter(a, sign)
        return ((a[0] + q[0]) * ROOT_HALF, (a[1] + q[1]) * ROOT_HALF)
    if 8 * step == 3 * count:
        q = quarter(a, sign)
        return ((q[0] - a[0]) * ROOT_HALF, (q[1] - a[1]) * ROOT_HALF)
    angle = sign * 2.0 * math.pi * step / count
    cosine, sine = math.cos(angle), math.sin(angle)
    return (a[0] * cosine - a[1] * sine, a[0] * sine + a[1] * cosine)


def fourier4(x, sign):
    t0, t1 = add(x[0], x[2]), sub(x[0], x[2])
    t2, t3 = add(x[1], x[3]), quarter(sub(x[1], x[3]), sign)
    return [add(t0, t2), add(t1, t3), sub(t0, t2), sub(t1, t3)]


def fourier8(x, sign):
    even = fourier4(x[0::2], sign)
    odd = fourier4(x[1::2], sign)
    odd = [turn(odd[k], k, 8, sign) for k in range(4)]
    return [add(even[k], odd[k]) for k in range(4)] + [sub(even[k], odd[k]) for k in range(4)]


def fourier(x, sign):
    if len(x) == 1:
        return x
    if len(x) == 2:
        return [add(x[0], x[1]), sub(x[0], x[1])]
    return fourier4(x, sign) if len(x) == 4 else fourier8(x, sign)


def fourier64(load, store, middle, sign):
    for b in range(8):
        values = fourier8([load(8 * a + b) for a in range(8)], sign)
        for c in range(8):
            real, imag = turn(values[c], b * c, 64, sign)
            middle[c * 8 + b, 0] = real
            middle[c * 8 + b, 1] = imag
    for c in range(8):
        values = fourier8([(middle[c * 8 + b, 0], middle[c * 8 + b, 1]) for b in range(8)], sign)
        for d in range(8):
            store(c + 8 * d, values[d])


def fourier_part(load, store, middle, kept, radix):
    size = OUTER // radix
    first = size // 4
    for b in range(4):
        groups = [[] for _ in kept]
        for a in range(first):
            n = 4 * a + b
            values = fourier([load(n + size * t) for t in range(radix)], -1)
            for at, j in enumerate(kept):
                groups[at].append(turn(values[j], n * j, OUTER, -1))
        for at in range(len(kept)):
            values = fourier(groups[at], -1)
            for c in range(first):
                real, imag = turn(values[c], b * c, size, -1)
                middle[(at * first + c) * 4 + b, 0] = real
                middle[(at * first + c) * 4 + b, 1] = imag
    for at in range(len(kept)):
        for c in range(first):
            slot = (at * first + c) * 4
            values = fourier4([(middle[slot + b, 0], middle[slot + b, 1]) for b in range(4)], -1)
            for d in range(4):
                store(c + first * d, at, values[d])


def inverse_part(load, store, middle, kept, radix):
    size = OUTER // radix
    first = size // 4
    for at in range(len(kept)):
        for b in range(4):
            values = fourier([load(4 * a + b, at) for a in range(first)], 1)
            for c in range(first):
                real, imag = turn(values[c], b * c, size, 1)
                middle[(at * first + c) * 4 + b, 0] = real
                middle[(at * first + c) * 4 + b, 1] = imag
    for c in range(first):
        sums = []
        for at in range(len(kept)):
            slot = (at * first + c) * 4
            sums.append(
                fourier4([(middle[slot + b, 0], middle[slot + b, 1]) for b in range(4)], 1)
            )
        for d in range(4):
            n = c + first * d
            store(n, [turn(sums[at][d], n * j, OUTER, 1) for at, j in enumerate(kept)])


def fold(mixed):
    return mixed ^ lax.shift_right_logical(mixed, jnp.full(mixed.shape, 13, jnp.int32))


def phase_code(row_term, column_term):
    product = (row_term ^ column_term) * jnp.int32(wrap(4 * MIX_MULTIPLIER))
    code = lax.shift_right_arithmetic(product, jnp.full(product.shape, 30, jnp.int32))
    return code.astype(jnp.float32)


def rotate(value, code, direction):
    size = jnp.abs(code)
    cosine = 1 - size
    sine = code * (2 - size)
    left, right = value[0] * sine, value[1] * sine
    if direction > 0:
        return (value[0] * cosine - right, left + value[1] * cosine)
    return (value[0] * cosine + right, value[1] * cosine - left)


def row_hash(id_refs, base, mask):
    masks = len(id_refs)
    rows = lax.broadcasted_iota(jnp.int32, (TILE, INNER), 0) + base
    ahead = lax.rem(mask - lax.axis_index("mask") + masks, masks)
    mask_id = id_refs[0][0]
    for d in range(1, masks):
        mask_id = jnp.where(ahead == d, id_refs[d][0], mask_id)
    mask_term = (mask_id + 1) * jnp.int32(MASK_MULTIPLIER)
    return fold((rows * jnp.int32(ROW_MULTIPLIER)) ^ mask_term)


def column_hash(tile):
    lanes = lax.broadcasted_iota(jnp.int32, (TILE, INNER), 1)
    shift = jnp.int32(wrap(tile * INNER * COLUMN_MULTIPLIER))
    return fold(lanes * jnp.int32(COLUMN_MULTIPLIER) + shift)


def table_pair():
    inner = np.arange(INNER, dtype=np.int64)
    outer = np.arange(OUTER, dtype=np.int64)
    steps = inner[None, None, :] * (outer[:, None, None] + OUTER * inner[None, :, None]) % LENGTH
    angles = steps * (-2.0 * math.pi / LENGTH)
    cosine, sine = np.cos(angles), np.sin(angles)
    table = np.concatenate(
        [np.concatenate([cosine, -sine], axis=2), np.concatenate([sine, cosine], axis=2)], axis=1
    )
    forward = (table * 2.0**-7).astype(ml_dtypes.bfloat16)
    backward = (table.transpose(0, 2, 1) * 2.0**-6).astype(ml_dtypes.bfloat16)
    return forward, backward


def by_parity(step, last, early, both, late):
    @pl.when(step == 0)
    def _():
        early(0)

    for parity in range(2):

        @pl.when((step > 0) & (step < last) & (step % 2 == parity))
        def _():
            both(1 - parity, parity)

    @pl.when(step == last)
    def _():
        late((last - 1) % 2)


def rows_out_kernel(kept, masks, blocks, *refs):
    id_refs = refs[:masks]
    image_ref, table_hbm, out_ref, *rest = refs[masks:]
    code_ref = rest[0] if len(rest) == 7 else None
    table, middle, held_even, held_odd, column_terms, sem = rest[-6:]
    held = (held_even, held_odd)
    near, _, halves, _, rows, _ = out_ref.shape
    slots = halves * near
    radix = OUTER // slots
    slabs = rows // TILE
    step = pl.program_id(0)
    device = (lax.axis_index("half") * near + lax.axis_index("row")) * masks
    device = device + lax.axis_index("mask")
    copy = pltpu.make_async_copy(table_hbm.at[:, pl.ds(kept[0], len(kept))], table, sem)
    count = masks * slabs
    share = slots // count

    @pl.when(step == 0)
    def _():
        copy.start()
        for n in range(OUTER):
            column_terms[n] = column_hash(n)

    def spread(r, j, read):
        value = jnp.dot(held[read][r, j], table[r, j], preferred_element_type=jnp.float32)
        value = value.astype(jnp.bfloat16)
        span = slice(j * INNER, (j + 1) * INNER)
        for m in range(masks):
            for p in range(2):
                out_ref[lax.rem(r, near), m, lax.div(r, near), p, :, span] = value[
                    m * rows : (m + 1) * rows, p * INNER : (p + 1) * INNER
                ]

    def slab(index, carry, read, write):
        mask = index // slabs
        at = pl.multiple_of((index % slabs) * TILE, TILE)
        row_term = row_hash(id_refs, (device * blocks + step) * rows + at, mask)
        dots = [] if read is None else [(i, j) for i in range(share) for j in range(len(kept))]
        every = OUTER // max(len(dots), 1)
        calls = []

        def load(n):
            if dots and len(calls) % every == 0:
                i, j = dots[len(calls) // every]
                spread(index * share + i, j, read)
            calls.append(n)
            code = phase_code(row_term, column_terms[n])
            span = slice(n * INNER, (n + 1) * INNER)
            if code_ref is not None:
                code_ref[mask, pl.ds(at, TILE), span] = code.astype(jnp.bfloat16)
            value = [image_ref[p, pl.ds(at, TILE), span].astype(jnp.float32) for p in range(2)]
            return rotate(value, code, 1)

        def store(r, j, value):
            to = pl.ds(pl.multiple_of(index * TILE, TILE), TILE)
            held[write][r, j, to, 0:INNER] = value[0].astype(jnp.bfloat16)
            held[write][r, j, to, INNER:] = value[1].astype(jnp.bfloat16)

        fourier_part(load, store, middle, kept, radix)
        return carry

    def early(write):
        lax.fori_loop(0, count, functools.partial(slab, read=None, write=write), 0)
        copy.wait()

    def both(read, write):
        lax.fori_loop(0, count, functools.partial(slab, read=read, write=write), 0)

    def late(read):
        def some(index, carry):
            for i in range(share):
                for j in range(len(kept)):
                    spread(index * share + i, j, read)
            return carry

        lax.fori_loop(0, count, some, 0, unroll=2)

    by_parity(step, blocks, early, both, late)


def row_step(count, masks):
    return min(count, max(TILE, 128 // masks))


def row_scratch(slots, kept, masks, rows, buffers):
    held = pltpu.VMEM((slots, kept, masks * rows, 2 * INNER), jnp.bfloat16)
    return [
        pltpu.VMEM((slots, kept, 2 * INNER, 2 * INNER), jnp.bfloat16),
        pltpu.VMEM((slots * kept, 2, TILE, INNER), jnp.float32),
    ] + [held] * buffers


def parameters(flops):
    return {
        "compiler_params": pltpu.CompilerParams(
            vmem_limit_bytes=VMEM_LIMIT, dimension_semantics=("arbitrary",)
        ),
        "cost_estimate": pl.CostEstimate(
            flops=flops, bytes_accessed=40 << 20, transcendentals=0
        ),
    }


def rows_out(kept, ids, image, table, with_code):
    masks = len(ids)
    _, count, width = image.shape
    slots = table.shape[0]
    rows = row_step(count, masks)
    blocks = count // rows
    span = len(kept) * INNER

    def now(i):
        return jnp.minimum(i, blocks - 1)

    def before(i):
        return jnp.maximum(i - 1, 0)

    return pl.pallas_call(
        functools.partial(rows_out_kernel, kept, masks, blocks),
        grid=(blocks + 1,),
        in_specs=[pl.BlockSpec(memory_space=pltpu.SMEM)] * masks
        + [
            pl.BlockSpec((2, rows, width), lambda i: (0, now(i), 0)),
            pl.BlockSpec(memory_space=pl.ANY),
        ],
        out_specs=[
            pl.BlockSpec(
                (slots // HALVES, masks, HALVES, 2, rows, span),
                lambda i: (0, 0, 0, 0, before(i), 0),
            ),
            pl.BlockSpec((masks, rows, width), lambda i: (0, now(i), 0)),
        ][: 1 + with_code],
        out_shape=[
            jax.ShapeDtypeStruct(
                (slots // HALVES, masks, HALVES, 2, count, span), jnp.bfloat16
            ),
            jax.ShapeDtypeStruct((masks, count, width), jnp.bfloat16),
        ][: 1 + with_code],
        scratch_shapes=row_scratch(slots, len(kept), masks, rows, 2)
        + [pltpu.VMEM((OUTER, TILE, INNER), jnp.int32), pltpu.SemaphoreType.DMA],
        name="rows_out",
        **parameters(masks * count * width * 1000),
    )(*ids, image, table)


def columns_kernel(masks, share, in_ref, measured_ref, forward_hbm, backward_hbm, out_ref, loss_ref,
                   forward, backward, middle, held, sems):
    copies = [
        pltpu.make_async_copy(forward_hbm, forward, sems.at[0]),
        pltpu.make_async_copy(backward_hbm, backward, sems.at[1]),
    ]

    @pl.when(pl.program_id(0) == 0)
    def _():
        for copy in copies:
            copy.start()
        loss_ref[...] = jnp.zeros_like(loss_ref)

    slabs = INNER // TILE

    near = in_ref.shape[0] // (masks * HALVES)

    def position(source):
        row, mask = source // masks, source % masks
        return ((row % near) * masks + mask) * HALVES + row // near

    def place(n, at):
        if share >= INNER:
            per = share // INNER
            span = pl.ds(pl.multiple_of((n % per) * INNER + at, TILE), TILE)
            return position(n // per), span
        span = pl.ds(pl.multiple_of(at % share, TILE), TILE)
        return position(n * (INNER // share) + at // share), span

    def arrive(index, carry):
        at = pl.multiple_of(index * TILE, TILE)

        def load(n):
            source, span = place(n, at)
            return [in_ref[source, p, span, :].astype(jnp.float32) for p in range(2)]

        def store(k, value):
            for p in range(2):
                to = pl.ds(pl.multiple_of(p * INNER + at, TILE), TILE)
                held[k, to, :] = value[p].astype(jnp.bfloat16)

        fourier64(load, store, middle, -1)
        return carry

    lax.fori_loop(0, slabs, arrive, 0)

    @pl.when(pl.program_id(0) == 0)
    def _():
        for copy in copies:
            copy.wait()

    def residual(k, carry):
        spectrum = jnp.dot(forward[k], held[k], preferred_element_type=jnp.float32)
        real, imag = spectrum[:INNER], spectrum[INNER:]
        measured = measured_ref[
            0, pl.ds(pl.multiple_of(k * INNER, INNER), INNER), :
        ].astype(jnp.float32)
        square = real * real + imag * imag + EPSILON
        inverse = lax.rsqrt(square)
        misfit = square * inverse - measured
        kept = 1.0 - measured * inverse
        loss_ref[...] += jnp.sum((misfit * misfit).reshape(INNER // 8, 8, INNER), axis=0)
        weighted = jnp.concatenate([real * kept, imag * kept], axis=0).astype(jnp.bfloat16)
        back = jnp.dot(backward[k], weighted, preferred_element_type=jnp.float32)
        held[k] = back.astype(jnp.bfloat16)
        return carry

    lax.fori_loop(0, OUTER, residual, 0, unroll=2)

    def leave(index, carry):
        at = pl.multiple_of(index * TILE, TILE)

        def load(k):
            return [
                held[k, pl.ds(pl.multiple_of(p * INNER + at, TILE), TILE), :].astype(jnp.float32)
                for p in range(2)
            ]

        def store(n, value):
            source, span = place(n, at)
            for p in range(2):
                out_ref[source, p, span, :] = value[p].astype(jnp.bfloat16)

        fourier64(load, store, middle, 1)
        return carry

    lax.fori_loop(0, slabs, leave, 0)


def columns(chunk, masks, arrived, measured, forward, backward):
    devices, _, share, width = arrived.shape
    length = devices * share
    steps = width // INNER
    return pl.pallas_call(
        functools.partial(columns_kernel, masks, share),
        grid=(steps,),
        in_specs=[
            pl.BlockSpec((devices, 2, share, INNER), lambda i: (0, 0, 0, i)),
            pl.BlockSpec((1, length, INNER), lambda i: (0, 0, chunk * steps + i)),
            pl.BlockSpec(memory_space=pl.ANY),
            pl.BlockSpec(memory_space=pl.ANY),
        ],
        out_specs=[
            pl.BlockSpec((devices, 2, share, INNER), lambda i: (0, 0, 0, i)),
            pl.BlockSpec((8, INNER), lambda i: (0, 0)),
        ],
        out_shape=[
            jax.ShapeDtypeStruct(arrived.shape, jnp.bfloat16),
            jax.ShapeDtypeStruct((8, INNER), jnp.float32),
        ],
        scratch_shapes=[
            pltpu.VMEM((OUTER, 2 * INNER, 2 * INNER), jnp.bfloat16),
            pltpu.VMEM((OUTER, 2 * INNER, 2 * INNER), jnp.bfloat16),
            pltpu.VMEM((OUTER, 2, TILE, INNER), jnp.float32),
            pltpu.VMEM((OUTER, 2 * INNER, INNER), jnp.bfloat16),
            pltpu.SemaphoreType.DMA((2,)),
        ],
        name="columns",
        **parameters(length * width * 2200),
    )(arrived, measured, forward, backward)


def gather_one(r, j, in_ref, table, held):
    near, masks = in_ref.shape[:2]
    span = slice(j * INNER, (j + 1) * INNER)
    at, half = lax.rem(r, near), lax.div(r, near)
    value = jnp.concatenate(
        [
            jnp.concatenate([in_ref[at, m, half, p, :, span] for p in range(2)], axis=1)
            for m in range(masks)
        ],
        axis=0,
    )
    held[r, j] = jnp.dot(value, table[r, j], preferred_element_type=jnp.float32).astype(
        jnp.bfloat16
    )


def gather_all(kept, in_ref, table, held):
    def some(r, carry):
        for j in range(len(kept)):
            gather_one(r, j, in_ref, table, held)
        return carry

    lax.fori_loop(0, in_ref.shape[0] * HALVES, some, 0, unroll=4)


def fetch_table(kept, table_hbm, table, sem):
    copy = pltpu.make_async_copy(table_hbm.at[:, pl.ds(kept[0], len(kept))], table, sem)

    @pl.when(pl.program_id(0) == 0)
    def _():
        copy.start()
        copy.wait()


def held_tile(held, r, j, index):
    take = pl.ds(pl.multiple_of(index * TILE, TILE), TILE)
    return [
        held[r, j, take, p * INNER : (p + 1) * INNER].astype(jnp.float32) for p in range(2)
    ]


def rows_part_kernel(kept, in_ref, table_hbm, out_ref, table, middle, held, sem):
    near, masks, _, _, rows, _ = in_ref.shape
    slots = near * HALVES
    slabs = rows // TILE
    fetch_table(kept, table_hbm, table, sem)
    gather_all(kept, in_ref, table, held)

    def slab(index, carry):
        mask = index // slabs
        at = pl.multiple_of((index % slabs) * TILE, TILE)

        def load(r, j):
            return held_tile(held, r, j, index)

        def store(n, values):
            for j, value in enumerate(values):
                for p in range(2):
                    out_ref[n, j, mask, p, pl.ds(at, TILE), :] = value[p].astype(jnp.bfloat16)

        inverse_part(load, store, middle, kept, OUTER // slots)
        return carry

    lax.fori_loop(0, masks * slabs, slab, 0)


def rows_part(kept, arrived, table):
    near, masks, _, _, count, span = arrived.shape
    slots = near * HALVES
    rows = row_step(count, masks)
    return pl.pallas_call(
        functools.partial(rows_part_kernel, kept),
        grid=(count // rows,),
        in_specs=[
            pl.BlockSpec((near, masks, HALVES, 2, rows, span), lambda i: (0, 0, 0, 0, i, 0)),
            pl.BlockSpec(memory_space=pl.ANY),
        ],
        out_specs=pl.BlockSpec(
            (slots, len(kept), masks, 2, rows, INNER), lambda i: (0, 0, 0, 0, i, 0)
        ),
        out_shape=jax.ShapeDtypeStruct(
            (slots, len(kept), masks, 2, count, INNER), jnp.bfloat16
        ),
        scratch_shapes=row_scratch(slots, len(kept), masks, rows, 1)
        + [pltpu.SemaphoreType.DMA],
        name="rows_part",
        **parameters(masks * count * LENGTH * 600),
    )(arrived, table)


def rows_in_kernel(kept, blocks, code_ref, in_ref, part_ref, table_hbm, out_ref, table, middle,
                   held_even, held_odd, sem):
    held = (held_even, held_odd)
    near, masks, _, _, rows, _ = in_ref.shape
    slots = near * HALVES
    radix = OUTER // slots
    slabs = rows // TILE
    count = masks * slabs
    share = slots // count
    fetch_table(kept, table_hbm, table, sem)

    def slab(index, carry, first, read, write):
        mask = index // slabs
        at = pl.multiple_of((index % slabs) * TILE, TILE)
        dots = [] if write is None else [(i, j) for i in range(share) for j in range(len(kept))]
        every = slots * len(kept) // max(len(dots), 1)
        calls = []

        def load(r, j):
            if dots and len(calls) % every == 0:
                i, k = dots[len(calls) // every]
                gather_one(index * share + i, k, in_ref, table, held[write])
            calls.append(r)
            return held_tile(held[read], r, j, index)

        def store(n, values):
            early = [
                [part_ref[n, j, mask, p, pl.ds(at, TILE), :].astype(jnp.float32) for p in range(2)]
                for j in range(radix - len(kept))
            ]
            for t, value in enumerate(fourier(early + values, 1)):
                tile = n + slots * t
                span = slice(tile * INNER, (tile + 1) * INNER)
                code = code_ref[mask, pl.ds(at, TILE), span].astype(jnp.float32)
                value = rotate(value, code, -1)
                for p in range(2):
                    if first:
                        out_ref[p, pl.ds(at, TILE), span] = value[p]
                    else:
                        out_ref[p, pl.ds(at, TILE), span] += value[p]

        inverse_part(load, store, middle, kept, radix)
        return carry

    def early(write):
        gather_all(kept, in_ref, table, held[write])

    def both(read, write):
        pair = {"read": read, "write": write}
        lax.fori_loop(0, slabs, functools.partial(slab, first=True, **pair), 0)
        lax.fori_loop(slabs, count, functools.partial(slab, first=False, **pair), 0)

    def late(read):
        both(read, None)

    by_parity(pl.program_id(0), blocks, early, both, late)


def rows_in(kept, code, arrived, part, table):
    near, masks, _, _, count, span = arrived.shape
    slots = near * HALVES
    rows = row_step(count, masks)
    blocks = count // rows

    def now(i):
        return jnp.minimum(i, blocks - 1)

    def before(i):
        return jnp.maximum(i - 1, 0)

    return pl.pallas_call(
        functools.partial(rows_in_kernel, kept, blocks),
        grid=(blocks + 1,),
        in_specs=[
            pl.BlockSpec((masks, rows, LENGTH), lambda i: (0, before(i), 0)),
            pl.BlockSpec(
                (near, masks, HALVES, 2, rows, span), lambda i: (0, 0, 0, 0, now(i), 0)
            ),
            pl.BlockSpec(
                (slots,) + part.shape[1:4] + (rows, INNER), lambda i: (0, 0, 0, 0, before(i), 0)
            ),
            pl.BlockSpec(memory_space=pl.ANY),
        ],
        out_specs=pl.BlockSpec((2, rows, LENGTH), lambda i: (0, before(i), 0)),
        out_shape=jax.ShapeDtypeStruct((2, count, LENGTH), jnp.float32),
        scratch_shapes=row_scratch(slots, len(kept), masks, rows, 2)
        + [pltpu.SemaphoreType.DMA],
        name="rows_in",
        **parameters(masks * count * LENGTH * 1000),
    )(code, arrived, part, table)


AXES = ("half", "row", "mask")
SEND_ORDER = ("row", "mask", "half")
CHUNKS = 2


def exchange(blocks):
    flat = blocks.reshape((-1,) + blocks.shape[-3:])
    flat = lax.all_to_all(flat, SEND_ORDER, split_axis=0, concat_axis=0, tiled=True)
    return flat.reshape(blocks.shape)


def stages(devices):
    bits = devices.bit_length() - 1
    first = -(-bits // 3)
    second = -(-(bits - first) // 2)
    return [2**first, 2**second, 2 ** (bits - first - second)]


def add_over(value, devices, factor, stride):
    total = value
    for d in range(1, factor):
        pairs = []
        for i in range(devices):
            digit = i // stride % factor
            pairs.append((i, i + ((digit + d) % factor - digit) * stride))
        total = total + lax.ppermute(value, AXES, pairs)
    return total


def shards(slots, masks, image, measured, mask_ids):
    forward, backward = (jnp.asarray(table) for table in table_pair())
    _, count, width = image.shape
    devices = slots * masks
    radix = OUTER // slots
    each = radix // CHUNKS
    kept = [tuple(range(c * each, (c + 1) * each)) for c in range(CHUNKS)]
    by_slot = (slots, radix, 2 * INNER, 2 * INNER)
    out_table, in_table = backward.reshape(by_slot), forward.reshape(by_slot)
    ids = [mask_ids] + [
        lax.ppermute(mask_ids, "mask", [((m + d) % masks, m) for m in range(masks)])
        for d in range(1, masks)
    ]
    loss = jnp.zeros((1,), jnp.float32)
    leaving = []
    for c in range(CHUNKS):
        sent, *code = rows_out(kept[c], ids, image, out_table, c == CHUNKS - 1)
        sent, image = lax.optimization_barrier((sent, image))
        arrived = exchange(sent).reshape((-1,) + sent.shape[3:])
        left, part_loss = columns(c, masks, arrived, measured, forward, backward)
        leaving.append(left.reshape(sent.shape))
        loss = loss + jnp.sum(part_loss)
    first, second, third = stages(devices)
    loss = add_over(loss, devices, first, 1)
    returned = exchange(leaving[0])
    returned, loss = lax.optimization_barrier((returned, loss))
    loss = add_over(loss, devices, second, first)
    part = rows_part(kept[0], returned, in_table)
    last, part, loss = lax.optimization_barrier((exchange(leaving[1]), part, loss))
    loss = add_over(loss, devices, third, first * second)
    gradient = rows_in(kept[1], code[0], last, part, in_table)
    return gradient, loss[0] / (masks * width * width)


def solution(mesh):
    slots, masks = mesh.shape["rows"], mesh.shape["mask"]
    parted = jax.sharding.Mesh(mesh.devices.reshape(HALVES, slots // HALVES, masks), AXES)
    return jax.shard_map(
        functools.partial(shards, slots, masks),
        mesh=parted,
        in_specs=(P(None, AXES, None), P("mask", None, AXES[:2]), P("mask")),
        out_specs=(P(None, AXES, None), P()),
        check_vma=False,
    )
```

```python
import functools
import math

import jax
import jax.numpy as jnp
import ml_dtypes
import numpy as np
from jax import lax
from jax.experimental import pallas as pl
from jax.experimental.pallas import tpu as pltpu
from jax.sharding import PartitionSpec as P

INNER = 128
OUTER = 64
LENGTH = INNER * OUTER
EPSILON = 0.25
TILE = 16
VMEM_LIMIT = 58 * 1024 * 1024
ROOT_HALF = math.sqrt(0.5)

ROW_MULTIPLIER = 73856093
COLUMN_MULTIPLIER = 19349663
MASK_MULTIPLIER = 83492791
MIX_MULTIPLIER = 1274126177


def wrap(value):
    return (value + 2**31) % 2**32 - 2**31


def add(a, b):
    return (a[0] + b[0], a[1] + b[1])


def sub(a, b):
    return (a[0] - b[0], a[1] - b[1])


def quarter(a, sign):
    return (-a[1], a[0]) if sign > 0 else (a[1], -a[0])


def turn(a, step, count, sign):
    step = step % count
    if step == 0:
        return a
    if 4 * step == count:
        return quarter(a, sign)
    if 2 * step == count:
        return (-a[0], -a[1])
    if 4 * step == 3 * count:
        return quarter(a, -sign)
    if 8 * step == count:
        q = quarter(a, sign)
        return ((a[0] + q[0]) * ROOT_HALF, (a[1] + q[1]) * ROOT_HALF)
    if 8 * step == 3 * count:
        q = quarter(a, sign)
        return ((q[0] - a[0]) * ROOT_HALF, (q[1] - a[1]) * ROOT_HALF)
    angle = sign * 2.0 * math.pi * step / count
    cosine, sine = math.cos(angle), math.sin(angle)
    return (a[0] * cosine - a[1] * sine, a[0] * sine + a[1] * cosine)


def fourier4(x, sign):
    t0, t1 = add(x[0], x[2]), sub(x[0], x[2])
    t2, t3 = add(x[1], x[3]), quarter(sub(x[1], x[3]), sign)
    return [add(t0, t2), add(t1, t3), sub(t0, t2), sub(t1, t3)]


def fourier8(x, sign):
    even = fourier4(x[0::2], sign)
    odd = fourier4(x[1::2], sign)
    odd = [turn(odd[k], k, 8, sign) for k in range(4)]
    return [add(even[k], odd[k]) for k in range(4)] + [sub(even[k], odd[k]) for k in range(4)]


def fourier(x, sign):
    if len(x) == 1:
        return x
    if len(x) == 2:
        return [add(x[0], x[1]), sub(x[0], x[1])]
    return fourier4(x, sign) if len(x) == 4 else fourier8(x, sign)


def fourier64(load, store, middle, sign):
    for b in range(8):
        values = fourier8([load(8 * a + b) for a in range(8)], sign)
        for c in range(8):
            real, imag = turn(values[c], b * c, 64, sign)
            middle[c * 8 + b, 0] = real
            middle[c * 8 + b, 1] = imag
    for c in range(8):
        values = fourier8([(middle[c * 8 + b, 0], middle[c * 8 + b, 1]) for b in range(8)], sign)
        for d in range(8):
            store(c + 8 * d, values[d])


def fourier_part(load, store, middle, kept, radix):
    size = OUTER // radix
    first = size // 4
    for b in range(4):
        groups = [[] for _ in kept]
        for a in range(first):
            n = 4 * a + b
            values = fourier([load(n + size * t) for t in range(radix)], -1)
            for at, j in enumerate(kept):
                groups[at].append(turn(values[j], n * j, OUTER, -1))
        for at in range(len(kept)):
            values = fourier(groups[at], -1)
            for c in range(first):
                real, imag = turn(values[c], b * c, size, -1)
                middle[(at * first + c) * 4 + b, 0] = real
                middle[(at * first + c) * 4 + b, 1] = imag
    for at in range(len(kept)):
        for c in range(first):
            slot = (at * first + c) * 4
            values = fourier4([(middle[slot + b, 0], middle[slot + b, 1]) for b in range(4)], -1)
            for d in range(4):
                store(c + first * d, at, values[d])


def inverse_part(load, store, middle, kept, radix):
    size = OUTER // radix
    first = size // 4
    for at in range(len(kept)):
        for b in range(4):
            values = fourier([load(4 * a + b, at) for a in range(first)], 1)
            for c in range(first):
                real, imag = turn(values[c], b * c, size, 1)
                middle[(at * first + c) * 4 + b, 0] = real
                middle[(at * first + c) * 4 + b, 1] = imag
    for c in range(first):
        sums = []
        for at in range(len(kept)):
            slot = (at * first + c) * 4
            sums.append(
                fourier4([(middle[slot + b, 0], middle[slot + b, 1]) for b in range(4)], 1)
            )
        for d in range(4):
            n = c + first * d
            store(n, [turn(sums[at][d], n * j, OUTER, 1) for at, j in enumerate(kept)])


def fold(mixed):
    return mixed ^ lax.shift_right_logical(mixed, jnp.full(mixed.shape, 13, jnp.int32))


def phase_code(row_term, column_term):
    product = (row_term ^ column_term) * jnp.int32(wrap(4 * MIX_MULTIPLIER))
    code = lax.shift_right_arithmetic(product, jnp.full(product.shape, 30, jnp.int32))
    return code.astype(jnp.float32)


def rotate(value, code, direction):
    size = jnp.abs(code)
    cosine = 1 - size
    sine = code * (2 - size)
    left, right = value[0] * sine, value[1] * sine
    if direction > 0:
        return (value[0] * cosine - right, left + value[1] * cosine)
    return (value[0] * cosine + right, value[1] * cosine - left)


def row_hash(id_refs, base, mask):
    masks = len(id_refs)
    rows = lax.broadcasted_iota(jnp.int32, (TILE, INNER), 0) + base
    ahead = lax.rem(mask - lax.axis_index("mask") + masks, masks)
    mask_id = id_refs[0][0]
    for d in range(1, masks):
        mask_id = jnp.where(ahead == d, id_refs[d][0], mask_id)
    mask_term = (mask_id + 1) * jnp.int32(MASK_MULTIPLIER)
    return fold((rows * jnp.int32(ROW_MULTIPLIER)) ^ mask_term)


def column_hash(tile):
    lanes = lax.broadcasted_iota(jnp.int32, (TILE, INNER), 1)
    shift = jnp.int32(wrap(tile * INNER * COLUMN_MULTIPLIER))
    return fold(lanes * jnp.int32(COLUMN_MULTIPLIER) + shift)


def table_pair():
    inner = np.arange(INNER, dtype=np.int64)
    outer = np.arange(OUTER, dtype=np.int64)
    steps = inner[None, None, :] * (outer[:, None, None] + OUTER * inner[None, :, None]) % LENGTH
    angles = steps * (-2.0 * math.pi / LENGTH)
    cosine, sine = np.cos(angles), np.sin(angles)
    table = np.concatenate(
        [np.concatenate([cosine, -sine], axis=2), np.concatenate([sine, cosine], axis=2)], axis=1
    )
    forward = (table * 2.0**-7).astype(ml_dtypes.bfloat16)
    backward = (table.transpose(0, 2, 1) * 2.0**-6).astype(ml_dtypes.bfloat16)
    return forward, backward


def by_parity(step, last, early, both, late):
    @pl.when(step == 0)
    def _():
        early(0)

    for parity in range(2):

        @pl.when((step > 0) & (step < last) & (step % 2 == parity))
        def _():
            both(1 - parity, parity)

    @pl.when(step == last)
    def _():
        late((last - 1) % 2)


def rows_out_kernel(kept, masks, total, first, blocks, *refs):
    id_refs = refs[:masks]
    image_ref, table_hbm, out_ref, *rest = refs[masks:]
    code_ref = rest[0] if len(rest) == 7 else None
    table, middle, held_even, held_odd, column_terms, sem = rest[-6:]
    held = (held_even, held_odd)
    slots, _, _, rows, _ = out_ref.shape
    radix = OUTER // slots
    slabs = rows // TILE
    step = pl.program_id(0)
    device = lax.axis_index("rows") * masks + lax.axis_index("mask")
    copy = pltpu.make_async_copy(table_hbm.at[:, pl.ds(kept[0], len(kept))], table, sem)
    count = masks * slabs
    share = slots // count

    @pl.when(step == 0)
    def _():
        copy.start()
        for n in range(OUTER):
            column_terms[n] = column_hash(n)

    def spread(r, j, read):
        value = jnp.dot(held[read][r, j], table[r, j], preferred_element_type=jnp.float32)
        value = value.astype(jnp.bfloat16)
        for m in range(masks):
            for p in range(2):
                out_ref[r, m, p, :, j * INNER : (j + 1) * INNER] = value[
                    m * rows : (m + 1) * rows, p * INNER : (p + 1) * INNER
                ]

    def slab(index, carry, read, write):
        mask = index // slabs
        at = pl.multiple_of((index % slabs) * TILE, TILE)
        row_term = row_hash(id_refs, (device * total + first + step) * rows + at, mask)
        dots = [] if read is None else [(i, j) for i in range(share) for j in range(len(kept))]
        every = OUTER // max(len(dots), 1)
        calls = []

        def load(n):
            if dots and len(calls) % every == 0:
                i, j = dots[len(calls) // every]
                spread(index * share + i, j, read)
            calls.append(n)
            code = phase_code(row_term, column_terms[n])
            span = slice(n * INNER, (n + 1) * INNER)
            if code_ref is not None:
                code_ref[mask, pl.ds(at, TILE), span] = code.astype(jnp.bfloat16)
            value = [image_ref[p, pl.ds(at, TILE), span].astype(jnp.float32) for p in range(2)]
            return rotate(value, code, 1)

        def store(r, j, value):
            to = pl.ds(pl.multiple_of(index * TILE, TILE), TILE)
            held[write][r, j, to, 0:INNER] = value[0].astype(jnp.bfloat16)
            held[write][r, j, to, INNER:] = value[1].astype(jnp.bfloat16)

        fourier_part(load, store, middle, kept, radix)
        return carry

    def early(write):
        lax.fori_loop(0, count, functools.partial(slab, read=None, write=write), 0)
        copy.wait()

    def both(read, write):
        lax.fori_loop(0, count, functools.partial(slab, read=read, write=write), 0)

    def late(read):
        def some(index, carry):
            for i in range(share):
                for j in range(len(kept)):
                    spread(index * share + i, j, read)
            return carry

        lax.fori_loop(0, count, some, 0, unroll=2)

    by_parity(step, blocks, early, both, late)


def row_step(count, masks):
    return min(count, max(TILE, 128 // masks))


def row_scratch(slots, kept, masks, rows, buffers):
    held = pltpu.VMEM((slots, kept, masks * rows, 2 * INNER), jnp.bfloat16)
    return [
        pltpu.VMEM((slots, kept, 2 * INNER, 2 * INNER), jnp.bfloat16),
        pltpu.VMEM((slots * kept, 2, TILE, INNER), jnp.float32),
    ] + [held] * buffers


def parameters(flops):
    return {
        "compiler_params": pltpu.CompilerParams(
            vmem_limit_bytes=VMEM_LIMIT, dimension_semantics=("arbitrary",)
        ),
        "cost_estimate": pl.CostEstimate(
            flops=flops, bytes_accessed=40 << 20, transcendentals=0
        ),
    }


def rows_out(kept, ids, image, table, with_code, piece):
    masks = len(ids)
    _, total, width = image.shape
    slots = table.shape[0]
    rows = row_step(total, masks)
    first, count = piece[0] // rows, piece[1]
    blocks = count // rows
    span = len(kept) * INNER

    def now(i):
        return jnp.minimum(i, blocks - 1)

    def before(i):
        return jnp.maximum(i - 1, 0)

    return pl.pallas_call(
        functools.partial(rows_out_kernel, kept, masks, total // rows, first, blocks),
        grid=(blocks + 1,),
        in_specs=[pl.BlockSpec(memory_space=pltpu.SMEM)] * masks
        + [
            pl.BlockSpec((2, rows, width), lambda i: (0, first + now(i), 0)),
            pl.BlockSpec(memory_space=pl.ANY),
        ],
        out_specs=[
            pl.BlockSpec((slots, masks, 2, rows, span), lambda i: (0, 0, 0, before(i), 0)),
            pl.BlockSpec((masks, rows, width), lambda i: (0, now(i), 0)),
        ][: 1 + with_code],
        out_shape=[
            jax.ShapeDtypeStruct((slots, masks, 2, count, span), jnp.bfloat16),
            jax.ShapeDtypeStruct((masks, count, width), jnp.bfloat16),
        ][: 1 + with_code],
        scratch_shapes=row_scratch(slots, len(kept), masks, rows, 2)
        + [pltpu.VMEM((OUTER, TILE, INNER), jnp.int32), pltpu.SemaphoreType.DMA],
        name="rows_out",
        **parameters(masks * count * width * 1000),
    )(*ids, image, table)


def columns_kernel(share, ins, outs, *refs):
    in_refs = refs[: len(ins)]
    measured_ref, forward_hbm, backward_hbm = refs[len(ins) : len(ins) + 3]
    out_refs = refs[len(ins) + 3 : len(ins) + 3 + len(outs)]
    loss_ref, forward, backward, middle, held, sems = refs[len(ins) + 3 + len(outs) :]
    copies = [
        pltpu.make_async_copy(forward_hbm, forward, sems.at[0]),
        pltpu.make_async_copy(backward_hbm, backward, sems.at[1]),
    ]

    @pl.when(pl.program_id(0) == 0)
    def _():
        for copy in copies:
            copy.start()
        loss_ref[...] = jnp.zeros_like(loss_ref)

    def place(begins, n, group, size, inside):
        if share >= INNER:
            per = share // INNER
            row = (n % per) * INNER + group * size
            piece = max(i for i in range(len(begins)) if begins[i] <= row)
            at = row - begins[piece] + inside
            return piece, n // per, pl.ds(pl.multiple_of(at, TILE), TILE)
        at = group * size + inside
        span = pl.ds(pl.multiple_of(at % share, TILE), TILE)
        return 0, n * (INNER // share) + at // share, span

    def groups(begins, body):
        size = math.gcd(INNER, *begins)
        for group in range(INNER // size):
            lax.fori_loop(0, size // TILE, body(group, size), 0)

    def arrive(group, size, index, carry):
        inside = pl.multiple_of(index * TILE, TILE)

        def load(n):
            piece, source, span = place(ins, n, group, size, inside)
            return [in_refs[piece][source, p, span, :].astype(jnp.float32) for p in range(2)]

        def store(k, value):
            for p in range(2):
                to = pl.multiple_of(p * INNER + group * size + inside, TILE)
                held[k, pl.ds(to, TILE), :] = value[p].astype(jnp.bfloat16)

        fourier64(load, store, middle, -1)
        return carry

    groups(ins, lambda group, size: functools.partial(arrive, group, size))

    @pl.when(pl.program_id(0) == 0)
    def _():
        for copy in copies:
            copy.wait()

    def residual(k, carry):
        spectrum = jnp.dot(forward[k], held[k], preferred_element_type=jnp.float32)
        real, imag = spectrum[:INNER], spectrum[INNER:]
        measured = measured_ref[
            0, pl.ds(pl.multiple_of(k * INNER, INNER), INNER), :
        ].astype(jnp.float32)
        square = real * real + imag * imag + EPSILON
        inverse = lax.rsqrt(square)
        misfit = square * inverse - measured
        kept = 1.0 - measured * inverse
        loss_ref[...] += jnp.sum((misfit * misfit).reshape(INNER // 8, 8, INNER), axis=0)
        weighted = jnp.concatenate([real * kept, imag * kept], axis=0).astype(jnp.bfloat16)
        back = jnp.dot(backward[k], weighted, preferred_element_type=jnp.float32)
        held[k] = back.astype(jnp.bfloat16)
        return carry

    lax.fori_loop(0, OUTER, residual, 0, unroll=2)

    def leave(group, size, index, carry):
        inside = pl.multiple_of(index * TILE, TILE)

        def load(k):
            at = [pl.multiple_of(p * INNER + group * size + inside, TILE) for p in range(2)]
            return [held[k, pl.ds(at[p], TILE), :].astype(jnp.float32) for p in range(2)]

        def store(n, value):
            piece, source, span = place(outs, n, group, size, inside)
            for p in range(2):
                out_refs[piece][source, p, span, :] = value[p].astype(jnp.bfloat16)

        fourier64(load, store, middle, 1)
        return carry

    groups(outs, lambda group, size: functools.partial(leave, group, size))


def columns(chunk, arrived, pieces, measured, forward, backward):
    devices, _, _, width = arrived[0].shape
    share = sum(blocks.shape[2] for blocks in arrived)
    length = devices * share
    steps = width // INNER
    begins = [0]
    for blocks in arrived[:-1]:
        begins.append(begins[-1] + blocks.shape[2])

    def some_rows(count):
        return pl.BlockSpec((devices, 2, count, INNER), lambda i: (0, 0, 0, i))

    *leaving, loss = pl.pallas_call(
        functools.partial(columns_kernel, share, begins, [first for first, _ in pieces]),
        grid=(steps,),
        in_specs=[some_rows(blocks.shape[2]) for blocks in arrived]
        + [
            pl.BlockSpec((1, length, INNER), lambda i: (0, 0, chunk * steps + i)),
            pl.BlockSpec(memory_space=pl.ANY),
            pl.BlockSpec(memory_space=pl.ANY),
        ],
        out_specs=[some_rows(count) for _, count in pieces]
        + [pl.BlockSpec((8, INNER), lambda i: (0, 0))],
        out_shape=[
            jax.ShapeDtypeStruct((devices, 2, count, width), jnp.bfloat16) for _, count in pieces
        ]
        + [jax.ShapeDtypeStruct((8, INNER), jnp.float32)],
        scratch_shapes=[
            pltpu.VMEM((OUTER, 2 * INNER, 2 * INNER), jnp.bfloat16),
            pltpu.VMEM((OUTER, 2 * INNER, 2 * INNER), jnp.bfloat16),
            pltpu.VMEM((OUTER, 2, TILE, INNER), jnp.float32),
            pltpu.VMEM((OUTER, 2 * INNER, INNER), jnp.bfloat16),
            pltpu.SemaphoreType.DMA((2,)),
        ],
        name="columns",
        **parameters(length * width * 2200),
    )(*arrived, measured, forward, backward)
    return leaving, loss


def gather_one(r, j, in_ref, table, held):
    masks = in_ref.shape[1]
    span = slice(j * INNER, (j + 1) * INNER)
    value = jnp.concatenate(
        [
            jnp.concatenate([in_ref[r, m, p, :, span] for p in range(2)], axis=1)
            for m in range(masks)
        ],
        axis=0,
    )
    held[r, j] = jnp.dot(value, table[r, j], preferred_element_type=jnp.float32).astype(
        jnp.bfloat16
    )


def gather_all(kept, in_ref, table, held):
    def some(r, carry):
        for j in range(len(kept)):
            gather_one(r, j, in_ref, table, held)
        return carry

    lax.fori_loop(0, in_ref.shape[0], some, 0, unroll=4)


def fetch_table(kept, table_hbm, table, sem):
    copy = pltpu.make_async_copy(table_hbm.at[:, pl.ds(kept[0], len(kept))], table, sem)

    @pl.when(pl.program_id(0) == 0)
    def _():
        copy.start()
        copy.wait()


def held_tile(held, r, j, index):
    take = pl.ds(pl.multiple_of(index * TILE, TILE), TILE)
    return [
        held[r, j, take, p * INNER : (p + 1) * INNER].astype(jnp.float32) for p in range(2)
    ]


def rows_part_kernel(kept, in_ref, table_hbm, out_ref, table, middle, held, sem):
    slots, masks, _, rows, _ = in_ref.shape
    slabs = rows // TILE
    fetch_table(kept, table_hbm, table, sem)
    gather_all(kept, in_ref, table, held)

    def slab(index, carry):
        mask = index // slabs
        at = pl.multiple_of((index % slabs) * TILE, TILE)

        def load(r, j):
            return held_tile(held, r, j, index)

        def store(n, values):
            for j, value in enumerate(values):
                for p in range(2):
                    out_ref[n, j, mask, p, pl.ds(at, TILE), :] = value[p].astype(jnp.bfloat16)

        inverse_part(load, store, middle, kept, OUTER // slots)
        return carry

    lax.fori_loop(0, masks * slabs, slab, 0)


def rows_part(kept, arrived, table):
    slots, masks, _, count, span = arrived.shape
    rows = row_step(count, masks)
    return pl.pallas_call(
        functools.partial(rows_part_kernel, kept),
        grid=(count // rows,),
        in_specs=[
            pl.BlockSpec((slots, masks, 2, rows, span), lambda i: (0, 0, 0, i, 0)),
            pl.BlockSpec(memory_space=pl.ANY),
        ],
        out_specs=pl.BlockSpec(
            (slots, len(kept), masks, 2, rows, INNER), lambda i: (0, 0, 0, 0, i, 0)
        ),
        out_shape=jax.ShapeDtypeStruct(
            (slots, len(kept), masks, 2, count, INNER), jnp.bfloat16
        ),
        scratch_shapes=row_scratch(slots, len(kept), masks, rows, 1)
        + [pltpu.SemaphoreType.DMA],
        name="rows_part",
        **parameters(masks * count * LENGTH * 600),
    )(arrived, table)


def rows_in_kernel(kept, blocks, code_ref, in_ref, part_ref, table_hbm, *rest):
    out_ref, table, middle, held_even, held_odd, sem = rest[-6:]
    held = (held_even, held_odd)
    slots, masks, _, rows, _ = in_ref.shape
    radix = OUTER // slots
    slabs = rows // TILE
    count = masks * slabs
    share = slots // count
    fetch_table(kept, table_hbm, table, sem)

    def slab(index, carry, first, read, write):
        mask = index // slabs
        at = pl.multiple_of((index % slabs) * TILE, TILE)
        dots = [] if write is None else [(i, j) for i in range(share) for j in range(len(kept))]
        every = slots * len(kept) // max(len(dots), 1)
        calls = []

        def load(r, j):
            if dots and len(calls) % every == 0:
                i, k = dots[len(calls) // every]
                gather_one(index * share + i, k, in_ref, table, held[write])
            calls.append(r)
            return held_tile(held[read], r, j, index)

        def store(n, values):
            early = [
                [part_ref[n, j, mask, p, pl.ds(at, TILE), :].astype(jnp.float32) for p in range(2)]
                for j in range(radix - len(kept))
            ]
            for t, value in enumerate(fourier(early + values, 1)):
                tile = n + slots * t
                span = slice(tile * INNER, (tile + 1) * INNER)
                code = code_ref[mask, pl.ds(at, TILE), span].astype(jnp.float32)
                value = rotate(value, code, -1)
                for p in range(2):
                    if first:
                        out_ref[p, pl.ds(at, TILE), span] = value[p]
                    else:
                        out_ref[p, pl.ds(at, TILE), span] += value[p]

        inverse_part(load, store, middle, kept, radix)
        return carry

    def early(write):
        gather_all(kept, in_ref, table, held[write])

    def both(read, write):
        pair = {"read": read, "write": write}
        lax.fori_loop(0, slabs, functools.partial(slab, first=True, **pair), 0)
        lax.fori_loop(slabs, count, functools.partial(slab, first=False, **pair), 0)

    def late(read):
        both(read, None)

    by_parity(pl.program_id(0), blocks, early, both, late)


def rows_in(kept, code, arrived, part, table, piece, filled):
    slots, masks, _, count, span = arrived.shape
    total = code.shape[1]
    rows = row_step(total, masks)
    first, blocks = piece[0] // rows, count // rows

    def now(i):
        return jnp.minimum(i, blocks - 1)

    def before(i):
        return jnp.maximum(i - 1, 0)

    return pl.pallas_call(
        functools.partial(rows_in_kernel, kept, blocks),
        grid=(blocks + 1,),
        in_specs=[
            pl.BlockSpec((masks, rows, LENGTH), lambda i: (0, first + before(i), 0)),
            pl.BlockSpec((slots, masks, 2, rows, span), lambda i: (0, 0, 0, now(i), 0)),
            pl.BlockSpec(
                (slots,) + part.shape[1:4] + (rows, INNER),
                lambda i: (0, 0, 0, 0, first + before(i), 0),
            ),
            pl.BlockSpec(memory_space=pl.ANY),
        ]
        + [pl.BlockSpec(memory_space=pl.ANY)] * len(filled),
        out_specs=pl.BlockSpec((2, rows, LENGTH), lambda i: (0, first + before(i), 0)),
        out_shape=jax.ShapeDtypeStruct((2, total, LENGTH), jnp.float32),
        input_output_aliases={4: 0} if filled else {},
        scratch_shapes=row_scratch(slots, len(kept), masks, rows, 2)
        + [pltpu.SemaphoreType.DMA],
        name="rows_in",
        **parameters(masks * count * LENGTH * 1000),
    )(code, arrived, part, table, *filled)


AXES = ("rows", "mask")
CHUNKS = 2


def exchange(blocks):
    flat = blocks.reshape((-1,) + blocks.shape[-3:])
    flat = lax.all_to_all(flat, AXES, split_axis=0, concat_axis=0, tiled=True)
    return flat.reshape(blocks.shape)


def stages(devices):
    bits = devices.bit_length() - 1
    first = -(-bits // 3)
    second = -(-(bits - first) // 2)
    return [2**first, 2**second, 2 ** (bits - first - second)]


def add_over(value, devices, factor, stride):
    total = value
    for d in range(1, factor):
        pairs = []
        for i in range(devices):
            digit = i // stride % factor
            pairs.append((i, i + ((digit + d) % factor - digit) * stride))
        total = total + lax.ppermute(value, AXES, pairs)
    return total


def shards(slots, masks, image, measured, mask_ids):
    forward, backward = (jnp.asarray(table) for table in table_pair())
    _, count, width = image.shape
    devices = slots * masks
    radix = OUTER // slots
    each = radix // CHUNKS
    kept = [tuple(range(c * each, (c + 1) * each)) for c in range(CHUNKS)]
    by_slot = (slots, radix, 2 * INNER, 2 * INNER)
    out_table, in_table = backward.reshape(by_slot), forward.reshape(by_slot)
    ids = [mask_ids] + [
        lax.ppermute(mask_ids, "mask", [((m + d) % masks, m) for m in range(masks)])
        for d in range(1, masks)
    ]
    rows = row_step(count, masks)
    whole = [(0, count)]
    head, tail = whole, whole
    if count >= 2 * INNER:
        head, tail = [(0, rows), (rows, count - rows)], [(0, count - rows), (count - rows, rows)]
    code = ()

    def forth(c, pieces, image, with_code):
        arrived = []
        for piece in pieces:
            sent, *code = rows_out(kept[c], ids, image, out_table, with_code, piece)
            sent, image = lax.optimization_barrier((sent, image))
            if arrived:
                sent, arrived[-1] = lax.optimization_barrier((sent, arrived[-1]))
            arrived.append(exchange(sent.reshape((-1,) + sent.shape[2:])))
        return arrived, code, image

    def back(blocks):
        arrived = exchange(blocks)
        return arrived.reshape((slots, masks) + blocks.shape[1:])

    arrived, _, image = forth(0, head, image, False)
    (leaving,), loss_early = columns(0, arrived, whole, measured, forward, backward)
    arrived, (code,), image = forth(1, whole, image, True)
    leaving_last, loss_late = columns(1, arrived, tail, measured, forward, backward)
    first, second, third = stages(devices)
    loss = (jnp.sum(loss_early) + jnp.sum(loss_late)).reshape(1)
    loss = add_over(loss, devices, first, 1)
    returned, leaving_last, loss = lax.optimization_barrier((back(leaving), leaving_last, loss))
    part = rows_part(kept[0], returned, in_table)
    loss = add_over(loss, devices, second, first)
    filled = ()
    last = ()
    for piece, blocks in zip(tail, leaving_last):
        blocks, last = lax.optimization_barrier((blocks, last))
        last = back(blocks)
        if piece == tail[-1]:
            last, part, loss = lax.optimization_barrier((last, part, loss))
            loss = add_over(loss, devices, third, first * second)
        filled = (rows_in(kept[1], code, last, part, in_table, piece, filled),)
    return filled[0], loss[0] / (masks * width * width)


def solution(mesh):
    slots, masks = mesh.shape["rows"], mesh.shape["mask"]
    return jax.shard_map(
        functools.partial(shards, slots, masks),
        mesh=mesh,
        in_specs=(P(None, AXES, None), P("mask", None, "rows"), P("mask")),
        out_specs=(P(None, AXES, None), P()),
        check_vma=False,
    )
```

```python
import functools
import math

import jax
import jax.numpy as jnp
import ml_dtypes
import numpy as np
from jax import lax
from jax.experimental import pallas as pl
from jax.experimental.pallas import tpu as pltpu
from jax.sharding import PartitionSpec as P

INNER = 128
OUTER = 64
LENGTH = INNER * OUTER
EPSILON = 0.25
TILE = 16
VMEM_LIMIT = 58 * 1024 * 1024
ROOT_HALF = math.sqrt(0.5)

ROW_MULTIPLIER = 73856093
COLUMN_MULTIPLIER = 19349663
MASK_MULTIPLIER = 83492791
MIX_MULTIPLIER = 1274126177


def wrap(value):
    return (value + 2**31) % 2**32 - 2**31


def add(a, b):
    return (a[0] + b[0], a[1] + b[1])


def sub(a, b):
    return (a[0] - b[0], a[1] - b[1])


def quarter(a, sign):
    return (-a[1], a[0]) if sign > 0 else (a[1], -a[0])


def turn(a, step, count, sign):
    step = step % count
    if step == 0:
        return a
    if 4 * step == count:
        return quarter(a, sign)
    if 2 * step == count:
        return (-a[0], -a[1])
    if 4 * step == 3 * count:
        return quarter(a, -sign)
    if 8 * step == count:
        q = quarter(a, sign)
        return ((a[0] + q[0]) * ROOT_HALF, (a[1] + q[1]) * ROOT_HALF)
    if 8 * step == 3 * count:
        q = quarter(a, sign)
        return ((q[0] - a[0]) * ROOT_HALF, (q[1] - a[1]) * ROOT_HALF)
    angle = sign * 2.0 * math.pi * step / count
    cosine, sine = math.cos(angle), math.sin(angle)
    return (a[0] * cosine - a[1] * sine, a[0] * sine + a[1] * cosine)


def fourier4(x, sign):
    t0, t1 = add(x[0], x[2]), sub(x[0], x[2])
    t2, t3 = add(x[1], x[3]), quarter(sub(x[1], x[3]), sign)
    return [add(t0, t2), add(t1, t3), sub(t0, t2), sub(t1, t3)]


def fourier8(x, sign):
    even = fourier4(x[0::2], sign)
    odd = fourier4(x[1::2], sign)
    odd = [turn(odd[k], k, 8, sign) for k in range(4)]
    return [add(even[k], odd[k]) for k in range(4)] + [sub(even[k], odd[k]) for k in range(4)]


def fourier(x, sign):
    if len(x) == 1:
        return x
    if len(x) == 2:
        return [add(x[0], x[1]), sub(x[0], x[1])]
    return fourier4(x, sign) if len(x) == 4 else fourier8(x, sign)


def fourier64(load, store, middle, sign):
    for b in range(8):
        values = fourier8([load(8 * a + b) for a in range(8)], sign)
        for c in range(8):
            real, imag = turn(values[c], b * c, 64, sign)
            middle[c * 8 + b, 0] = real
            middle[c * 8 + b, 1] = imag
    for c in range(8):
        values = fourier8([(middle[c * 8 + b, 0], middle[c * 8 + b, 1]) for b in range(8)], sign)
        for d in range(8):
            store(c + 8 * d, values[d])


def fourier_part(load, store, middle, kept, radix):
    size = OUTER // radix
    first = size // 4
    for b in range(4):
        groups = [[] for _ in kept]
        for a in range(first):
            n = 4 * a + b
            values = fourier([load(n + size * t) for t in range(radix)], -1)
            for at, j in enumerate(kept):
                groups[at].append(turn(values[j], n * j, OUTER, -1))
        for at in range(len(kept)):
            values = fourier(groups[at], -1)
            for c in range(first):
                real, imag = turn(values[c], b * c, size, -1)
                middle[(at * first + c) * 4 + b, 0] = real
                middle[(at * first + c) * 4 + b, 1] = imag
    for at in range(len(kept)):
        for c in range(first):
            slot = (at * first + c) * 4
            values = fourier4([(middle[slot + b, 0], middle[slot + b, 1]) for b in range(4)], -1)
            for d in range(4):
                store(c + first * d, at, values[d])


def inverse_part(load, store, middle, kept, radix):
    size = OUTER // radix
    first = size // 4
    for at in range(len(kept)):
        for b in range(4):
            values = fourier([load(4 * a + b, at) for a in range(first)], 1)
            for c in range(first):
                real, imag = turn(values[c], b * c, size, 1)
                middle[(at * first + c) * 4 + b, 0] = real
                middle[(at * first + c) * 4 + b, 1] = imag
    for c in range(first):
        sums = []
        for at in range(len(kept)):
            slot = (at * first + c) * 4
            sums.append(
                fourier4([(middle[slot + b, 0], middle[slot + b, 1]) for b in range(4)], 1)
            )
        for d in range(4):
            n = c + first * d
            store(n, [turn(sums[at][d], n * j, OUTER, 1) for at, j in enumerate(kept)])


def fold(mixed):
    return mixed ^ lax.shift_right_logical(mixed, jnp.full(mixed.shape, 13, jnp.int32))


def phase_code(row_term, column_term):
    product = (row_term ^ column_term) * jnp.int32(wrap(4 * MIX_MULTIPLIER))
    code = lax.shift_right_arithmetic(product, jnp.full(product.shape, 30, jnp.int32))
    return code.astype(jnp.float32)


def rotate(value, code, direction):
    size = jnp.abs(code)
    cosine = 1 - size
    sine = code * (2 - size)
    left, right = value[0] * sine, value[1] * sine
    if direction > 0:
        return (value[0] * cosine - right, left + value[1] * cosine)
    return (value[0] * cosine + right, value[1] * cosine - left)


def row_hash(id_refs, base, mask):
    masks = len(id_refs)
    rows = lax.broadcasted_iota(jnp.int32, (TILE, INNER), 0) + base
    ahead = lax.rem(mask - lax.axis_index("mask") + masks, masks)
    mask_id = id_refs[0][0]
    for d in range(1, masks):
        mask_id = jnp.where(ahead == d, id_refs[d][0], mask_id)
    mask_term = (mask_id + 1) * jnp.int32(MASK_MULTIPLIER)
    return fold((rows * jnp.int32(ROW_MULTIPLIER)) ^ mask_term)


def column_hash(tile):
    lanes = lax.broadcasted_iota(jnp.int32, (TILE, INNER), 1)
    shift = jnp.int32(wrap(tile * INNER * COLUMN_MULTIPLIER))
    return fold(lanes * jnp.int32(COLUMN_MULTIPLIER) + shift)


def table_pair():
    inner = np.arange(INNER, dtype=np.int64)
    outer = np.arange(OUTER, dtype=np.int64)
    steps = inner[None, None, :] * (outer[:, None, None] + OUTER * inner[None, :, None]) % LENGTH
    angles = steps * (-2.0 * math.pi / LENGTH)
    cosine, sine = np.cos(angles), np.sin(angles)
    table = np.concatenate(
        [np.concatenate([cosine, -sine], axis=2), np.concatenate([sine, cosine], axis=2)], axis=1
    )
    forward = (table * 2.0**-7).astype(ml_dtypes.bfloat16)
    backward = (table.transpose(0, 2, 1) * 2.0**-6).astype(ml_dtypes.bfloat16)
    return forward, backward


def by_parity(step, last, early, both, late):
    @pl.when(step == 0)
    def _():
        early(0)

    for parity in range(2):

        @pl.when((step > 0) & (step < last) & (step % 2 == parity))
        def _():
            both(1 - parity, parity)

    @pl.when(step == last)
    def _():
        late((last - 1) % 2)


def rows_out_kernel(kept, masks, total, first, blocks, *refs):
    id_refs = refs[:masks]
    image_ref, table_hbm, out_ref, *rest = refs[masks:]
    code_ref = rest[0] if len(rest) == 7 else None
    table, middle, held_even, held_odd, column_terms, sem = rest[-6:]
    held = (held_even, held_odd)
    slots, _, _, rows, _ = out_ref.shape
    radix = OUTER // slots
    slabs = rows // TILE
    step = pl.program_id(0)
    device = lax.axis_index("rows") * masks + lax.axis_index("mask")
    copy = pltpu.make_async_copy(table_hbm.at[:, pl.ds(kept[0], len(kept))], table, sem)
    count = masks * slabs
    share = slots // count

    @pl.when(step == 0)
    def _():
        copy.start()
        for n in range(OUTER):
            column_terms[n] = column_hash(n)

    def spread(r, j, read):
        value = jnp.dot(held[read][r, j], table[r, j], preferred_element_type=jnp.float32)
        value = value.astype(jnp.bfloat16)
        for m in range(masks):
            for p in range(2):
                out_ref[r, m, p, :, j * INNER : (j + 1) * INNER] = value[
                    m * rows : (m + 1) * rows, p * INNER : (p + 1) * INNER
                ]

    def slab(index, carry, read, write):
        mask = index // slabs
        at = pl.multiple_of((index % slabs) * TILE, TILE)
        row_term = row_hash(id_refs, (device * total + first + step) * rows + at, mask)
        dots = [] if read is None else [(i, j) for i in range(share) for j in range(len(kept))]
        every = OUTER // max(len(dots), 1)
        calls = []

        def load(n):
            if dots and len(calls) % every == 0:
                i, j = dots[len(calls) // every]
                spread(index * share + i, j, read)
            calls.append(n)
            code = phase_code(row_term, column_terms[n])
            span = slice(n * INNER, (n + 1) * INNER)
            if code_ref is not None:
                code_ref[mask, pl.ds(at, TILE), span] = code.astype(jnp.bfloat16)
            value = [image_ref[p, pl.ds(at, TILE), span].astype(jnp.float32) for p in range(2)]
            return rotate(value, code, 1)

        def store(r, j, value):
            to = pl.ds(pl.multiple_of(index * TILE, TILE), TILE)
            held[write][r, j, to, 0:INNER] = value[0].astype(jnp.bfloat16)
            held[write][r, j, to, INNER:] = value[1].astype(jnp.bfloat16)

        fourier_part(load, store, middle, kept, radix)
        return carry

    def early(write):
        lax.fori_loop(0, count, functools.partial(slab, read=None, write=write), 0)
        copy.wait()

    def both(read, write):
        lax.fori_loop(0, count, functools.partial(slab, read=read, write=write), 0)

    def late(read):
        def some(index, carry):
            for i in range(share):
                for j in range(len(kept)):
                    spread(index * share + i, j, read)
            return carry

        lax.fori_loop(0, count, some, 0, unroll=2)

    by_parity(step, blocks, early, both, late)


def row_step(count, masks):
    return min(count, max(TILE, 128 // masks))


def row_scratch(slots, kept, masks, rows, buffers):
    held = pltpu.VMEM((slots, kept, masks * rows, 2 * INNER), jnp.bfloat16)
    return [
        pltpu.VMEM((slots, kept, 2 * INNER, 2 * INNER), jnp.bfloat16),
        pltpu.VMEM((slots * kept, 2, TILE, INNER), jnp.float32),
    ] + [held] * buffers


def parameters(flops):
    return {
        "compiler_params": pltpu.CompilerParams(
            vmem_limit_bytes=VMEM_LIMIT, dimension_semantics=("arbitrary",)
        ),
        "cost_estimate": pl.CostEstimate(
            flops=flops, bytes_accessed=40 << 20, transcendentals=0
        ),
    }


def rows_out(kept, ids, image, table, with_code, piece):
    masks = len(ids)
    _, total, width = image.shape
    slots = table.shape[0]
    rows = math.gcd(row_step(total, masks), *piece)
    first, count = piece[0] // rows, piece[1]
    blocks = count // rows
    span = len(kept) * INNER

    def now(i):
        return jnp.minimum(i, blocks - 1)

    def before(i):
        return jnp.maximum(i - 1, 0)

    return pl.pallas_call(
        functools.partial(rows_out_kernel, kept, masks, total // rows, first, blocks),
        grid=(blocks + 1,),
        in_specs=[pl.BlockSpec(memory_space=pltpu.SMEM)] * masks
        + [
            pl.BlockSpec((2, rows, width), lambda i: (0, first + now(i), 0)),
            pl.BlockSpec(memory_space=pl.ANY),
        ],
        out_specs=[
            pl.BlockSpec((slots, masks, 2, rows, span), lambda i: (0, 0, 0, before(i), 0)),
            pl.BlockSpec((masks, rows, width), lambda i: (0, now(i), 0)),
        ][: 1 + with_code],
        out_shape=[
            jax.ShapeDtypeStruct((slots, masks, 2, count, span), jnp.bfloat16),
            jax.ShapeDtypeStruct((masks, count, width), jnp.bfloat16),
        ][: 1 + with_code],
        scratch_shapes=row_scratch(slots, len(kept), masks, rows, 2)
        + [pltpu.VMEM((OUTER, TILE, INNER), jnp.int32), pltpu.SemaphoreType.DMA],
        name="rows_out",
        **parameters(masks * count * width * 1000),
    )(*ids, image, table)


def columns_kernel(share, ins, outs, *refs):
    in_refs = refs[: len(ins)]
    measured_ref, forward_hbm, backward_hbm = refs[len(ins) : len(ins) + 3]
    out_refs = refs[len(ins) + 3 : len(ins) + 3 + len(outs)]
    loss_ref, forward, backward, middle, held, sems = refs[len(ins) + 3 + len(outs) :]
    copies = [
        pltpu.make_async_copy(forward_hbm, forward, sems.at[0]),
        pltpu.make_async_copy(backward_hbm, backward, sems.at[1]),
    ]

    @pl.when(pl.program_id(0) == 0)
    def _():
        for copy in copies:
            copy.start()
        loss_ref[...] = jnp.zeros_like(loss_ref)

    def place(begins, n, group, size, inside):
        if share >= INNER:
            per = share // INNER
            row = (n % per) * INNER + group * size
            piece = max(i for i in range(len(begins)) if begins[i] <= row)
            at = row - begins[piece] + inside
            return piece, n // per, pl.ds(pl.multiple_of(at, TILE), TILE)
        at = group * size + inside
        span = pl.ds(pl.multiple_of(at % share, TILE), TILE)
        return 0, n * (INNER // share) + at // share, span

    def groups(begins, body):
        size = math.gcd(INNER, *begins)
        for group in range(INNER // size):
            lax.fori_loop(0, size // TILE, body(group, size), 0)

    def arrive(group, size, index, carry):
        inside = pl.multiple_of(index * TILE, TILE)

        def load(n):
            piece, source, span = place(ins, n, group, size, inside)
            return [in_refs[piece][source, p, span, :].astype(jnp.float32) for p in range(2)]

        def store(k, value):
            for p in range(2):
                to = pl.multiple_of(p * INNER + group * size + inside, TILE)
                held[k, pl.ds(to, TILE), :] = value[p].astype(jnp.bfloat16)

        fourier64(load, store, middle, -1)
        return carry

    groups(ins, lambda group, size: functools.partial(arrive, group, size))

    @pl.when(pl.program_id(0) == 0)
    def _():
        for copy in copies:
            copy.wait()

    def residual(k, carry):
        spectrum = jnp.dot(forward[k], held[k], preferred_element_type=jnp.float32)
        real, imag = spectrum[:INNER], spectrum[INNER:]
        measured = measured_ref[
            0, pl.ds(pl.multiple_of(k * INNER, INNER), INNER), :
        ].astype(jnp.float32)
        square = real * real + imag * imag + EPSILON
        inverse = lax.rsqrt(square)
        misfit = square * inverse - measured
        kept = 1.0 - measured * inverse
        loss_ref[...] += jnp.sum((misfit * misfit).reshape(INNER // 8, 8, INNER), axis=0)
        weighted = jnp.concatenate([real * kept, imag * kept], axis=0).astype(jnp.bfloat16)
        back = jnp.dot(backward[k], weighted, preferred_element_type=jnp.float32)
        held[k] = back.astype(jnp.bfloat16)
        return carry

    lax.fori_loop(0, OUTER, residual, 0, unroll=2)

    def leave(group, size, index, carry):
        inside = pl.multiple_of(index * TILE, TILE)

        def load(k):
            at = [pl.multiple_of(p * INNER + group * size + inside, TILE) for p in range(2)]
            return [held[k, pl.ds(at[p], TILE), :].astype(jnp.float32) for p in range(2)]

        def store(n, value):
            piece, source, span = place(outs, n, group, size, inside)
            for p in range(2):
                out_refs[piece][source, p, span, :] = value[p].astype(jnp.bfloat16)

        fourier64(load, store, middle, 1)
        return carry

    groups(outs, lambda group, size: functools.partial(leave, group, size))


def columns(chunk, arrived, pieces, measured, forward, backward):
    devices, _, _, width = arrived[0].shape
    share = sum(blocks.shape[2] for blocks in arrived)
    length = devices * share
    steps = width // INNER
    begins = [0]
    for blocks in arrived[:-1]:
        begins.append(begins[-1] + blocks.shape[2])

    def some_rows(count):
        return pl.BlockSpec((devices, 2, count, INNER), lambda i: (0, 0, 0, i))

    *leaving, loss = pl.pallas_call(
        functools.partial(columns_kernel, share, begins, [first for first, _ in pieces]),
        grid=(steps,),
        in_specs=[some_rows(blocks.shape[2]) for blocks in arrived]
        + [
            pl.BlockSpec((1, length, INNER), lambda i: (0, 0, chunk * steps + i)),
            pl.BlockSpec(memory_space=pl.ANY),
            pl.BlockSpec(memory_space=pl.ANY),
        ],
        out_specs=[some_rows(count) for _, count in pieces]
        + [pl.BlockSpec((8, INNER), lambda i: (0, 0))],
        out_shape=[
            jax.ShapeDtypeStruct((devices, 2, count, width), jnp.bfloat16) for _, count in pieces
        ]
        + [jax.ShapeDtypeStruct((8, INNER), jnp.float32)],
        scratch_shapes=[
            pltpu.VMEM((OUTER, 2 * INNER, 2 * INNER), jnp.bfloat16),
            pltpu.VMEM((OUTER, 2 * INNER, 2 * INNER), jnp.bfloat16),
            pltpu.VMEM((OUTER, 2, TILE, INNER), jnp.float32),
            pltpu.VMEM((OUTER, 2 * INNER, INNER), jnp.bfloat16),
            pltpu.SemaphoreType.DMA((2,)),
        ],
        name="columns",
        **parameters(length * width * 2200),
    )(*arrived, measured, forward, backward)
    return leaving, loss


def gather_one(r, j, in_ref, table, held):
    masks = in_ref.shape[1]
    span = slice(j * INNER, (j + 1) * INNER)
    value = jnp.concatenate(
        [
            jnp.concatenate([in_ref[r, m, p, :, span] for p in range(2)], axis=1)
            for m in range(masks)
        ],
        axis=0,
    )
    held[r, j] = jnp.dot(value, table[r, j], preferred_element_type=jnp.float32).astype(
        jnp.bfloat16
    )


def gather_all(kept, in_ref, table, held):
    def some(r, carry):
        for j in range(len(kept)):
            gather_one(r, j, in_ref, table, held)
        return carry

    lax.fori_loop(0, in_ref.shape[0], some, 0, unroll=4)


def fetch_table(kept, table_hbm, table, sem):
    copy = pltpu.make_async_copy(table_hbm.at[:, pl.ds(kept[0], len(kept))], table, sem)

    @pl.when(pl.program_id(0) == 0)
    def _():
        copy.start()
        copy.wait()


def held_tile(held, r, j, index):
    take = pl.ds(pl.multiple_of(index * TILE, TILE), TILE)
    return [
        held[r, j, take, p * INNER : (p + 1) * INNER].astype(jnp.float32) for p in range(2)
    ]


def rows_part_kernel(kept, in_ref, table_hbm, out_ref, table, middle, held, sem):
    slots, masks, _, rows, _ = in_ref.shape
    slabs = rows // TILE
    fetch_table(kept, table_hbm, table, sem)
    gather_all(kept, in_ref, table, held)

    def slab(index, carry):
        mask = index // slabs
        at = pl.multiple_of((index % slabs) * TILE, TILE)

        def load(r, j):
            return held_tile(held, r, j, index)

        def store(n, values):
            for j, value in enumerate(values):
                for p in range(2):
                    out_ref[n, j, mask, p, pl.ds(at, TILE), :] = value[p].astype(jnp.bfloat16)

        inverse_part(load, store, middle, kept, OUTER // slots)
        return carry

    lax.fori_loop(0, masks * slabs, slab, 0)


def rows_part(kept, arrived, table):
    slots, masks, _, count, span = arrived.shape
    rows = row_step(count, masks)
    return pl.pallas_call(
        functools.partial(rows_part_kernel, kept),
        grid=(count // rows,),
        in_specs=[
            pl.BlockSpec((slots, masks, 2, rows, span), lambda i: (0, 0, 0, i, 0)),
            pl.BlockSpec(memory_space=pl.ANY),
        ],
        out_specs=pl.BlockSpec(
            (slots, len(kept), masks, 2, rows, INNER), lambda i: (0, 0, 0, 0, i, 0)
        ),
        out_shape=jax.ShapeDtypeStruct(
            (slots, len(kept), masks, 2, count, INNER), jnp.bfloat16
        ),
        scratch_shapes=row_scratch(slots, len(kept), masks, rows, 1)
        + [pltpu.SemaphoreType.DMA],
        name="rows_part",
        **parameters(masks * count * LENGTH * 600),
    )(arrived, table)


def rows_in_kernel(kept, blocks, code_ref, in_ref, part_ref, table_hbm, *rest):
    out_ref, table, middle, held_even, held_odd, sem = rest[-6:]
    held = (held_even, held_odd)
    slots, masks, _, rows, _ = in_ref.shape
    radix = OUTER // slots
    slabs = rows // TILE
    count = masks * slabs
    share = slots // count
    fetch_table(kept, table_hbm, table, sem)

    def slab(index, carry, first, read, write):
        mask = index // slabs
        at = pl.multiple_of((index % slabs) * TILE, TILE)
        dots = [] if write is None else [(i, j) for i in range(share) for j in range(len(kept))]
        every = slots * len(kept) // max(len(dots), 1)
        calls = []

        def load(r, j):
            if dots and len(calls) % every == 0:
                i, k = dots[len(calls) // every]
                gather_one(index * share + i, k, in_ref, table, held[write])
            calls.append(r)
            return held_tile(held[read], r, j, index)

        def store(n, values):
            early = [
                [part_ref[n, j, mask, p, pl.ds(at, TILE), :].astype(jnp.float32) for p in range(2)]
                for j in range(radix - len(kept))
            ]
            for t, value in enumerate(fourier(early + values, 1)):
                tile = n + slots * t
                span = slice(tile * INNER, (tile + 1) * INNER)
                code = code_ref[mask, pl.ds(at, TILE), span].astype(jnp.float32)
                value = rotate(value, code, -1)
                for p in range(2):
                    if first:
                        out_ref[p, pl.ds(at, TILE), span] = value[p]
                    else:
                        out_ref[p, pl.ds(at, TILE), span] += value[p]

        inverse_part(load, store, middle, kept, radix)
        return carry

    def early(write):
        gather_all(kept, in_ref, table, held[write])

    def both(read, write):
        pair = {"read": read, "write": write}
        lax.fori_loop(0, slabs, functools.partial(slab, first=True, **pair), 0)
        lax.fori_loop(slabs, count, functools.partial(slab, first=False, **pair), 0)

    def late(read):
        both(read, None)

    by_parity(pl.program_id(0), blocks, early, both, late)


def rows_in(kept, code, arrived, part, table, piece, filled):
    slots, masks, _, count, span = arrived.shape
    total = code.shape[1]
    rows = math.gcd(row_step(total, masks), *piece)
    first, blocks = piece[0] // rows, count // rows

    def now(i):
        return jnp.minimum(i, blocks - 1)

    def before(i):
        return jnp.maximum(i - 1, 0)

    return pl.pallas_call(
        functools.partial(rows_in_kernel, kept, blocks),
        grid=(blocks + 1,),
        in_specs=[
            pl.BlockSpec((masks, rows, LENGTH), lambda i: (0, first + before(i), 0)),
            pl.BlockSpec((slots, masks, 2, rows, span), lambda i: (0, 0, 0, now(i), 0)),
            pl.BlockSpec(
                (slots,) + part.shape[1:4] + (rows, INNER),
                lambda i: (0, 0, 0, 0, first + before(i), 0),
            ),
            pl.BlockSpec(memory_space=pl.ANY),
        ]
        + [pl.BlockSpec(memory_space=pl.ANY)] * len(filled),
        out_specs=pl.BlockSpec((2, rows, LENGTH), lambda i: (0, first + before(i), 0)),
        out_shape=jax.ShapeDtypeStruct((2, total, LENGTH), jnp.float32),
        input_output_aliases={4: 0} if filled else {},
        scratch_shapes=row_scratch(slots, len(kept), masks, rows, 2)
        + [pltpu.SemaphoreType.DMA],
        name="rows_in",
        **parameters(masks * count * LENGTH * 1000),
    )(code, arrived, part, table, *filled)


AXES = ("rows", "mask")
CHUNKS = 2


def exchange(blocks):
    flat = blocks.reshape((-1,) + blocks.shape[-3:])
    flat = lax.all_to_all(flat, AXES, split_axis=0, concat_axis=0, tiled=True)
    return flat.reshape(blocks.shape)


def add_over(value, devices, factor, stride):
    total = value
    for d in range(1, factor):
        pairs = []
        for i in range(devices):
            digit = i // stride % factor
            pairs.append((i, i + ((digit + d) % factor - digit) * stride))
        total = total + lax.ppermute(value, AXES, pairs)
    return total


def shards(slots, masks, image, measured, mask_ids):
    forward, backward = (jnp.asarray(table) for table in table_pair())
    _, count, width = image.shape
    devices = slots * masks
    radix = OUTER // slots
    each = radix // CHUNKS
    kept = [tuple(range(c * each, (c + 1) * each)) for c in range(CHUNKS)]
    by_slot = (slots, radix, 2 * INNER, 2 * INNER)
    out_table, in_table = backward.reshape(by_slot), forward.reshape(by_slot)
    ids = [mask_ids] + [
        lax.ppermute(mask_ids, "mask", [((m + d) % masks, m) for m in range(masks)])
        for d in range(1, masks)
    ]
    whole = [(0, count)]
    head, tail = whole, whole
    if count >= 2 * INNER:
        small = 2 * TILE
        head = [(0, small), (small, count - small)]
        tail = [(0, count - small), (count - small, small)]

    def forth(c, pieces, image, with_code):
        arrived = []
        for piece in pieces:
            sent, *code = rows_out(kept[c], ids, image, out_table, with_code, piece)
            sent, image = lax.optimization_barrier((sent, image))
            if arrived:
                sent, arrived[-1] = lax.optimization_barrier((sent, arrived[-1]))
            arrived.append(exchange(sent.reshape((-1,) + sent.shape[2:])))
        return arrived, code, image

    def back(blocks):
        arrived = exchange(blocks)
        return arrived.reshape((slots, masks) + blocks.shape[1:])

    arrived, _, image = forth(0, head, image, False)
    (leaving,), loss_early = columns(0, arrived, whole, measured, forward, backward)
    arrived, (code,), image = forth(1, whole, image, True)
    leaving_last, loss_late = columns(1, arrived, tail, measured, forward, backward)
    first = 1 << (3 * devices.bit_length() // 5)
    loss = (jnp.sum(loss_early) + jnp.sum(loss_late)).reshape(1)
    loss = add_over(loss, devices, first, 1)
    returned, leaving_last, loss = lax.optimization_barrier((back(leaving), leaving_last, loss))
    part = rows_part(kept[0], returned, in_table)
    loss = add_over(loss, devices, devices // first, first)
    last = ()
    filled = ()
    for piece, blocks in zip(tail, leaving_last):
        if piece != tail[0]:
            blocks, last, part, loss = lax.optimization_barrier((blocks, last, part, loss))
        last = back(blocks)
        filled = (rows_in(kept[1], code, last, part, in_table, piece, filled),)
    return filled[0], loss[0] / (masks * width * width)


def solution(mesh):
    slots, masks = mesh.shape["rows"], mesh.shape["mask"]
    return jax.shard_map(
        functools.partial(shards, slots, masks),
        mesh=mesh,
        in_specs=(P(None, AXES, None), P("mask", None, "rows"), P("mask")),
        out_specs=(P(None, AXES, None), P()),
        check_vma=False,
    )
```

```python
import functools
import math

import jax
import jax.numpy as jnp
import ml_dtypes
import numpy as np
from jax import lax
from jax.experimental import pallas as pl
from jax.experimental.pallas import tpu as pltpu
from jax.sharding import PartitionSpec as P

INNER = 128
OUTER = 64
LENGTH = INNER * OUTER
EPSILON = 0.25
TILE = 16
VMEM_LIMIT = 58 * 1024 * 1024
ROOT_HALF = math.sqrt(0.5)

ROW_MULTIPLIER = 73856093
COLUMN_MULTIPLIER = 19349663
MASK_MULTIPLIER = 83492791
MIX_MULTIPLIER = 1274126177


def wrap(value):
    return (value + 2**31) % 2**32 - 2**31


def add(a, b):
    return (a[0] + b[0], a[1] + b[1])


def sub(a, b):
    return (a[0] - b[0], a[1] - b[1])


def quarter(a, sign):
    return (-a[1], a[0]) if sign > 0 else (a[1], -a[0])


def turn(a, step, count, sign):
    step = step % count
    if step == 0:
        return a
    if 4 * step == count:
        return quarter(a, sign)
    if 2 * step == count:
        return (-a[0], -a[1])
    if 4 * step == 3 * count:
        return quarter(a, -sign)
    if 8 * step == count:
        q = quarter(a, sign)
        return ((a[0] + q[0]) * ROOT_HALF, (a[1] + q[1]) * ROOT_HALF)
    if 8 * step == 3 * count:
        q = quarter(a, sign)
        return ((q[0] - a[0]) * ROOT_HALF, (q[1] - a[1]) * ROOT_HALF)
    angle = sign * 2.0 * math.pi * step / count
    cosine, sine = math.cos(angle), math.sin(angle)
    return (a[0] * cosine - a[1] * sine, a[0] * sine + a[1] * cosine)


def fourier4(x, sign):
    t0, t1 = add(x[0], x[2]), sub(x[0], x[2])
    t2, t3 = add(x[1], x[3]), quarter(sub(x[1], x[3]), sign)
    return [add(t0, t2), add(t1, t3), sub(t0, t2), sub(t1, t3)]


def fourier8(x, sign):
    even = fourier4(x[0::2], sign)
    odd = fourier4(x[1::2], sign)
    odd = [turn(odd[k], k, 8, sign) for k in range(4)]
    return [add(even[k], odd[k]) for k in range(4)] + [sub(even[k], odd[k]) for k in range(4)]


def fourier(x, sign):
    if len(x) == 1:
        return x
    if len(x) == 2:
        return [add(x[0], x[1]), sub(x[0], x[1])]
    return fourier4(x, sign) if len(x) == 4 else fourier8(x, sign)


def fourier64(load, store, middle, sign):
    for b in range(8):
        values = fourier8([load(8 * a + b) for a in range(8)], sign)
        for c in range(8):
            real, imag = turn(values[c], b * c, 64, sign)
            middle[c * 8 + b, 0] = real
            middle[c * 8 + b, 1] = imag
    for c in range(8):
        values = fourier8([(middle[c * 8 + b, 0], middle[c * 8 + b, 1]) for b in range(8)], sign)
        for d in range(8):
            store(c + 8 * d, values[d])


def fourier_part(load, store, middle, kept, radix):
    size = OUTER // radix
    first = size // 4
    for b in range(4):
        groups = [[] for _ in kept]
        for a in range(first):
            n = 4 * a + b
            values = fourier([load(n + size * t) for t in range(radix)], -1)
            for at, j in enumerate(kept):
                groups[at].append(turn(values[j], n * j, OUTER, -1))
        for at in range(len(kept)):
            values = fourier(groups[at], -1)
            for c in range(first):
                real, imag = turn(values[c], b * c, size, -1)
                middle[(at * first + c) * 4 + b, 0] = real
                middle[(at * first + c) * 4 + b, 1] = imag
    for at in range(len(kept)):
        for c in range(first):
            slot = (at * first + c) * 4
            values = fourier4([(middle[slot + b, 0], middle[slot + b, 1]) for b in range(4)], -1)
            for d in range(4):
                store(c + first * d, at, values[d])


def inverse_part(load, store, middle, kept, radix):
    size = OUTER // radix
    first = size // 4
    for at in range(len(kept)):
        for b in range(4):
            values = fourier([load(4 * a + b, at) for a in range(first)], 1)
            for c in range(first):
                real, imag = turn(values[c], b * c, size, 1)
                middle[(at * first + c) * 4 + b, 0] = real
                middle[(at * first + c) * 4 + b, 1] = imag
    for c in range(first):
        sums = []
        for at in range(len(kept)):
            slot = (at * first + c) * 4
            sums.append(
                fourier4([(middle[slot + b, 0], middle[slot + b, 1]) for b in range(4)], 1)
            )
        for d in range(4):
            n = c + first * d
            store(n, [turn(sums[at][d], n * j, OUTER, 1) for at, j in enumerate(kept)])


def fold(mixed):
    return mixed ^ lax.shift_right_logical(mixed, jnp.full(mixed.shape, 13, jnp.int32))


def phase_code(row_term, column_term):
    product = (row_term ^ column_term) * jnp.int32(wrap(4 * MIX_MULTIPLIER))
    code = lax.shift_right_arithmetic(product, jnp.full(product.shape, 30, jnp.int32))
    return code.astype(jnp.float32)


def rotate(value, code, direction):
    size = jnp.abs(code)
    cosine = 1 - size
    sine = code * (2 - size)
    left, right = value[0] * sine, value[1] * sine
    if direction > 0:
        return (value[0] * cosine - right, left + value[1] * cosine)
    return (value[0] * cosine + right, value[1] * cosine - left)


def row_hash(id_refs, base, mask):
    masks = len(id_refs)
    rows = lax.broadcasted_iota(jnp.int32, (TILE, INNER), 0) + base
    ahead = lax.rem(mask - lax.axis_index("mask") + masks, masks)
    mask_id = id_refs[0][0]
    for d in range(1, masks):
        mask_id = jnp.where(ahead == d, id_refs[d][0], mask_id)
    mask_term = (mask_id + 1) * jnp.int32(MASK_MULTIPLIER)
    return fold((rows * jnp.int32(ROW_MULTIPLIER)) ^ mask_term)


def column_hash(tile):
    lanes = lax.broadcasted_iota(jnp.int32, (TILE, INNER), 1)
    shift = jnp.int32(wrap(tile * INNER * COLUMN_MULTIPLIER))
    return fold(lanes * jnp.int32(COLUMN_MULTIPLIER) + shift)


def table_pair():
    inner = np.arange(INNER, dtype=np.int64)
    outer = np.arange(OUTER, dtype=np.int64)
    steps = inner[None, None, :] * (outer[:, None, None] + OUTER * inner[None, :, None]) % LENGTH
    angles = steps * (-2.0 * math.pi / LENGTH)
    cosine, sine = np.cos(angles), np.sin(angles)
    table = np.concatenate(
        [np.concatenate([cosine, -sine], axis=2), np.concatenate([sine, cosine], axis=2)], axis=1
    )
    forward = (table * 2.0**-7).astype(ml_dtypes.bfloat16)
    backward = (table.transpose(0, 2, 1) * 2.0**-6).astype(ml_dtypes.bfloat16)
    return forward, backward


def by_parity(step, last, early, both, late):
    @pl.when(step == 0)
    def _():
        early(0)

    for parity in range(2):

        @pl.when((step > 0) & (step < last) & (step % 2 == parity))
        def _():
            both(1 - parity, parity)

    @pl.when(step == last)
    def _():
        late((last - 1) % 2)


def rows_out_kernel(kept, masks, total, first, blocks, *refs):
    id_refs = refs[:masks]
    image_ref, table_hbm, out_ref, *rest = refs[masks:]
    code_ref = rest[0] if len(rest) == 7 else None
    table, middle, held_even, held_odd, column_terms, sem = rest[-6:]
    held = (held_even, held_odd)
    slots, _, _, rows, _ = out_ref.shape
    radix = OUTER // slots
    slabs = rows // TILE
    step = pl.program_id(0)
    device = lax.axis_index("rows") * masks + lax.axis_index("mask")
    copy = pltpu.make_async_copy(table_hbm.at[:, pl.ds(kept[0], len(kept))], table, sem)
    count = masks * slabs
    share = slots // count

    @pl.when(step == 0)
    def _():
        copy.start()
        for n in range(OUTER):
            column_terms[n] = column_hash(n)

    def spread(r, j, read):
        value = jnp.dot(held[read][r, j], table[r, j], preferred_element_type=jnp.float32)
        value = value.astype(jnp.bfloat16)
        for m in range(masks):
            for p in range(2):
                out_ref[r, m, p, :, j * INNER : (j + 1) * INNER] = value[
                    m * rows : (m + 1) * rows, p * INNER : (p + 1) * INNER
                ]

    def slab(index, carry, read, write):
        mask = index // slabs
        at = pl.multiple_of((index % slabs) * TILE, TILE)
        row_term = row_hash(id_refs, (device * total + first + step) * rows + at, mask)
        dots = [] if read is None else [(i, j) for i in range(share) for j in range(len(kept))]
        every = OUTER // max(len(dots), 1)
        calls = []

        def load(n):
            if dots and len(calls) % every == 0:
                i, j = dots[len(calls) // every]
                spread(index * share + i, j, read)
            calls.append(n)
            code = phase_code(row_term, column_terms[n])
            span = slice(n * INNER, (n + 1) * INNER)
            if code_ref is not None:
                code_ref[mask, pl.ds(at, TILE), span] = code.astype(jnp.bfloat16)
            value = [image_ref[p, pl.ds(at, TILE), span].astype(jnp.float32) for p in range(2)]
            return rotate(value, code, 1)

        def store(r, j, value):
            to = pl.ds(pl.multiple_of(index * TILE, TILE), TILE)
            held[write][r, j, to, 0:INNER] = value[0].astype(jnp.bfloat16)
            held[write][r, j, to, INNER:] = value[1].astype(jnp.bfloat16)

        fourier_part(load, store, middle, kept, radix)
        return carry

    def early(write):
        lax.fori_loop(0, count, functools.partial(slab, read=None, write=write), 0)
        copy.wait()

    def both(read, write):
        lax.fori_loop(0, count, functools.partial(slab, read=read, write=write), 0)

    def late(read):
        def some(index, carry):
            for i in range(share):
                for j in range(len(kept)):
                    spread(index * share + i, j, read)
            return carry

        lax.fori_loop(0, count, some, 0, unroll=2)

    by_parity(step, blocks, early, both, late)


def row_step(count, masks):
    return min(count, max(TILE, 128 // masks))


def row_scratch(slots, kept, masks, rows, buffers):
    held = pltpu.VMEM((slots, kept, masks * rows, 2 * INNER), jnp.bfloat16)
    return [
        pltpu.VMEM((slots, kept, 2 * INNER, 2 * INNER), jnp.bfloat16),
        pltpu.VMEM((slots * kept, 2, TILE, INNER), jnp.float32),
    ] + [held] * buffers


def parameters(flops):
    return {
        "compiler_params": pltpu.CompilerParams(
            vmem_limit_bytes=VMEM_LIMIT, dimension_semantics=("arbitrary",)
        ),
        "cost_estimate": pl.CostEstimate(
            flops=flops, bytes_accessed=40 << 20, transcendentals=0
        ),
    }


def rows_out(kept, ids, image, table, with_code, piece):
    masks = len(ids)
    _, total, width = image.shape
    slots = table.shape[0]
    rows = math.gcd(row_step(total, masks), *piece)
    first, count = piece[0] // rows, piece[1]
    blocks = count // rows
    span = len(kept) * INNER

    def now(i):
        return jnp.minimum(i, blocks - 1)

    def before(i):
        return jnp.maximum(i - 1, 0)

    return pl.pallas_call(
        functools.partial(rows_out_kernel, kept, masks, total // rows, first, blocks),
        grid=(blocks + 1,),
        in_specs=[pl.BlockSpec(memory_space=pltpu.SMEM)] * masks
        + [
            pl.BlockSpec((2, rows, width), lambda i: (0, first + now(i), 0)),
            pl.BlockSpec(memory_space=pl.ANY),
        ],
        out_specs=[
            pl.BlockSpec((slots, masks, 2, rows, span), lambda i: (0, 0, 0, before(i), 0)),
            pl.BlockSpec((masks, rows, width), lambda i: (0, now(i), 0)),
        ][: 1 + with_code],
        out_shape=[
            jax.ShapeDtypeStruct((slots, masks, 2, count, span), jnp.bfloat16),
            jax.ShapeDtypeStruct((masks, count, width), jnp.bfloat16),
        ][: 1 + with_code],
        scratch_shapes=row_scratch(slots, len(kept), masks, rows, 2)
        + [pltpu.VMEM((OUTER, TILE, INNER), jnp.int32), pltpu.SemaphoreType.DMA],
        name="rows_out",
        **parameters(masks * count * width * 1000),
    )(*ids, image, table)


def columns_kernel(share, ins, outs, *refs):
    in_refs = refs[: len(ins)]
    measured_ref, forward_hbm, backward_hbm = refs[len(ins) : len(ins) + 3]
    out_refs = refs[len(ins) + 3 : len(ins) + 3 + len(outs)]
    loss_ref, forward, backward, middle, held, sems = refs[len(ins) + 3 + len(outs) :]
    copies = [
        pltpu.make_async_copy(forward_hbm, forward, sems.at[0]),
        pltpu.make_async_copy(backward_hbm, backward, sems.at[1]),
    ]

    @pl.when(pl.program_id(0) == 0)
    def _():
        for copy in copies:
            copy.start()
        loss_ref[...] = jnp.zeros_like(loss_ref)

    def place(begins, n, group, size, inside):
        if share >= INNER:
            per = share // INNER
            row = (n % per) * INNER + group * size
            piece = max(i for i in range(len(begins)) if begins[i] <= row)
            at = row - begins[piece] + inside
            return piece, n // per, pl.ds(pl.multiple_of(at, TILE), TILE)
        at = group * size + inside
        span = pl.ds(pl.multiple_of(at % share, TILE), TILE)
        return 0, n * (INNER // share) + at // share, span

    def groups(begins, body):
        size = math.gcd(INNER, *begins)
        for group in range(INNER // size):
            lax.fori_loop(0, size // TILE, body(group, size), 0)

    def arrive(group, size, index, carry):
        inside = pl.multiple_of(index * TILE, TILE)

        def load(n):
            piece, source, span = place(ins, n, group, size, inside)
            return [in_refs[piece][source, p, span, :].astype(jnp.float32) for p in range(2)]

        def store(k, value):
            for p in range(2):
                to = pl.multiple_of(p * INNER + group * size + inside, TILE)
                held[k, pl.ds(to, TILE), :] = value[p].astype(jnp.bfloat16)

        fourier64(load, store, middle, -1)
        return carry

    groups(ins, lambda group, size: functools.partial(arrive, group, size))

    @pl.when(pl.program_id(0) == 0)
    def _():
        for copy in copies:
            copy.wait()

    def residual(k, carry):
        spectrum = jnp.dot(forward[k], held[k], preferred_element_type=jnp.float32)
        real, imag = spectrum[:INNER], spectrum[INNER:]
        measured = measured_ref[
            0, pl.ds(pl.multiple_of(k * INNER, INNER), INNER), :
        ].astype(jnp.float32)
        square = real * real + imag * imag + EPSILON
        inverse = lax.rsqrt(square)
        misfit = square * inverse - measured
        kept = 1.0 - measured * inverse
        loss_ref[...] += jnp.sum((misfit * misfit).reshape(INNER // 8, 8, INNER), axis=0)
        weighted = jnp.concatenate([real * kept, imag * kept], axis=0).astype(jnp.bfloat16)
        back = jnp.dot(backward[k], weighted, preferred_element_type=jnp.float32)
        held[k] = back.astype(jnp.bfloat16)
        return carry

    lax.fori_loop(0, OUTER, residual, 0, unroll=2)

    def leave(group, size, index, carry):
        inside = pl.multiple_of(index * TILE, TILE)

        def load(k):
            at = [pl.multiple_of(p * INNER + group * size + inside, TILE) for p in range(2)]
            return [held[k, pl.ds(at[p], TILE), :].astype(jnp.float32) for p in range(2)]

        def store(n, value):
            piece, source, span = place(outs, n, group, size, inside)
            for p in range(2):
                out_refs[piece][source, p, span, :] = value[p].astype(jnp.bfloat16)

        fourier64(load, store, middle, 1)
        return carry

    groups(outs, lambda group, size: functools.partial(leave, group, size))


def columns(chunk, arrived, pieces, measured, forward, backward):
    devices, _, _, width = arrived[0].shape
    share = sum(blocks.shape[2] for blocks in arrived)
    length = devices * share
    steps = width // INNER
    begins = [0]
    for blocks in arrived[:-1]:
        begins.append(begins[-1] + blocks.shape[2])

    def some_rows(count):
        return pl.BlockSpec((devices, 2, count, INNER), lambda i: (0, 0, 0, i))

    *leaving, loss = pl.pallas_call(
        functools.partial(columns_kernel, share, begins, [first for first, _ in pieces]),
        grid=(steps,),
        in_specs=[some_rows(blocks.shape[2]) for blocks in arrived]
        + [
            pl.BlockSpec((1, length, INNER), lambda i: (0, 0, chunk * steps + i)),
            pl.BlockSpec(memory_space=pl.ANY),
            pl.BlockSpec(memory_space=pl.ANY),
        ],
        out_specs=[some_rows(count) for _, count in pieces]
        + [pl.BlockSpec((8, INNER), lambda i: (0, 0))],
        out_shape=[
            jax.ShapeDtypeStruct((devices, 2, count, width), jnp.bfloat16) for _, count in pieces
        ]
        + [jax.ShapeDtypeStruct((8, INNER), jnp.float32)],
        scratch_shapes=[
            pltpu.VMEM((OUTER, 2 * INNER, 2 * INNER), jnp.bfloat16),
            pltpu.VMEM((OUTER, 2 * INNER, 2 * INNER), jnp.bfloat16),
            pltpu.VMEM((OUTER, 2, TILE, INNER), jnp.float32),
            pltpu.VMEM((OUTER, 2 * INNER, INNER), jnp.bfloat16),
            pltpu.SemaphoreType.DMA((2,)),
        ],
        name="columns",
        **parameters(length * width * 2200),
    )(*arrived, measured, forward, backward)
    return leaving, loss


def gather_one(r, j, in_ref, table, held):
    masks = in_ref.shape[1]
    span = slice(j * INNER, (j + 1) * INNER)
    value = jnp.concatenate(
        [
            jnp.concatenate([in_ref[r, m, p, :, span] for p in range(2)], axis=1)
            for m in range(masks)
        ],
        axis=0,
    )
    held[r, j] = jnp.dot(value, table[r, j], preferred_element_type=jnp.float32).astype(
        jnp.bfloat16
    )


def gather_all(kept, in_ref, table, held):
    def some(r, carry):
        for j in range(len(kept)):
            gather_one(r, j, in_ref, table, held)
        return carry

    lax.fori_loop(0, in_ref.shape[0], some, 0, unroll=4)


def fetch_table(kept, table_hbm, table, sem):
    copy = pltpu.make_async_copy(table_hbm.at[:, pl.ds(kept[0], len(kept))], table, sem)

    @pl.when(pl.program_id(0) == 0)
    def _():
        copy.start()
        copy.wait()


def held_tile(held, r, j, index):
    take = pl.ds(pl.multiple_of(index * TILE, TILE), TILE)
    return [
        held[r, j, take, p * INNER : (p + 1) * INNER].astype(jnp.float32) for p in range(2)
    ]


def rows_part_kernel(kept, in_ref, table_hbm, out_ref, table, middle, held, sem):
    slots, masks, _, rows, _ = in_ref.shape
    slabs = rows // TILE
    fetch_table(kept, table_hbm, table, sem)
    gather_all(kept, in_ref, table, held)

    def slab(index, carry):
        mask = index // slabs
        at = pl.multiple_of((index % slabs) * TILE, TILE)

        def load(r, j):
            return held_tile(held, r, j, index)

        def store(n, values):
            for j, value in enumerate(values):
                for p in range(2):
                    out_ref[n, j, mask, p, pl.ds(at, TILE), :] = value[p].astype(jnp.bfloat16)

        inverse_part(load, store, middle, kept, OUTER // slots)
        return carry

    lax.fori_loop(0, masks * slabs, slab, 0)


def rows_part(kept, arrived, table):
    slots, masks, _, count, span = arrived.shape
    rows = row_step(count, masks)
    return pl.pallas_call(
        functools.partial(rows_part_kernel, kept),
        grid=(count // rows,),
        in_specs=[
            pl.BlockSpec((slots, masks, 2, rows, span), lambda i: (0, 0, 0, i, 0)),
            pl.BlockSpec(memory_space=pl.ANY),
        ],
        out_specs=pl.BlockSpec(
            (slots, len(kept), masks, 2, rows, INNER), lambda i: (0, 0, 0, 0, i, 0)
        ),
        out_shape=jax.ShapeDtypeStruct(
            (slots, len(kept), masks, 2, count, INNER), jnp.bfloat16
        ),
        scratch_shapes=row_scratch(slots, len(kept), masks, rows, 1)
        + [pltpu.SemaphoreType.DMA],
        name="rows_part",
        **parameters(masks * count * LENGTH * 600),
    )(arrived, table)


def rows_in_kernel(kept, blocks, code_ref, in_ref, part_ref, table_hbm, *rest):
    out_ref, table, middle, held_even, held_odd, sem = rest[-6:]
    held = (held_even, held_odd)
    slots, masks, _, rows, _ = in_ref.shape
    radix = OUTER // slots
    slabs = rows // TILE
    count = masks * slabs
    share = slots // count
    fetch_table(kept, table_hbm, table, sem)

    def slab(index, carry, first, read, write):
        mask = index // slabs
        at = pl.multiple_of((index % slabs) * TILE, TILE)
        dots = [] if write is None else [(i, j) for i in range(share) for j in range(len(kept))]
        every = slots * len(kept) // max(len(dots), 1)
        calls = []

        def load(r, j):
            if dots and len(calls) % every == 0:
                i, k = dots[len(calls) // every]
                gather_one(index * share + i, k, in_ref, table, held[write])
            calls.append(r)
            return held_tile(held[read], r, j, index)

        def store(n, values):
            early = [
                [part_ref[n, j, mask, p, pl.ds(at, TILE), :].astype(jnp.float32) for p in range(2)]
                for j in range(radix - len(kept))
            ]
            for t, value in enumerate(fourier(early + values, 1)):
                tile = n + slots * t
                span = slice(tile * INNER, (tile + 1) * INNER)
                code = code_ref[mask, pl.ds(at, TILE), span].astype(jnp.float32)
                value = rotate(value, code, -1)
                for p in range(2):
                    if first:
                        out_ref[p, pl.ds(at, TILE), span] = value[p]
                    else:
                        out_ref[p, pl.ds(at, TILE), span] += value[p]

        inverse_part(load, store, middle, kept, radix)
        return carry

    def early(write):
        gather_all(kept, in_ref, table, held[write])

    def both(read, write):
        pair = {"read": read, "write": write}
        lax.fori_loop(0, slabs, functools.partial(slab, first=True, **pair), 0)
        lax.fori_loop(slabs, count, functools.partial(slab, first=False, **pair), 0)

    def late(read):
        both(read, None)

    by_parity(pl.program_id(0), blocks, early, both, late)


def rows_in(kept, code, arrived, part, table, piece, filled):
    slots, masks, _, count, span = arrived.shape
    total = code.shape[1]
    rows = math.gcd(row_step(total, masks), *piece)
    first, blocks = piece[0] // rows, count // rows

    def now(i):
        return jnp.minimum(i, blocks - 1)

    def before(i):
        return jnp.maximum(i - 1, 0)

    return pl.pallas_call(
        functools.partial(rows_in_kernel, kept, blocks),
        grid=(blocks + 1,),
        in_specs=[
            pl.BlockSpec((masks, rows, LENGTH), lambda i: (0, first + before(i), 0)),
            pl.BlockSpec((slots, masks, 2, rows, span), lambda i: (0, 0, 0, now(i), 0)),
            pl.BlockSpec(
                (slots,) + part.shape[1:4] + (rows, INNER),
                lambda i: (0, 0, 0, 0, first + before(i), 0),
            ),
            pl.BlockSpec(memory_space=pl.ANY),
        ]
        + [pl.BlockSpec(memory_space=pl.ANY)] * len(filled),
        out_specs=pl.BlockSpec((2, rows, LENGTH), lambda i: (0, first + before(i), 0)),
        out_shape=jax.ShapeDtypeStruct((2, total, LENGTH), jnp.float32),
        input_output_aliases={4: 0} if filled else {},
        scratch_shapes=row_scratch(slots, len(kept), masks, rows, 2)
        + [pltpu.SemaphoreType.DMA],
        name="rows_in",
        **parameters(masks * count * LENGTH * 1000),
    )(code, arrived, part, table, *filled)


AXES = ("rows", "mask")
CHUNKS = 2


def exchange(blocks):
    flat = blocks.reshape((-1,) + blocks.shape[-3:])
    flat = lax.all_to_all(flat, AXES, split_axis=0, concat_axis=0, tiled=True)
    return flat.reshape(blocks.shape)


def add_over(value, devices, factor, stride):
    total = value
    for d in range(1, factor):
        pairs = []
        for i in range(devices):
            digit = i // stride % factor
            pairs.append((i, i + ((digit + d) % factor - digit) * stride))
        total = total + lax.ppermute(value, AXES, pairs)
    return total


def shards(slots, masks, image, measured, mask_ids):
    forward, backward = (jnp.asarray(table) for table in table_pair())
    _, count, width = image.shape
    devices = slots * masks
    radix = OUTER // slots
    each = radix // CHUNKS
    kept = [tuple(range(c * each, (c + 1) * each)) for c in range(CHUNKS)]
    by_slot = (slots, radix, 2 * INNER, 2 * INNER)
    out_table, in_table = backward.reshape(by_slot), forward.reshape(by_slot)
    ids = [mask_ids] + [
        lax.ppermute(mask_ids, "mask", [((m + d) % masks, m) for m in range(masks)])
        for d in range(1, masks)
    ]
    whole = [(0, count)]
    head, tail = whole, whole
    if count >= 2 * INNER:
        small = 2 * TILE
        head = [(0, small), (small, count - small)]
        tail = [(0, count - small), (count - small, small)]

    def forth(c, pieces, image, with_code):
        arrived = []
        for piece in pieces:
            sent, *code = rows_out(kept[c], ids, image, out_table, with_code, piece)
            sent, image = lax.optimization_barrier((sent, image))
            if arrived:
                sent, arrived[-1] = lax.optimization_barrier((sent, arrived[-1]))
            arrived.append(exchange(sent.reshape((-1,) + sent.shape[2:])))
        return arrived, code, image

    def back(blocks):
        arrived = exchange(blocks)
        return arrived.reshape((slots, masks) + blocks.shape[1:])

    arrived, _, image = forth(0, head, image, False)
    (leaving,), loss_early = columns(0, arrived, whole, measured, forward, backward)
    arrived, (code,), image = forth(1, whole, image, True)
    leaving_last, loss_late = columns(1, arrived, tail, measured, forward, backward)
    first = 1 << (3 * devices.bit_length() // 5)
    loss = (jnp.sum(loss_early) + jnp.sum(loss_late)).reshape(1)
    loss = add_over(loss, devices, first, 1)
    returned, leaving_last, loss = lax.optimization_barrier((back(leaving), leaving_last, loss))
    part = rows_part(kept[0], returned, in_table)
    part, loss = lax.optimization_barrier((part, loss))
    loss = add_over(loss, devices, devices // first, first)
    last = ()
    filled = ()
    for piece, blocks in zip(tail, leaving_last):
        if piece != tail[0]:
            blocks, last, part, loss = lax.optimization_barrier((blocks, last, part, loss))
        last = back(blocks)
        filled = (rows_in(kept[1], code, last, part, in_table, piece, filled),)
    return filled[0], loss[0] / (masks * width * width)


def solution(mesh):
    slots, masks = mesh.shape["rows"], mesh.shape["mask"]
    return jax.shard_map(
        functools.partial(shards, slots, masks),
        mesh=mesh,
        in_specs=(P(None, AXES, None), P("mask", None, "rows"), P("mask")),
        out_specs=(P(None, AXES, None), P()),
        check_vma=False,
    )
```

```python
import functools
import math

import jax
import jax.numpy as jnp
import ml_dtypes
import numpy as np
from jax import lax
from jax.experimental import pallas as pl
from jax.experimental.pallas import tpu as pltpu
from jax.sharding import PartitionSpec as P

INNER = 128
OUTER = 64
LENGTH = INNER * OUTER
EPSILON = 0.25
TILE = 16
VMEM_LIMIT = 58 * 1024 * 1024
ROOT_HALF = math.sqrt(0.5)

ROW_MULTIPLIER = 73856093
COLUMN_MULTIPLIER = 19349663
MASK_MULTIPLIER = 83492791
MIX_MULTIPLIER = 1274126177


def wrap(value):
    return (value + 2**31) % 2**32 - 2**31


def add(a, b):
    return (a[0] + b[0], a[1] + b[1])


def sub(a, b):
    return (a[0] - b[0], a[1] - b[1])


def quarter(a, sign):
    return (-a[1], a[0]) if sign > 0 else (a[1], -a[0])


def turn(a, step, count, sign):
    step = step % count
    if step == 0:
        return a
    if 4 * step == count:
        return quarter(a, sign)
    if 2 * step == count:
        return (-a[0], -a[1])
    if 4 * step == 3 * count:
        return quarter(a, -sign)
    if 8 * step == count:
        q = quarter(a, sign)
        return ((a[0] + q[0]) * ROOT_HALF, (a[1] + q[1]) * ROOT_HALF)
    if 8 * step == 3 * count:
        q = quarter(a, sign)
        return ((q[0] - a[0]) * ROOT_HALF, (q[1] - a[1]) * ROOT_HALF)
    angle = sign * 2.0 * math.pi * step / count
    cosine, sine = math.cos(angle), math.sin(angle)
    return (a[0] * cosine - a[1] * sine, a[0] * sine + a[1] * cosine)


def fourier4(x, sign):
    t0, t1 = add(x[0], x[2]), sub(x[0], x[2])
    t2, t3 = add(x[1], x[3]), quarter(sub(x[1], x[3]), sign)
    return [add(t0, t2), add(t1, t3), sub(t0, t2), sub(t1, t3)]


def fourier8(x, sign):
    even = fourier4(x[0::2], sign)
    odd = fourier4(x[1::2], sign)
    odd = [turn(odd[k], k, 8, sign) for k in range(4)]
    return [add(even[k], odd[k]) for k in range(4)] + [sub(even[k], odd[k]) for k in range(4)]


def fourier(x, sign):
    if len(x) == 1:
        return x
    if len(x) == 2:
        return [add(x[0], x[1]), sub(x[0], x[1])]
    return fourier4(x, sign) if len(x) == 4 else fourier8(x, sign)


def fourier64(load, store, middle, sign):
    for b in range(8):
        values = fourier8([load(8 * a + b) for a in range(8)], sign)
        for c in range(8):
            real, imag = turn(values[c], b * c, 64, sign)
            middle[c * 8 + b, 0] = real
            middle[c * 8 + b, 1] = imag
    for c in range(8):
        values = fourier8([(middle[c * 8 + b, 0], middle[c * 8 + b, 1]) for b in range(8)], sign)
        for d in range(8):
            store(c + 8 * d, values[d])


def fourier_part(load, store, middle, kept, radix):
    size = OUTER // radix
    first = size // 4
    for b in range(4):
        groups = [[] for _ in kept]
        for a in range(first):
            n = 4 * a + b
            values = fourier([load(n + size * t) for t in range(radix)], -1)
            for at, j in enumerate(kept):
                groups[at].append(turn(values[j], n * j, OUTER, -1))
        for at in range(len(kept)):
            values = fourier(groups[at], -1)
            for c in range(first):
                real, imag = turn(values[c], b * c, size, -1)
                middle[(at * first + c) * 4 + b, 0] = real
                middle[(at * first + c) * 4 + b, 1] = imag
    for at in range(len(kept)):
        for c in range(first):
            slot = (at * first + c) * 4
            values = fourier4([(middle[slot + b, 0], middle[slot + b, 1]) for b in range(4)], -1)
            for d in range(4):
                store(c + first * d, at, values[d])


def inverse_part(load, store, middle, kept, radix):
    size = OUTER // radix
    first = size // 4
    for at in range(len(kept)):
        for b in range(4):
            values = fourier([load(4 * a + b, at) for a in range(first)], 1)
            for c in range(first):
                real, imag = turn(values[c], b * c, size, 1)
                middle[(at * first + c) * 4 + b, 0] = real
                middle[(at * first + c) * 4 + b, 1] = imag
    for c in range(first):
        sums = []
        for at in range(len(kept)):
            slot = (at * first + c) * 4
            sums.append(
                fourier4([(middle[slot + b, 0], middle[slot + b, 1]) for b in range(4)], 1)
            )
        for d in range(4):
            n = c + first * d
            store(n, [turn(sums[at][d], n * j, OUTER, 1) for at, j in enumerate(kept)])


def fold(mixed):
    return mixed ^ lax.shift_right_logical(mixed, jnp.full(mixed.shape, 13, jnp.int32))


def phase_code(row_term, column_term):
    product = (row_term ^ column_term) * jnp.int32(wrap(4 * MIX_MULTIPLIER))
    code = lax.shift_right_arithmetic(product, jnp.full(product.shape, 30, jnp.int32))
    return code.astype(jnp.float32)


def rotate(value, code, direction):
    size = jnp.abs(code)
    cosine = 1 - size
    sine = code * (2 - size)
    left, right = value[0] * sine, value[1] * sine
    if direction > 0:
        return (value[0] * cosine - right, left + value[1] * cosine)
    return (value[0] * cosine + right, value[1] * cosine - left)


def row_hash(id_refs, base, mask):
    masks = len(id_refs)
    rows = lax.broadcasted_iota(jnp.int32, (TILE, INNER), 0) + base
    ahead = lax.rem(mask - lax.axis_index("mask") + masks, masks)
    mask_id = id_refs[0][0]
    for d in range(1, masks):
        mask_id = jnp.where(ahead == d, id_refs[d][0], mask_id)
    mask_term = (mask_id + 1) * jnp.int32(MASK_MULTIPLIER)
    return fold((rows * jnp.int32(ROW_MULTIPLIER)) ^ mask_term)


def column_hash(tile):
    lanes = lax.broadcasted_iota(jnp.int32, (TILE, INNER), 1)
    shift = jnp.int32(wrap(tile * INNER * COLUMN_MULTIPLIER))
    return fold(lanes * jnp.int32(COLUMN_MULTIPLIER) + shift)


def table_pair():
    inner = np.arange(INNER, dtype=np.int64)
    outer = np.arange(OUTER, dtype=np.int64)
    steps = inner[None, None, :] * (outer[:, None, None] + OUTER * inner[None, :, None]) % LENGTH
    angles = steps * (-2.0 * math.pi / LENGTH)
    cosine, sine = np.cos(angles), np.sin(angles)
    table = np.concatenate(
        [np.concatenate([cosine, -sine], axis=2), np.concatenate([sine, cosine], axis=2)], axis=1
    )
    forward = (table * 2.0**-7).astype(ml_dtypes.bfloat16)
    backward = (table.transpose(0, 2, 1) * 2.0**-6).astype(ml_dtypes.bfloat16)
    return forward, backward


def by_parity(step, last, early, both, late):
    @pl.when(step == 0)
    def _():
        early(0)

    for parity in range(2):

        @pl.when((step > 0) & (step < last) & (step % 2 == parity))
        def _():
            both(1 - parity, parity)

    @pl.when(step == last)
    def _():
        late((last - 1) % 2)


def rows_out_kernel(kept, masks, total, first, blocks, *refs):
    id_refs = refs[:masks]
    image_ref, table_hbm, out_ref, *rest = refs[masks:]
    code_ref = rest[0] if len(rest) == 7 else None
    table, middle, held_even, held_odd, column_terms, sem = rest[-6:]
    held = (held_even, held_odd)
    _, slots, _, rows, _ = out_ref.shape
    radix = OUTER // slots
    slabs = rows // TILE
    step = pl.program_id(0)
    device = lax.axis_index("rows") * masks + lax.axis_index("mask")
    copy = pltpu.make_async_copy(table_hbm.at[:, pl.ds(kept[0], len(kept))], table, sem)
    count = masks * slabs
    share = slots // count

    @pl.when(step == 0)
    def _():
        copy.start()
        for n in range(OUTER):
            column_terms[n] = column_hash(n)

    def spread(r, j, read):
        value = jnp.dot(held[read][r, j], table[r, j], preferred_element_type=jnp.float32)
        value = value.astype(jnp.bfloat16)
        for m in range(masks):
            for p in range(2):
                out_ref[m, r, p, :, j * INNER : (j + 1) * INNER] = value[
                    m * rows : (m + 1) * rows, p * INNER : (p + 1) * INNER
                ]

    def slab(index, carry, read, write):
        mask = index // slabs
        at = pl.multiple_of((index % slabs) * TILE, TILE)
        row_term = row_hash(id_refs, (device * total + first + step) * rows + at, mask)
        dots = [] if read is None else [(i, j) for i in range(share) for j in range(len(kept))]
        every = OUTER // max(len(dots), 1)
        calls = []

        def load(n):
            if dots and len(calls) % every == 0:
                i, j = dots[len(calls) // every]
                spread(index * share + i, j, read)
            calls.append(n)
            code = phase_code(row_term, column_terms[n])
            span = slice(n * INNER, (n + 1) * INNER)
            if code_ref is not None:
                code_ref[mask, pl.ds(at, TILE), span] = code.astype(jnp.bfloat16)
            value = [image_ref[p, pl.ds(at, TILE), span].astype(jnp.float32) for p in range(2)]
            return rotate(value, code, 1)

        def store(r, j, value):
            to = pl.ds(pl.multiple_of(index * TILE, TILE), TILE)
            held[write][r, j, to, 0:INNER] = value[0].astype(jnp.bfloat16)
            held[write][r, j, to, INNER:] = value[1].astype(jnp.bfloat16)

        fourier_part(load, store, middle, kept, radix)
        return carry

    def early(write):
        lax.fori_loop(0, count, functools.partial(slab, read=None, write=write), 0)
        copy.wait()

    def both(read, write):
        lax.fori_loop(0, count, functools.partial(slab, read=read, write=write), 0)

    def late(read):
        def some(index, carry):
            for i in range(share):
                for j in range(len(kept)):
                    spread(index * share + i, j, read)
            return carry

        lax.fori_loop(0, count, some, 0, unroll=2)

    by_parity(step, blocks, early, both, late)


def row_step(count, masks):
    return min(count, max(TILE, 128 // masks))


def row_scratch(slots, kept, masks, rows, buffers):
    held = pltpu.VMEM((slots, kept, masks * rows, 2 * INNER), jnp.bfloat16)
    return [
        pltpu.VMEM((slots, kept, 2 * INNER, 2 * INNER), jnp.bfloat16),
        pltpu.VMEM((slots * kept, 2, TILE, INNER), jnp.float32),
    ] + [held] * buffers


def parameters(flops):
    return {
        "compiler_params": pltpu.CompilerParams(
            vmem_limit_bytes=VMEM_LIMIT, dimension_semantics=("arbitrary",)
        ),
        "cost_estimate": pl.CostEstimate(
            flops=flops, bytes_accessed=40 << 20, transcendentals=0
        ),
    }


def rows_out(kept, ids, image, table, with_code, piece):
    masks = len(ids)
    _, total, width = image.shape
    slots = table.shape[0]
    rows = math.gcd(row_step(total, masks), *piece)
    first, count = piece[0] // rows, piece[1]
    blocks = count // rows
    span = len(kept) * INNER

    def now(i):
        return jnp.minimum(i, blocks - 1)

    def before(i):
        return jnp.maximum(i - 1, 0)

    return pl.pallas_call(
        functools.partial(rows_out_kernel, kept, masks, total // rows, first, blocks),
        grid=(blocks + 1,),
        in_specs=[pl.BlockSpec(memory_space=pltpu.SMEM)] * masks
        + [
            pl.BlockSpec((2, rows, width), lambda i: (0, first + now(i), 0)),
            pl.BlockSpec(memory_space=pl.ANY),
        ],
        out_specs=[
            pl.BlockSpec((masks, slots, 2, rows, span), lambda i: (0, 0, 0, before(i), 0)),
            pl.BlockSpec((masks, rows, width), lambda i: (0, now(i), 0)),
        ][: 1 + with_code],
        out_shape=[
            jax.ShapeDtypeStruct((masks, slots, 2, count, span), jnp.bfloat16),
            jax.ShapeDtypeStruct((masks, count, width), jnp.bfloat16),
        ][: 1 + with_code],
        scratch_shapes=row_scratch(slots, len(kept), masks, rows, 2)
        + [pltpu.VMEM((OUTER, TILE, INNER), jnp.int32), pltpu.SemaphoreType.DMA],
        name="rows_out",
        **parameters(masks * count * width * 1000),
    )(*ids, image, table)


def columns_kernel(masks, share, ins, outs, *refs):
    in_refs = refs[: len(ins)]
    measured_ref, forward_hbm, backward_hbm = refs[len(ins) : len(ins) + 3]
    out_refs = refs[len(ins) + 3 : len(ins) + 3 + len(outs)]
    loss_ref, forward, backward, middle, held, sems = refs[len(ins) + 3 + len(outs) :]
    copies = [
        pltpu.make_async_copy(forward_hbm, forward, sems.at[0]),
        pltpu.make_async_copy(backward_hbm, backward, sems.at[1]),
    ]

    @pl.when(pl.program_id(0) == 0)
    def _():
        for copy in copies:
            copy.start()
        loss_ref[...] = jnp.zeros_like(loss_ref)

    def position(device):
        return device % masks * (in_refs[0].shape[0] // masks) + device // masks

    def place(begins, n, group, size, inside):
        if share >= INNER:
            per = share // INNER
            row = (n % per) * INNER + group * size
            piece = max(i for i in range(len(begins)) if begins[i] <= row)
            at = row - begins[piece] + inside
            return piece, position(n // per), pl.ds(pl.multiple_of(at, TILE), TILE)
        at = group * size + inside
        span = pl.ds(pl.multiple_of(at % share, TILE), TILE)
        return 0, position(n * (INNER // share) + at // share), span

    def groups(begins, body):
        size = math.gcd(INNER, *begins)
        for group in range(INNER // size):
            lax.fori_loop(0, size // TILE, body(group, size), 0)

    def arrive(group, size, index, carry):
        inside = pl.multiple_of(index * TILE, TILE)

        def load(n):
            piece, source, span = place(ins, n, group, size, inside)
            return [in_refs[piece][source, p, span, :].astype(jnp.float32) for p in range(2)]

        def store(k, value):
            for p in range(2):
                to = pl.multiple_of(p * INNER + group * size + inside, TILE)
                held[k, pl.ds(to, TILE), :] = value[p].astype(jnp.bfloat16)

        fourier64(load, store, middle, -1)
        return carry

    groups(ins, lambda group, size: functools.partial(arrive, group, size))

    @pl.when(pl.program_id(0) == 0)
    def _():
        for copy in copies:
            copy.wait()

    def residual(k, carry):
        spectrum = jnp.dot(forward[k], held[k], preferred_element_type=jnp.float32)
        real, imag = spectrum[:INNER], spectrum[INNER:]
        measured = measured_ref[
            0, pl.ds(pl.multiple_of(k * INNER, INNER), INNER), :
        ].astype(jnp.float32)
        square = real * real + imag * imag + EPSILON
        inverse = lax.rsqrt(square)
        misfit = square * inverse - measured
        kept = 1.0 - measured * inverse
        loss_ref[...] += jnp.sum((misfit * misfit).reshape(INNER // 8, 8, INNER), axis=0)
        weighted = jnp.concatenate([real * kept, imag * kept], axis=0).astype(jnp.bfloat16)
        back = jnp.dot(backward[k], weighted, preferred_element_type=jnp.float32)
        held[k] = back.astype(jnp.bfloat16)
        return carry

    lax.fori_loop(0, OUTER, residual, 0, unroll=2)

    def leave(group, size, index, carry):
        inside = pl.multiple_of(index * TILE, TILE)

        def load(k):
            at = [pl.multiple_of(p * INNER + group * size + inside, TILE) for p in range(2)]
            return [held[k, pl.ds(at[p], TILE), :].astype(jnp.float32) for p in range(2)]

        def store(n, value):
            piece, source, span = place(outs, n, group, size, inside)
            for p in range(2):
                out_refs[piece][source, p, span, :] = value[p].astype(jnp.bfloat16)

        fourier64(load, store, middle, 1)
        return carry

    groups(outs, lambda group, size: functools.partial(leave, group, size))


def columns(chunk, masks, arrived, pieces, measured, forward, backward):
    devices, _, _, width = arrived[0].shape
    share = sum(blocks.shape[2] for blocks in arrived)
    length = devices * share
    steps = width // INNER
    begins = [0]
    for blocks in arrived[:-1]:
        begins.append(begins[-1] + blocks.shape[2])

    def some_rows(count):
        return pl.BlockSpec((devices, 2, count, INNER), lambda i: (0, 0, 0, i))

    *leaving, loss = pl.pallas_call(
        functools.partial(columns_kernel, masks, share, begins, [first for first, _ in pieces]),
        grid=(steps,),
        in_specs=[some_rows(blocks.shape[2]) for blocks in arrived]
        + [
            pl.BlockSpec((1, length, INNER), lambda i: (0, 0, chunk * steps + i)),
            pl.BlockSpec(memory_space=pl.ANY),
            pl.BlockSpec(memory_space=pl.ANY),
        ],
        out_specs=[some_rows(count) for _, count in pieces]
        + [pl.BlockSpec((8, INNER), lambda i: (0, 0))],
        out_shape=[
            jax.ShapeDtypeStruct((devices, 2, count, width), jnp.bfloat16) for _, count in pieces
        ]
        + [jax.ShapeDtypeStruct((8, INNER), jnp.float32)],
        scratch_shapes=[
            pltpu.VMEM((OUTER, 2 * INNER, 2 * INNER), jnp.bfloat16),
            pltpu.VMEM((OUTER, 2 * INNER, 2 * INNER), jnp.bfloat16),
            pltpu.VMEM((OUTER, 2, TILE, INNER), jnp.float32),
            pltpu.VMEM((OUTER, 2 * INNER, INNER), jnp.bfloat16),
            pltpu.SemaphoreType.DMA((2,)),
        ],
        name="columns",
        **parameters(length * width * 2200),
    )(*arrived, measured, forward, backward)
    return leaving, loss


def gather_one(r, j, in_ref, table, held):
    masks = in_ref.shape[0]
    span = slice(j * INNER, (j + 1) * INNER)
    value = jnp.concatenate(
        [
            jnp.concatenate([in_ref[m, r, p, :, span] for p in range(2)], axis=1)
            for m in range(masks)
        ],
        axis=0,
    )
    held[r, j] = jnp.dot(value, table[r, j], preferred_element_type=jnp.float32).astype(
        jnp.bfloat16
    )


def gather_all(kept, in_ref, table, held):
    def some(r, carry):
        for j in range(len(kept)):
            gather_one(r, j, in_ref, table, held)
        return carry

    lax.fori_loop(0, in_ref.shape[1], some, 0, unroll=4)


def fetch_table(kept, table_hbm, table, sem):
    copy = pltpu.make_async_copy(table_hbm.at[:, pl.ds(kept[0], len(kept))], table, sem)

    @pl.when(pl.program_id(0) == 0)
    def _():
        copy.start()
        copy.wait()


def held_tile(held, r, j, index):
    take = pl.ds(pl.multiple_of(index * TILE, TILE), TILE)
    return [
        held[r, j, take, p * INNER : (p + 1) * INNER].astype(jnp.float32) for p in range(2)
    ]


def rows_part_kernel(kept, in_ref, table_hbm, out_ref, table, middle, held, sem):
    masks, slots, _, rows, _ = in_ref.shape
    slabs = rows // TILE
    fetch_table(kept, table_hbm, table, sem)
    gather_all(kept, in_ref, table, held)

    def slab(index, carry):
        mask = index // slabs
        at = pl.multiple_of((index % slabs) * TILE, TILE)

        def load(r, j):
            return held_tile(held, r, j, index)

        def store(n, values):
            for j, value in enumerate(values):
                for p in range(2):
                    out_ref[n, j, mask, p, pl.ds(at, TILE), :] = value[p].astype(jnp.bfloat16)

        inverse_part(load, store, middle, kept, OUTER // slots)
        return carry

    lax.fori_loop(0, masks * slabs, slab, 0)


def rows_part(kept, arrived, table):
    masks, slots, _, count, span = arrived.shape
    rows = row_step(count, masks)
    return pl.pallas_call(
        functools.partial(rows_part_kernel, kept),
        grid=(count // rows,),
        in_specs=[
            pl.BlockSpec((masks, slots, 2, rows, span), lambda i: (0, 0, 0, i, 0)),
            pl.BlockSpec(memory_space=pl.ANY),
        ],
        out_specs=pl.BlockSpec(
            (slots, len(kept), masks, 2, rows, INNER), lambda i: (0, 0, 0, 0, i, 0)
        ),
        out_shape=jax.ShapeDtypeStruct(
            (slots, len(kept), masks, 2, count, INNER), jnp.bfloat16
        ),
        scratch_shapes=row_scratch(slots, len(kept), masks, rows, 1)
        + [pltpu.SemaphoreType.DMA],
        name="rows_part",
        **parameters(masks * count * LENGTH * 600),
    )(arrived, table)


def rows_in_kernel(kept, blocks, code_ref, in_ref, part_ref, table_hbm, *rest):
    out_ref, table, middle, held_even, held_odd, sem = rest[-6:]
    held = (held_even, held_odd)
    masks, slots, _, rows, _ = in_ref.shape
    radix = OUTER // slots
    slabs = rows // TILE
    count = masks * slabs
    share = slots // count
    fetch_table(kept, table_hbm, table, sem)

    def slab(index, carry, first, read, write):
        mask = index // slabs
        at = pl.multiple_of((index % slabs) * TILE, TILE)
        dots = [] if write is None else [(i, j) for i in range(share) for j in range(len(kept))]
        every = slots * len(kept) // max(len(dots), 1)
        calls = []

        def load(r, j):
            if dots and len(calls) % every == 0:
                i, k = dots[len(calls) // every]
                gather_one(index * share + i, k, in_ref, table, held[write])
            calls.append(r)
            return held_tile(held[read], r, j, index)

        def store(n, values):
            early = [
                [part_ref[n, j, mask, p, pl.ds(at, TILE), :].astype(jnp.float32) for p in range(2)]
                for j in range(radix - len(kept))
            ]
            for t, value in enumerate(fourier(early + values, 1)):
                tile = n + slots * t
                span = slice(tile * INNER, (tile + 1) * INNER)
                code = code_ref[mask, pl.ds(at, TILE), span].astype(jnp.float32)
                value = rotate(value, code, -1)
                for p in range(2):
                    if first:
                        out_ref[p, pl.ds(at, TILE), span] = value[p]
                    else:
                        out_ref[p, pl.ds(at, TILE), span] += value[p]

        inverse_part(load, store, middle, kept, radix)
        return carry

    def early(write):
        gather_all(kept, in_ref, table, held[write])

    def both(read, write):
        pair = {"read": read, "write": write}
        lax.fori_loop(0, slabs, functools.partial(slab, first=True, **pair), 0)
        lax.fori_loop(slabs, count, functools.partial(slab, first=False, **pair), 0)

    def late(read):
        both(read, None)

    by_parity(pl.program_id(0), blocks, early, both, late)


def rows_in(kept, code, arrived, part, table, piece, filled):
    masks, slots, _, count, span = arrived.shape
    total = code.shape[1]
    rows = math.gcd(row_step(total, masks), *piece)
    first, blocks = piece[0] // rows, count // rows

    def now(i):
        return jnp.minimum(i, blocks - 1)

    def before(i):
        return jnp.maximum(i - 1, 0)

    return pl.pallas_call(
        functools.partial(rows_in_kernel, kept, blocks),
        grid=(blocks + 1,),
        in_specs=[
            pl.BlockSpec((masks, rows, LENGTH), lambda i: (0, first + before(i), 0)),
            pl.BlockSpec((masks, slots, 2, rows, span), lambda i: (0, 0, 0, now(i), 0)),
            pl.BlockSpec(
                (slots,) + part.shape[1:4] + (rows, INNER),
                lambda i: (0, 0, 0, 0, first + before(i), 0),
            ),
            pl.BlockSpec(memory_space=pl.ANY),
        ]
        + [pl.BlockSpec(memory_space=pl.ANY)] * len(filled),
        out_specs=pl.BlockSpec((2, rows, LENGTH), lambda i: (0, first + before(i), 0)),
        out_shape=jax.ShapeDtypeStruct((2, total, LENGTH), jnp.float32),
        input_output_aliases={4: 0} if filled else {},
        scratch_shapes=row_scratch(slots, len(kept), masks, rows, 2)
        + [pltpu.SemaphoreType.DMA],
        name="rows_in",
        **parameters(masks * count * LENGTH * 1000),
    )(code, arrived, part, table, *filled)


AXES = ("rows", "mask")
CHUNKS = 2


def exchange(blocks):
    flat = blocks.reshape((-1,) + blocks.shape[-3:])
    flat = lax.all_to_all(flat, AXES[::-1], split_axis=0, concat_axis=0, tiled=True)
    return flat.reshape(blocks.shape)


def add_over(value, devices, factor, stride):
    total = value
    for d in range(1, factor):
        pairs = []
        for i in range(devices):
            digit = i // stride % factor
            pairs.append((i, i + ((digit + d) % factor - digit) * stride))
        total = total + lax.ppermute(value, AXES, pairs)
    return total


def shards(slots, masks, image, measured, mask_ids):
    forward, backward = (jnp.asarray(table) for table in table_pair())
    _, count, width = image.shape
    devices = slots * masks
    radix = OUTER // slots
    each = radix // CHUNKS
    kept = [tuple(range(c * each, (c + 1) * each)) for c in range(CHUNKS)]
    by_slot = (slots, radix, 2 * INNER, 2 * INNER)
    out_table, in_table = backward.reshape(by_slot), forward.reshape(by_slot)
    ids = [mask_ids] + [
        lax.ppermute(mask_ids, "mask", [((m + d) % masks, m) for m in range(masks)])
        for d in range(1, masks)
    ]
    whole = [(0, count)]
    head, tail = whole, whole
    if count >= 2 * INNER:
        small = 2 * TILE
        head = [(0, small), (small, count - small)]
        tail = [(0, count - small), (count - small, small)]

    def forth(c, pieces, image, with_code):
        arrived = []
        for piece in pieces:
            sent, *code = rows_out(kept[c], ids, image, out_table, with_code, piece)
            sent, image = lax.optimization_barrier((sent, image))
            if arrived:
                sent, arrived[-1] = lax.optimization_barrier((sent, arrived[-1]))
            arrived.append(exchange(sent.reshape((-1,) + sent.shape[2:])))
        return arrived, code, image

    def back(blocks):
        arrived = exchange(blocks)
        return arrived.reshape((masks, slots) + blocks.shape[1:])

    arrived, _, image = forth(0, head, image, False)
    (leaving,), loss_early = columns(0, masks, arrived, whole, measured, forward, backward)
    arrived, (code,), image = forth(1, whole, image, True)
    leaving_last, loss_late = columns(1, masks, arrived, tail, measured, forward, backward)
    first = 1 << (3 * devices.bit_length() // 5)
    loss = (jnp.sum(loss_early) + jnp.sum(loss_late)).reshape(1)
    loss = add_over(loss, devices, first, 1)
    returned, leaving_last, loss = lax.optimization_barrier((back(leaving), leaving_last, loss))
    part = rows_part(kept[0], returned, in_table)
    part, loss = lax.optimization_barrier((part, loss))
    loss = add_over(loss, devices, devices // first, first)
    last = ()
    filled = ()
    for piece, blocks in zip(tail, leaving_last):
        if piece != tail[0]:
            blocks, last, part, loss = lax.optimization_barrier((blocks, last, part, loss))
        last = back(blocks)
        filled = (rows_in(kept[1], code, last, part, in_table, piece, filled),)
    return filled[0], loss[0] / (masks * width * width)


def solution(mesh):
    slots, masks = mesh.shape["rows"], mesh.shape["mask"]
    return jax.shard_map(
        functools.partial(shards, slots, masks),
        mesh=mesh,
        in_specs=(P(None, AXES, None), P("mask", None, "rows"), P("mask")),
        out_specs=(P(None, AXES, None), P()),
        check_vma=False,
    )
```

```python
import functools
import math

import jax
import jax.numpy as jnp
import ml_dtypes
import numpy as np
from jax import lax
from jax.experimental import pallas as pl
from jax.experimental.pallas import tpu as pltpu
from jax.sharding import PartitionSpec as P

INNER = 128
OUTER = 64
LENGTH = INNER * OUTER
EPSILON = 0.25
TILE = 16
VMEM_LIMIT = 58 * 1024 * 1024
ROOT_HALF = math.sqrt(0.5)

ROW_MULTIPLIER = 73856093
COLUMN_MULTIPLIER = 19349663
MASK_MULTIPLIER = 83492791
MIX_MULTIPLIER = 1274126177


def wrap(value):
    return (value + 2**31) % 2**32 - 2**31


def add(a, b):
    return (a[0] + b[0], a[1] + b[1])


def sub(a, b):
    return (a[0] - b[0], a[1] - b[1])


def quarter(a, sign):
    return (-a[1], a[0]) if sign > 0 else (a[1], -a[0])


def turn(a, step, count, sign):
    step = step % count
    if step == 0:
        return a
    if 4 * step == count:
        return quarter(a, sign)
    if 2 * step == count:
        return (-a[0], -a[1])
    if 4 * step == 3 * count:
        return quarter(a, -sign)
    if 8 * step == count:
        q = quarter(a, sign)
        return ((a[0] + q[0]) * ROOT_HALF, (a[1] + q[1]) * ROOT_HALF)
    if 8 * step == 3 * count:
        q = quarter(a, sign)
        return ((q[0] - a[0]) * ROOT_HALF, (q[1] - a[1]) * ROOT_HALF)
    angle = sign * 2.0 * math.pi * step / count
    cosine, sine = math.cos(angle), math.sin(angle)
    return (a[0] * cosine - a[1] * sine, a[0] * sine + a[1] * cosine)


def fourier4(x, sign):
    t0, t1 = add(x[0], x[2]), sub(x[0], x[2])
    t2, t3 = add(x[1], x[3]), quarter(sub(x[1], x[3]), sign)
    return [add(t0, t2), add(t1, t3), sub(t0, t2), sub(t1, t3)]


def fourier8(x, sign):
    even = fourier4(x[0::2], sign)
    odd = fourier4(x[1::2], sign)
    odd = [turn(odd[k], k, 8, sign) for k in range(4)]
    return [add(even[k], odd[k]) for k in range(4)] + [sub(even[k], odd[k]) for k in range(4)]


def fourier(x, sign):
    if len(x) == 1:
        return x
    if len(x) == 2:
        return [add(x[0], x[1]), sub(x[0], x[1])]
    return fourier4(x, sign) if len(x) == 4 else fourier8(x, sign)


def fourier64(load, store, middle, sign):
    for b in range(8):
        values = fourier8([load(8 * a + b) for a in range(8)], sign)
        for c in range(8):
            real, imag = turn(values[c], b * c, 64, sign)
            middle[c * 8 + b, 0] = real
            middle[c * 8 + b, 1] = imag
    for c in range(8):
        values = fourier8([(middle[c * 8 + b, 0], middle[c * 8 + b, 1]) for b in range(8)], sign)
        for d in range(8):
            store(c + 8 * d, values[d])


def fourier_part(load, store, middle, kept, radix):
    size = OUTER // radix
    first = size // 4
    for b in range(4):
        groups = [[] for _ in kept]
        for a in range(first):
            n = 4 * a + b
            values = fourier([load(n + size * t) for t in range(radix)], -1)
            for at, j in enumerate(kept):
                groups[at].append(turn(values[j], n * j, OUTER, -1))
        for at in range(len(kept)):
            values = fourier(groups[at], -1)
            for c in range(first):
                real, imag = turn(values[c], b * c, size, -1)
                middle[(at * first + c) * 4 + b, 0] = real
                middle[(at * first + c) * 4 + b, 1] = imag
    for at in range(len(kept)):
        for c in range(first):
            slot = (at * first + c) * 4
            values = fourier4([(middle[slot + b, 0], middle[slot + b, 1]) for b in range(4)], -1)
            for d in range(4):
                store(c + first * d, at, values[d])


def inverse_part(load, store, middle, kept, radix):
    size = OUTER // radix
    first = size // 4
    for at in range(len(kept)):
        for b in range(4):
            values = fourier([load(4 * a + b, at) for a in range(first)], 1)
            for c in range(first):
                real, imag = turn(values[c], b * c, size, 1)
                middle[(at * first + c) * 4 + b, 0] = real
                middle[(at * first + c) * 4 + b, 1] = imag
    for c in range(first):
        sums = []
        for at in range(len(kept)):
            slot = (at * first + c) * 4
            sums.append(
                fourier4([(middle[slot + b, 0], middle[slot + b, 1]) for b in range(4)], 1)
            )
        for d in range(4):
            n = c + first * d
            store(n, [turn(sums[at][d], n * j, OUTER, 1) for at, j in enumerate(kept)])


def fold(mixed):
    return mixed ^ lax.shift_right_logical(mixed, jnp.full(mixed.shape, 13, jnp.int32))


def phase_code(row_term, column_term):
    product = (row_term ^ column_term) * jnp.int32(wrap(4 * MIX_MULTIPLIER))
    code = lax.shift_right_arithmetic(product, jnp.full(product.shape, 30, jnp.int32))
    return code.astype(jnp.float32)


def rotate(value, code, direction):
    size = jnp.abs(code)
    cosine = 1 - size
    sine = code * (2 - size)
    left, right = value[0] * sine, value[1] * sine
    if direction > 0:
        return (value[0] * cosine - right, left + value[1] * cosine)
    return (value[0] * cosine + right, value[1] * cosine - left)


def row_hash(id_refs, base, mask):
    masks = len(id_refs)
    rows = lax.broadcasted_iota(jnp.int32, (TILE, INNER), 0) + base
    ahead = lax.rem(mask - lax.axis_index("mask") + masks, masks)
    mask_id = id_refs[0][0]
    for d in range(1, masks):
        mask_id = jnp.where(ahead == d, id_refs[d][0], mask_id)
    mask_term = (mask_id + 1) * jnp.int32(MASK_MULTIPLIER)
    return fold((rows * jnp.int32(ROW_MULTIPLIER)) ^ mask_term)


def column_hash(tile):
    lanes = lax.broadcasted_iota(jnp.int32, (TILE, INNER), 1)
    shift = jnp.int32(wrap(tile * INNER * COLUMN_MULTIPLIER))
    return fold(lanes * jnp.int32(COLUMN_MULTIPLIER) + shift)


def table_pair():
    inner = np.arange(INNER, dtype=np.int64)
    outer = np.arange(OUTER, dtype=np.int64)
    steps = inner[None, None, :] * (outer[:, None, None] + OUTER * inner[None, :, None]) % LENGTH
    angles = steps * (-2.0 * math.pi / LENGTH)
    cosine, sine = np.cos(angles), np.sin(angles)
    table = np.concatenate(
        [np.concatenate([cosine, -sine], axis=2), np.concatenate([sine, cosine], axis=2)], axis=1
    )
    forward = (table * 2.0**-7).astype(ml_dtypes.bfloat16)
    backward = (table.transpose(0, 2, 1) * 2.0**-6).astype(ml_dtypes.bfloat16)
    return forward, backward


def by_parity(step, last, early, both, late):
    @pl.when(step == 0)
    def _():
        early(0)

    for parity in range(2):

        @pl.when((step > 0) & (step < last) & (step % 2 == parity))
        def _():
            both(1 - parity, parity)

    @pl.when(step == last)
    def _():
        late((last - 1) % 2)


def rows_out_kernel(kept, masks, total, first, blocks, *refs):
    id_refs = refs[:masks]
    image_ref, table_hbm, out_ref, *rest = refs[masks:]
    code_ref = rest[0] if len(rest) == 7 else None
    table, middle, held_even, held_odd, column_terms, sem = rest[-6:]
    held = (held_even, held_odd)
    slots, _, _, rows, _ = out_ref.shape
    radix = OUTER // slots
    slabs = rows // TILE
    step = pl.program_id(0)
    device = lax.axis_index("rows") * masks + lax.axis_index("mask")
    copy = pltpu.make_async_copy(table_hbm.at[:, pl.ds(kept[0], len(kept))], table, sem)
    count = masks * slabs
    share = slots // count

    @pl.when(step == 0)
    def _():
        copy.start()
        for n in range(OUTER):
            column_terms[n] = column_hash(n)

    def spread(r, j, read):
        value = jnp.dot(held[read][r, j], table[r, j], preferred_element_type=jnp.float32)
        value = value.astype(jnp.bfloat16)
        for m in range(masks):
            for p in range(2):
                out_ref[r, m, p, :, j * INNER : (j + 1) * INNER] = value[
                    m * rows : (m + 1) * rows, p * INNER : (p + 1) * INNER
                ]

    def slab(index, carry, read, write):
        mask = index // slabs
        at = pl.multiple_of((index % slabs) * TILE, TILE)
        row_term = row_hash(id_refs, (device * total + first + step) * rows + at, mask)
        dots = [] if read is None else [(i, j) for i in range(share) for j in range(len(kept))]
        every = OUTER // max(len(dots), 1)
        calls = []

        def load(n):
            if dots and len(calls) % every == 0:
                i, j = dots[len(calls) // every]
                spread(index * share + i, j, read)
            calls.append(n)
            code = phase_code(row_term, column_terms[n])
            span = slice(n * INNER, (n + 1) * INNER)
            if code_ref is not None:
                code_ref[mask, pl.ds(at, TILE), span] = code.astype(jnp.bfloat16)
            value = [image_ref[p, pl.ds(at, TILE), span].astype(jnp.float32) for p in range(2)]
            return rotate(value, code, 1)

        def store(r, j, value):
            to = pl.ds(pl.multiple_of(index * TILE, TILE), TILE)
            held[write][r, j, to, 0:INNER] = value[0].astype(jnp.bfloat16)
            held[write][r, j, to, INNER:] = value[1].astype(jnp.bfloat16)

        fourier_part(load, store, middle, kept, radix)
        return carry

    def early(write):
        lax.fori_loop(0, count, functools.partial(slab, read=None, write=write), 0)
        copy.wait()

    def both(read, write):
        lax.fori_loop(0, count, functools.partial(slab, read=read, write=write), 0)

    def late(read):
        def some(index, carry):
            for i in range(share):
                for j in range(len(kept)):
                    spread(index * share + i, j, read)
            return carry

        lax.fori_loop(0, count, some, 0, unroll=2)

    by_parity(step, blocks, early, both, late)


def row_step(count, masks):
    return min(count, max(TILE, 128 // masks))


def row_scratch(slots, kept, masks, rows, buffers):
    held = pltpu.VMEM((slots, kept, masks * rows, 2 * INNER), jnp.bfloat16)
    return [
        pltpu.VMEM((slots, kept, 2 * INNER, 2 * INNER), jnp.bfloat16),
        pltpu.VMEM((slots * kept, 2, TILE, INNER), jnp.float32),
    ] + [held] * buffers


def parameters(flops):
    return {
        "compiler_params": pltpu.CompilerParams(
            vmem_limit_bytes=VMEM_LIMIT, dimension_semantics=("arbitrary",)
        ),
        "cost_estimate": pl.CostEstimate(
            flops=flops, bytes_accessed=40 << 20, transcendentals=0
        ),
    }


def rows_out(kept, ids, image, table, with_code, piece):
    masks = len(ids)
    _, total, width = image.shape
    slots = table.shape[0]
    rows = math.gcd(row_step(total, masks), *piece)
    first, count = piece[0] // rows, piece[1]
    blocks = count // rows
    span = len(kept) * INNER

    def now(i):
        return jnp.minimum(i, blocks - 1)

    def before(i):
        return jnp.maximum(i - 1, 0)

    return pl.pallas_call(
        functools.partial(rows_out_kernel, kept, masks, total // rows, first, blocks),
        grid=(blocks + 1,),
        in_specs=[pl.BlockSpec(memory_space=pltpu.SMEM)] * masks
        + [
            pl.BlockSpec((2, rows, width), lambda i: (0, first + now(i), 0)),
            pl.BlockSpec(memory_space=pl.ANY),
        ],
        out_specs=[
            pl.BlockSpec((slots, masks, 2, rows, span), lambda i: (0, 0, 0, before(i), 0)),
            pl.BlockSpec((masks, rows, width), lambda i: (0, now(i), 0)),
        ][: 1 + with_code],
        out_shape=[
            jax.ShapeDtypeStruct((slots, masks, 2, count, span), jnp.bfloat16),
            jax.ShapeDtypeStruct((masks, count, width), jnp.bfloat16),
        ][: 1 + with_code],
        scratch_shapes=row_scratch(slots, len(kept), masks, rows, 2)
        + [pltpu.VMEM((OUTER, TILE, INNER), jnp.int32), pltpu.SemaphoreType.DMA],
        name="rows_out",
        **parameters(masks * count * width * 1000),
    )(*ids, image, table)


def columns_kernel(share, ins, outs, *refs):
    in_refs = refs[: len(ins)]
    measured_ref, forward_hbm, backward_hbm = refs[len(ins) : len(ins) + 3]
    out_refs = refs[len(ins) + 3 : len(ins) + 3 + len(outs)]
    loss_ref, forward, backward, middle, held, sems = refs[len(ins) + 3 + len(outs) :]
    copies = [
        pltpu.make_async_copy(forward_hbm, forward, sems.at[0]),
        pltpu.make_async_copy(backward_hbm, backward, sems.at[1]),
    ]

    @pl.when(pl.program_id(0) == 0)
    def _():
        for copy in copies:
            copy.start()
        loss_ref[...] = jnp.zeros_like(loss_ref)

    def place(begins, n, group, size, inside):
        if share >= INNER:
            per = share // INNER
            row = (n % per) * INNER + group * size
            piece = max(i for i in range(len(begins)) if begins[i] <= row)
            at = row - begins[piece] + inside
            return piece, n // per, pl.ds(pl.multiple_of(at, TILE), TILE)
        at = group * size + inside
        span = pl.ds(pl.multiple_of(at % share, TILE), TILE)
        return 0, n * (INNER // share) + at // share, span

    def groups(begins, body):
        size = math.gcd(INNER, *begins)
        for group in range(INNER // size):
            lax.fori_loop(0, size // TILE, body(group, size), 0)

    def arrive(group, size, index, carry):
        inside = pl.multiple_of(index * TILE, TILE)

        def load(n):
            piece, source, span = place(ins, n, group, size, inside)
            return [in_refs[piece][source, p, span, :].astype(jnp.float32) for p in range(2)]

        def store(k, value):
            for p in range(2):
                to = pl.multiple_of(p * INNER + group * size + inside, TILE)
                held[k, pl.ds(to, TILE), :] = value[p].astype(jnp.bfloat16)

        fourier64(load, store, middle, -1)
        return carry

    groups(ins, lambda group, size: functools.partial(arrive, group, size))

    @pl.when(pl.program_id(0) == 0)
    def _():
        for copy in copies:
            copy.wait()

    def residual(k, carry):
        spectrum = jnp.dot(forward[k], held[k], preferred_element_type=jnp.float32)
        real, imag = spectrum[:INNER], spectrum[INNER:]
        measured = measured_ref[
            0, pl.ds(pl.multiple_of(k * INNER, INNER), INNER), :
        ].astype(jnp.float32)
        square = real * real + imag * imag + EPSILON
        inverse = lax.rsqrt(square)
        misfit = square * inverse - measured
        kept = 1.0 - measured * inverse
        loss_ref[...] += jnp.sum((misfit * misfit).reshape(INNER // 8, 8, INNER), axis=0)
        weighted = jnp.concatenate([real * kept, imag * kept], axis=0).astype(jnp.bfloat16)
        back = jnp.dot(backward[k], weighted, preferred_element_type=jnp.float32)
        held[k] = back.astype(jnp.bfloat16)
        return carry

    lax.fori_loop(0, OUTER, residual, 0, unroll=2)

    def leave(group, size, index, carry):
        inside = pl.multiple_of(index * TILE, TILE)

        def load(k):
            at = [pl.multiple_of(p * INNER + group * size + inside, TILE) for p in range(2)]
            return [held[k, pl.ds(at[p], TILE), :].astype(jnp.float32) for p in range(2)]

        def store(n, value):
            piece, source, span = place(outs, n, group, size, inside)
            for p in range(2):
                out_refs[piece][source, p, span, :] = value[p].astype(jnp.bfloat16)

        fourier64(load, store, middle, 1)
        return carry

    groups(outs, lambda group, size: functools.partial(leave, group, size))


def columns(chunk, arrived, pieces, measured, forward, backward):
    devices, _, _, width = arrived[0].shape
    share = sum(blocks.shape[2] for blocks in arrived)
    length = devices * share
    steps = width // INNER
    begins = [0]
    for blocks in arrived[:-1]:
        begins.append(begins[-1] + blocks.shape[2])

    def some_rows(count):
        return pl.BlockSpec((devices, 2, count, INNER), lambda i: (0, 0, 0, i))

    *leaving, loss = pl.pallas_call(
        functools.partial(columns_kernel, share, begins, [first for first, _ in pieces]),
        grid=(steps,),
        in_specs=[some_rows(blocks.shape[2]) for blocks in arrived]
        + [
            pl.BlockSpec((1, length, INNER), lambda i: (0, 0, chunk * steps + i)),
            pl.BlockSpec(memory_space=pl.ANY),
            pl.BlockSpec(memory_space=pl.ANY),
        ],
        out_specs=[some_rows(count) for _, count in pieces]
        + [pl.BlockSpec((8, INNER), lambda i: (0, 0))],
        out_shape=[
            jax.ShapeDtypeStruct((devices, 2, count, width), jnp.bfloat16) for _, count in pieces
        ]
        + [jax.ShapeDtypeStruct((8, INNER), jnp.float32)],
        scratch_shapes=[
            pltpu.VMEM((OUTER, 2 * INNER, 2 * INNER), jnp.bfloat16),
            pltpu.VMEM((OUTER, 2 * INNER, 2 * INNER), jnp.bfloat16),
            pltpu.VMEM((OUTER, 2, TILE, INNER), jnp.float32),
            pltpu.VMEM((OUTER, 2 * INNER, INNER), jnp.bfloat16),
            pltpu.SemaphoreType.DMA((2,)),
        ],
        name="columns",
        **parameters(length * width * 2200),
    )(*arrived, measured, forward, backward)
    return leaving, loss


def gather_one(r, j, in_ref, table, held):
    masks = in_ref.shape[1]
    span = slice(j * INNER, (j + 1) * INNER)
    value = jnp.concatenate(
        [
            jnp.concatenate([in_ref[r, m, p, :, span] for p in range(2)], axis=1)
            for m in range(masks)
        ],
        axis=0,
    )
    held[r, j] = jnp.dot(value, table[r, j], preferred_element_type=jnp.float32).astype(
        jnp.bfloat16
    )


def gather_all(kept, in_ref, table, held):
    def some(r, carry):
        for j in range(len(kept)):
            gather_one(r, j, in_ref, table, held)
        return carry

    lax.fori_loop(0, in_ref.shape[0], some, 0, unroll=4)


def fetch_table(kept, table_hbm, table, sem):
    copy = pltpu.make_async_copy(table_hbm.at[:, pl.ds(kept[0], len(kept))], table, sem)

    @pl.when(pl.program_id(0) == 0)
    def _():
        copy.start()
        copy.wait()


def held_tile(held, r, j, index):
    take = pl.ds(pl.multiple_of(index * TILE, TILE), TILE)
    return [
        held[r, j, take, p * INNER : (p + 1) * INNER].astype(jnp.float32) for p in range(2)
    ]


def rows_part_kernel(kept, in_ref, table_hbm, out_ref, table, middle, held, sem):
    slots, masks, _, rows, _ = in_ref.shape
    slabs = rows // TILE
    fetch_table(kept, table_hbm, table, sem)
    gather_all(kept, in_ref, table, held)

    def slab(index, carry):
        mask = index // slabs
        at = pl.multiple_of((index % slabs) * TILE, TILE)

        def load(r, j):
            return held_tile(held, r, j, index)

        def store(n, values):
            for j, value in enumerate(values):
                for p in range(2):
                    out_ref[n, j, mask, p, pl.ds(at, TILE), :] = value[p].astype(jnp.bfloat16)

        inverse_part(load, store, middle, kept, OUTER // slots)
        return carry

    lax.fori_loop(0, masks * slabs, slab, 0)


def rows_part(kept, arrived, table):
    slots, masks, _, count, span = arrived.shape
    rows = row_step(count, masks)
    return pl.pallas_call(
        functools.partial(rows_part_kernel, kept),
        grid=(count // rows,),
        in_specs=[
            pl.BlockSpec((slots, masks, 2, rows, span), lambda i: (0, 0, 0, i, 0)),
            pl.BlockSpec(memory_space=pl.ANY),
        ],
        out_specs=pl.BlockSpec(
            (slots, len(kept), masks, 2, rows, INNER), lambda i: (0, 0, 0, 0, i, 0)
        ),
        out_shape=jax.ShapeDtypeStruct(
            (slots, len(kept), masks, 2, count, INNER), jnp.bfloat16
        ),
        scratch_shapes=row_scratch(slots, len(kept), masks, rows, 1)
        + [pltpu.SemaphoreType.DMA],
        name="rows_part",
        **parameters(masks * count * LENGTH * 600),
    )(arrived, table)


def rows_in_kernel(kept, blocks, code_ref, in_ref, part_ref, table_hbm, *rest):
    out_ref, table, middle, held_even, held_odd, sem = rest[-6:]
    held = (held_even, held_odd)
    slots, masks, _, rows, _ = in_ref.shape
    radix = OUTER // slots
    slabs = rows // TILE
    count = masks * slabs
    share = slots // count
    fetch_table(kept, table_hbm, table, sem)

    def slab(index, carry, first, read, write):
        mask = index // slabs
        at = pl.multiple_of((index % slabs) * TILE, TILE)
        dots = [] if write is None else [(i, j) for i in range(share) for j in range(len(kept))]
        every = slots * len(kept) // max(len(dots), 1)
        calls = []

        def load(r, j):
            if dots and len(calls) % every == 0:
                i, k = dots[len(calls) // every]
                gather_one(index * share + i, k, in_ref, table, held[write])
            calls.append(r)
            return held_tile(held[read], r, j, index)

        def store(n, values):
            early = [
                [part_ref[n, j, mask, p, pl.ds(at, TILE), :].astype(jnp.float32) for p in range(2)]
                for j in range(radix - len(kept))
            ]
            for t, value in enumerate(fourier(early + values, 1)):
                tile = n + slots * t
                span = slice(tile * INNER, (tile + 1) * INNER)
                code = code_ref[mask, pl.ds(at, TILE), span].astype(jnp.float32)
                value = rotate(value, code, -1)
                for p in range(2):
                    if first:
                        out_ref[p, pl.ds(at, TILE), span] = value[p]
                    else:
                        out_ref[p, pl.ds(at, TILE), span] += value[p]

        inverse_part(load, store, middle, kept, radix)
        return carry

    def early(write):
        gather_all(kept, in_ref, table, held[write])

    def both(read, write):
        pair = {"read": read, "write": write}
        lax.fori_loop(0, slabs, functools.partial(slab, first=True, **pair), 0)
        lax.fori_loop(slabs, count, functools.partial(slab, first=False, **pair), 0)

    def late(read):
        both(read, None)

    by_parity(pl.program_id(0), blocks, early, both, late)


def rows_in(kept, code, arrived, part, table, piece, filled):
    slots, masks, _, count, span = arrived.shape
    total = code.shape[1]
    rows = math.gcd(row_step(total, masks), *piece)
    first, blocks = piece[0] // rows, count // rows

    def now(i):
        return jnp.minimum(i, blocks - 1)

    def before(i):
        return jnp.maximum(i - 1, 0)

    return pl.pallas_call(
        functools.partial(rows_in_kernel, kept, blocks),
        grid=(blocks + 1,),
        in_specs=[
            pl.BlockSpec((masks, rows, LENGTH), lambda i: (0, first + before(i), 0)),
            pl.BlockSpec((slots, masks, 2, rows, span), lambda i: (0, 0, 0, now(i), 0)),
            pl.BlockSpec(
                (slots,) + part.shape[1:4] + (rows, INNER),
                lambda i: (0, 0, 0, 0, first + before(i), 0),
            ),
            pl.BlockSpec(memory_space=pl.ANY),
        ]
        + [pl.BlockSpec(memory_space=pl.ANY)] * len(filled),
        out_specs=pl.BlockSpec((2, rows, LENGTH), lambda i: (0, first + before(i), 0)),
        out_shape=jax.ShapeDtypeStruct((2, total, LENGTH), jnp.float32),
        input_output_aliases={4: 0} if filled else {},
        scratch_shapes=row_scratch(slots, len(kept), masks, rows, 2)
        + [pltpu.SemaphoreType.DMA],
        name="rows_in",
        **parameters(masks * count * LENGTH * 1000),
    )(code, arrived, part, table, *filled)


AXES = ("rows", "mask")
CHUNKS = 2


def exchange(blocks):
    flat = blocks.reshape((-1,) + blocks.shape[-3:])
    flat = lax.all_to_all(flat, AXES, split_axis=0, concat_axis=0, tiled=True)
    return flat.reshape(blocks.shape)


def add_over(value, devices, factor, stride):
    total = value
    for d in range(1, factor):
        pairs = []
        for i in range(devices):
            digit = i // stride % factor
            pairs.append((i, i + ((digit + d) % factor - digit) * stride))
        total = total + lax.ppermute(value, AXES, pairs)
    return total


def shards(slots, masks, image, measured, mask_ids):
    forward, backward = (jnp.asarray(table) for table in table_pair())
    _, count, width = image.shape
    devices = slots * masks
    radix = OUTER // slots
    each = radix // CHUNKS
    kept = [tuple(range(c * each, (c + 1) * each)) for c in range(CHUNKS)]
    by_slot = (slots, radix, 2 * INNER, 2 * INNER)
    out_table, in_table = backward.reshape(by_slot), forward.reshape(by_slot)
    ids = [mask_ids] + [
        lax.ppermute(mask_ids, "mask", [((m + d) % masks, m) for m in range(masks)])
        for d in range(1, masks)
    ]
    whole = [(0, count)]
    head, tail = whole, whole
    if count >= 2 * INNER:
        small = 2 * TILE
        head = [(0, small), (small, count - small)]
        tail = [(0, count - small), (count - small, small)]

    def forth(c, pieces, image, with_code):
        arrived = []
        for piece in pieces:
            sent, *code = rows_out(kept[c], ids, image, out_table, with_code, piece)
            sent, image = lax.optimization_barrier((sent, image))
            if arrived:
                sent, arrived[-1] = lax.optimization_barrier((sent, arrived[-1]))
            arrived.append(exchange(sent.reshape((-1,) + sent.shape[2:])))
        return arrived, code, image

    def back(blocks):
        arrived = exchange(blocks)
        return arrived.reshape((slots, masks) + blocks.shape[1:])

    arrived, _, image = forth(0, head, image, False)
    (leaving,), loss_early = columns(0, arrived, whole, measured, forward, backward)
    arrived, (code,), image = forth(1, whole, image, True)
    leaving_last, loss_late = columns(1, arrived, tail, measured, forward, backward)
    first = 1 << (3 * devices.bit_length() // 5)
    loss = (jnp.sum(loss_early) + jnp.sum(loss_late)).reshape(1)
    loss = add_over(loss, devices, first, 1)
    returned, leaving_last, loss = lax.optimization_barrier((back(leaving), leaving_last, loss))
    part = rows_part(kept[0], returned, in_table)
    last = ()
    filled = ()
    for piece, blocks in zip(tail, leaving_last):
        if piece != tail[0]:
            blocks, last, part = lax.optimization_barrier((blocks, last, part))
        last = back(blocks)
        filled = (rows_in(kept[1], code, last, part, in_table, piece, filled),)
        if piece == tail[0]:
            filled, loss = lax.optimization_barrier((filled, loss))
            loss = add_over(loss, devices, devices // first, first)
    return filled[0], loss[0] / (masks * width * width)


def solution(mesh):
    slots, masks = mesh.shape["rows"], mesh.shape["mask"]
    return jax.shard_map(
        functools.partial(shards, slots, masks),
        mesh=mesh,
        in_specs=(P(None, AXES, None), P("mask", None, "rows"), P("mask")),
        out_specs=(P(None, AXES, None), P()),
        check_vma=False,
    )
```

```python
import functools
import math

import jax
import jax.numpy as jnp
import ml_dtypes
import numpy as np
from jax import lax
from jax.experimental import pallas as pl
from jax.experimental.pallas import tpu as pltpu
from jax.sharding import PartitionSpec as P

INNER = 128
OUTER = 64
LENGTH = INNER * OUTER
EPSILON = 0.25
TILE = 16
VMEM_LIMIT = 58 * 1024 * 1024
ROOT_HALF = math.sqrt(0.5)

ROW_MULTIPLIER = 73856093
COLUMN_MULTIPLIER = 19349663
MASK_MULTIPLIER = 83492791
MIX_MULTIPLIER = 1274126177


def wrap(value):
    return (value + 2**31) % 2**32 - 2**31


def add(a, b):
    return (a[0] + b[0], a[1] + b[1])


def sub(a, b):
    return (a[0] - b[0], a[1] - b[1])


def quarter(a, sign):
    return (-a[1], a[0]) if sign > 0 else (a[1], -a[0])


def turn(a, step, count, sign):
    step = step % count
    if step == 0:
        return a
    if 4 * step == count:
        return quarter(a, sign)
    if 2 * step == count:
        return (-a[0], -a[1])
    if 4 * step == 3 * count:
        return quarter(a, -sign)
    if 8 * step == count:
        q = quarter(a, sign)
        return ((a[0] + q[0]) * ROOT_HALF, (a[1] + q[1]) * ROOT_HALF)
    if 8 * step == 3 * count:
        q = quarter(a, sign)
        return ((q[0] - a[0]) * ROOT_HALF, (q[1] - a[1]) * ROOT_HALF)
    angle = sign * 2.0 * math.pi * step / count
    cosine, sine = math.cos(angle), math.sin(angle)
    return (a[0] * cosine - a[1] * sine, a[0] * sine + a[1] * cosine)


def fourier4(x, sign):
    t0, t1 = add(x[0], x[2]), sub(x[0], x[2])
    t2, t3 = add(x[1], x[3]), quarter(sub(x[1], x[3]), sign)
    return [add(t0, t2), add(t1, t3), sub(t0, t2), sub(t1, t3)]


def fourier8(x, sign):
    even = fourier4(x[0::2], sign)
    odd = fourier4(x[1::2], sign)
    odd = [turn(odd[k], k, 8, sign) for k in range(4)]
    return [add(even[k], odd[k]) for k in range(4)] + [sub(even[k], odd[k]) for k in range(4)]


def fourier(x, sign):
    if len(x) == 1:
        return x
    if len(x) == 2:
        return [add(x[0], x[1]), sub(x[0], x[1])]
    return fourier4(x, sign) if len(x) == 4 else fourier8(x, sign)


def fourier64(load, store, middle, sign):
    for b in range(8):
        values = fourier8([load(8 * a + b) for a in range(8)], sign)
        for c in range(8):
            real, imag = turn(values[c], b * c, 64, sign)
            middle[c * 8 + b, 0] = real
            middle[c * 8 + b, 1] = imag
    for c in range(8):
        values = fourier8([(middle[c * 8 + b, 0], middle[c * 8 + b, 1]) for b in range(8)], sign)
        for d in range(8):
            store(c + 8 * d, values[d])


def fourier_part(load, store, middle, kept, radix):
    size = OUTER // radix
    first = size // 4
    for b in range(4):
        groups = [[] for _ in kept]
        for a in range(first):
            n = 4 * a + b
            values = fourier([load(n + size * t) for t in range(radix)], -1)
            for at, j in enumerate(kept):
                groups[at].append(turn(values[j], n * j, OUTER, -1))
        for at in range(len(kept)):
            values = fourier(groups[at], -1)
            for c in range(first):
                real, imag = turn(values[c], b * c, size, -1)
                middle[(at * first + c) * 4 + b, 0] = real
                middle[(at * first + c) * 4 + b, 1] = imag
    for at in range(len(kept)):
        for c in range(first):
            slot = (at * first + c) * 4
            values = fourier4([(middle[slot + b, 0], middle[slot + b, 1]) for b in range(4)], -1)
            for d in range(4):
                store(c + first * d, at, values[d])


def inverse_part(load, store, middle, kept, radix):
    size = OUTER // radix
    first = size // 4
    for at in range(len(kept)):
        for b in range(4):
            values = fourier([load(4 * a + b, at) for a in range(first)], 1)
            for c in range(first):
                real, imag = turn(values[c], b * c, size, 1)
                middle[(at * first + c) * 4 + b, 0] = real
                middle[(at * first + c) * 4 + b, 1] = imag
    for c in range(first):
        sums = []
        for at in range(len(kept)):
            slot = (at * first + c) * 4
            sums.append(
                fourier4([(middle[slot + b, 0], middle[slot + b, 1]) for b in range(4)], 1)
            )
        for d in range(4):
            n = c + first * d
            store(n, [turn(sums[at][d], n * j, OUTER, 1) for at, j in enumerate(kept)])


def fold(mixed):
    return mixed ^ lax.shift_right_logical(mixed, jnp.full(mixed.shape, 13, jnp.int32))


def phase_code(row_term, column_term):
    product = (row_term ^ column_term) * jnp.int32(wrap(4 * MIX_MULTIPLIER))
    code = lax.shift_right_arithmetic(product, jnp.full(product.shape, 30, jnp.int32))
    return code.astype(jnp.float32)


def rotate(value, code, direction):
    size = jnp.abs(code)
    cosine = 1 - size
    sine = code * (2 - size)
    left, right = value[0] * sine, value[1] * sine
    if direction > 0:
        return (value[0] * cosine - right, left + value[1] * cosine)
    return (value[0] * cosine + right, value[1] * cosine - left)


def row_hash(id_refs, base, mask):
    masks = len(id_refs)
    rows = lax.broadcasted_iota(jnp.int32, (TILE, INNER), 0) + base
    ahead = lax.rem(mask - lax.axis_index("mask") + masks, masks)
    mask_id = id_refs[0][0]
    for d in range(1, masks):
        mask_id = jnp.where(ahead == d, id_refs[d][0], mask_id)
    mask_term = (mask_id + 1) * jnp.int32(MASK_MULTIPLIER)
    return fold((rows * jnp.int32(ROW_MULTIPLIER)) ^ mask_term)


def column_hash(tile):
    lanes = lax.broadcasted_iota(jnp.int32, (TILE, INNER), 1)
    shift = jnp.int32(wrap(tile * INNER * COLUMN_MULTIPLIER))
    return fold(lanes * jnp.int32(COLUMN_MULTIPLIER) + shift)


def table_pair():
    inner = np.arange(INNER, dtype=np.int64)
    outer = np.arange(OUTER, dtype=np.int64)
    steps = inner[None, None, :] * (outer[:, None, None] + OUTER * inner[None, :, None]) % LENGTH
    angles = steps * (-2.0 * math.pi / LENGTH)
    cosine, sine = np.cos(angles), np.sin(angles)
    table = np.concatenate(
        [np.concatenate([cosine, -sine], axis=2), np.concatenate([sine, cosine], axis=2)], axis=1
    )
    forward = (table * 2.0**-7).astype(ml_dtypes.bfloat16)
    backward = (table.transpose(0, 2, 1) * 2.0**-6).astype(ml_dtypes.bfloat16)
    return forward, backward


def by_parity(step, last, early, both, late):
    @pl.when(step == 0)
    def _():
        early(0)

    for parity in range(2):

        @pl.when((step > 0) & (step < last) & (step % 2 == parity))
        def _():
            both(1 - parity, parity)

    @pl.when(step == last)
    def _():
        late((last - 1) % 2)


def rows_out_kernel(kept, masks, total, first, blocks, *refs):
    id_refs = refs[:masks]
    image_ref, table_hbm, out_ref, *rest = refs[masks:]
    code_ref = rest[0] if len(rest) == 7 else None
    table, middle, held_even, held_odd, column_terms, sem = rest[-6:]
    held = (held_even, held_odd)
    slots, _, _, rows, _ = out_ref.shape
    radix = OUTER // slots
    slabs = rows // TILE
    step = pl.program_id(0)
    device = lax.axis_index("rows") * masks + lax.axis_index("mask")
    copy = pltpu.make_async_copy(table_hbm.at[:, pl.ds(kept[0], len(kept))], table, sem)
    count = masks * slabs
    share = slots // count

    @pl.when(step == 0)
    def _():
        copy.start()
        for n in range(OUTER):
            column_terms[n] = column_hash(n)

    def spread(r, j, read):
        value = jnp.dot(held[read][r, j], table[r, j], preferred_element_type=jnp.float32)
        value = value.astype(jnp.bfloat16)
        for m in range(masks):
            for p in range(2):
                out_ref[r, m, p, :, j * INNER : (j + 1) * INNER] = value[
                    m * rows : (m + 1) * rows, p * INNER : (p + 1) * INNER
                ]

    def slab(index, carry, read, write):
        mask = index // slabs
        at = pl.multiple_of((index % slabs) * TILE, TILE)
        row_term = row_hash(id_refs, (device * total + first + step) * rows + at, mask)
        dots = [] if read is None else [(i, j) for i in range(share) for j in range(len(kept))]
        every = OUTER // max(len(dots), 1)
        calls = []

        def load(n):
            if dots and len(calls) % every == 0:
                i, j = dots[len(calls) // every]
                spread(index * share + i, j, read)
            calls.append(n)
            code = phase_code(row_term, column_terms[n])
            span = slice(n * INNER, (n + 1) * INNER)
            if code_ref is not None:
                code_ref[mask, pl.ds(at, TILE), span] = code.astype(jnp.bfloat16)
            value = [image_ref[p, pl.ds(at, TILE), span].astype(jnp.float32) for p in range(2)]
            return rotate(value, code, 1)

        def store(r, j, value):
            to = pl.ds(pl.multiple_of(index * TILE, TILE), TILE)
            held[write][r, j, to, 0:INNER] = value[0].astype(jnp.bfloat16)
            held[write][r, j, to, INNER:] = value[1].astype(jnp.bfloat16)

        fourier_part(load, store, middle, kept, radix)
        return carry

    def early(write):
        lax.fori_loop(0, count, functools.partial(slab, read=None, write=write), 0)
        copy.wait()

    def both(read, write):
        lax.fori_loop(0, count, functools.partial(slab, read=read, write=write), 0)

    def late(read):
        def some(index, carry):
            for i in range(share):
                for j in range(len(kept)):
                    spread(index * share + i, j, read)
            return carry

        lax.fori_loop(0, count, some, 0, unroll=2)

    by_parity(step, blocks, early, both, late)


def row_step(count, masks):
    return min(count, max(TILE, 128 // masks))


def row_scratch(slots, kept, masks, rows, buffers):
    held = pltpu.VMEM((slots, kept, masks * rows, 2 * INNER), jnp.bfloat16)
    return [
        pltpu.VMEM((slots, kept, 2 * INNER, 2 * INNER), jnp.bfloat16),
        pltpu.VMEM((slots * kept, 2, TILE, INNER), jnp.float32),
    ] + [held] * buffers


def parameters(flops):
    return {
        "compiler_params": pltpu.CompilerParams(
            vmem_limit_bytes=VMEM_LIMIT, dimension_semantics=("arbitrary",)
        ),
        "cost_estimate": pl.CostEstimate(
            flops=flops, bytes_accessed=40 << 20, transcendentals=0
        ),
    }


def rows_out(kept, ids, image, table, with_code, piece):
    masks = len(ids)
    _, total, width = image.shape
    slots = table.shape[0]
    rows = math.gcd(row_step(total, masks), *piece)
    first, count = piece[0] // rows, piece[1]
    blocks = count // rows
    span = len(kept) * INNER

    def now(i):
        return jnp.minimum(i, blocks - 1)

    def before(i):
        return jnp.maximum(i - 1, 0)

    return pl.pallas_call(
        functools.partial(rows_out_kernel, kept, masks, total // rows, first, blocks),
        grid=(blocks + 1,),
        in_specs=[pl.BlockSpec(memory_space=pltpu.SMEM)] * masks
        + [
            pl.BlockSpec((2, rows, width), lambda i: (0, first + now(i), 0)),
            pl.BlockSpec(memory_space=pl.ANY),
        ],
        out_specs=[
            pl.BlockSpec((slots, masks, 2, rows, span), lambda i: (0, 0, 0, before(i), 0)),
            pl.BlockSpec((masks, rows, width), lambda i: (0, now(i), 0)),
        ][: 1 + with_code],
        out_shape=[
            jax.ShapeDtypeStruct((slots, masks, 2, count, span), jnp.bfloat16),
            jax.ShapeDtypeStruct((masks, count, width), jnp.bfloat16),
        ][: 1 + with_code],
        scratch_shapes=row_scratch(slots, len(kept), masks, rows, 2)
        + [pltpu.VMEM((OUTER, TILE, INNER), jnp.int32), pltpu.SemaphoreType.DMA],
        name="rows_out",
        **parameters(masks * count * width * 1000),
    )(*ids, image, table)


def columns_kernel(share, ins, outs, *refs):
    in_refs = refs[: len(ins)]
    measured_ref, forward_hbm, backward_hbm = refs[len(ins) : len(ins) + 3]
    out_refs = refs[len(ins) + 3 : len(ins) + 3 + len(outs)]
    loss_ref, forward, backward, middle, held, sems = refs[len(ins) + 3 + len(outs) :]
    copies = [
        pltpu.make_async_copy(forward_hbm, forward, sems.at[0]),
        pltpu.make_async_copy(backward_hbm, backward, sems.at[1]),
    ]

    @pl.when(pl.program_id(0) == 0)
    def _():
        for copy in copies:
            copy.start()
        loss_ref[...] = jnp.zeros_like(loss_ref)

    def place(begins, n, group, size, inside):
        if share >= INNER:
            per = share // INNER
            row = (n % per) * INNER + group * size
            piece = max(i for i in range(len(begins)) if begins[i] <= row)
            at = row - begins[piece] + inside
            return piece, n // per, pl.ds(pl.multiple_of(at, TILE), TILE)
        at = group * size + inside
        span = pl.ds(pl.multiple_of(at % share, TILE), TILE)
        return 0, n * (INNER // share) + at // share, span

    def groups(begins, body):
        size = math.gcd(INNER, *begins)
        for group in range(INNER // size):
            lax.fori_loop(0, size // TILE, body(group, size), 0)

    def arrive(group, size, index, carry):
        inside = pl.multiple_of(index * TILE, TILE)

        def load(n):
            piece, source, span = place(ins, n, group, size, inside)
            return [in_refs[piece][source, p, span, :].astype(jnp.float32) for p in range(2)]

        def store(k, value):
            for p in range(2):
                to = pl.multiple_of(p * INNER + group * size + inside, TILE)
                held[k, pl.ds(to, TILE), :] = value[p].astype(jnp.bfloat16)

        fourier64(load, store, middle, -1)
        return carry

    groups(ins, lambda group, size: functools.partial(arrive, group, size))

    @pl.when(pl.program_id(0) == 0)
    def _():
        for copy in copies:
            copy.wait()

    def residual(k, carry):
        spectrum = jnp.dot(forward[k], held[k], preferred_element_type=jnp.float32)
        real, imag = spectrum[:INNER], spectrum[INNER:]
        measured = measured_ref[
            0, pl.ds(pl.multiple_of(k * INNER, INNER), INNER), :
        ].astype(jnp.float32)
        square = real * real + imag * imag + EPSILON
        inverse = lax.rsqrt(square)
        misfit = square * inverse - measured
        kept = 1.0 - measured * inverse
        loss_ref[...] += jnp.sum((misfit * misfit).reshape(INNER // 8, 8, INNER), axis=0)
        weighted = jnp.concatenate([real * kept, imag * kept], axis=0).astype(jnp.bfloat16)
        back = jnp.dot(backward[k], weighted, preferred_element_type=jnp.float32)
        held[k] = back.astype(jnp.bfloat16)
        return carry

    lax.fori_loop(0, OUTER, residual, 0, unroll=2)

    def leave(group, size, index, carry):
        inside = pl.multiple_of(index * TILE, TILE)

        def load(k):
            at = [pl.multiple_of(p * INNER + group * size + inside, TILE) for p in range(2)]
            return [held[k, pl.ds(at[p], TILE), :].astype(jnp.float32) for p in range(2)]

        def store(n, value):
            piece, source, span = place(outs, n, group, size, inside)
            for p in range(2):
                out_refs[piece][source, p, span, :] = value[p].astype(jnp.bfloat16)

        fourier64(load, store, middle, 1)
        return carry

    groups(outs, lambda group, size: functools.partial(leave, group, size))


def columns(chunk, arrived, pieces, measured, forward, backward):
    devices, _, _, width = arrived[0].shape
    share = sum(blocks.shape[2] for blocks in arrived)
    length = devices * share
    steps = width // INNER
    begins = [0]
    for blocks in arrived[:-1]:
        begins.append(begins[-1] + blocks.shape[2])

    def some_rows(count):
        return pl.BlockSpec((devices, 2, count, INNER), lambda i: (0, 0, 0, i))

    *leaving, loss = pl.pallas_call(
        functools.partial(columns_kernel, share, begins, [first for first, _ in pieces]),
        grid=(steps,),
        in_specs=[some_rows(blocks.shape[2]) for blocks in arrived]
        + [
            pl.BlockSpec((1, length, INNER), lambda i: (0, 0, chunk * steps + i)),
            pl.BlockSpec(memory_space=pl.ANY),
            pl.BlockSpec(memory_space=pl.ANY),
        ],
        out_specs=[some_rows(count) for _, count in pieces]
        + [pl.BlockSpec((8, INNER), lambda i: (0, 0))],
        out_shape=[
            jax.ShapeDtypeStruct((devices, 2, count, width), jnp.bfloat16) for _, count in pieces
        ]
        + [jax.ShapeDtypeStruct((8, INNER), jnp.float32)],
        scratch_shapes=[
            pltpu.VMEM((OUTER, 2 * INNER, 2 * INNER), jnp.bfloat16),
            pltpu.VMEM((OUTER, 2 * INNER, 2 * INNER), jnp.bfloat16),
            pltpu.VMEM((OUTER, 2, TILE, INNER), jnp.float32),
            pltpu.VMEM((OUTER, 2 * INNER, INNER), jnp.bfloat16),
            pltpu.SemaphoreType.DMA((2,)),
        ],
        name="columns",
        **parameters(length * width * 2200),
    )(*arrived, measured, forward, backward)
    return leaving, loss


def gather_one(r, j, in_ref, table, held):
    masks = in_ref.shape[1]
    span = slice(j * INNER, (j + 1) * INNER)
    value = jnp.concatenate(
        [
            jnp.concatenate([in_ref[r, m, p, :, span] for p in range(2)], axis=1)
            for m in range(masks)
        ],
        axis=0,
    )
    held[r, j] = jnp.dot(value, table[r, j], preferred_element_type=jnp.float32).astype(
        jnp.bfloat16
    )


def gather_all(kept, in_ref, table, held):
    def some(r, carry):
        for j in range(len(kept)):
            gather_one(r, j, in_ref, table, held)
        return carry

    lax.fori_loop(0, in_ref.shape[0], some, 0, unroll=4)


def fetch_table(kept, table_hbm, table, sem):
    copy = pltpu.make_async_copy(table_hbm.at[:, pl.ds(kept[0], len(kept))], table, sem)

    @pl.when(pl.program_id(0) == 0)
    def _():
        copy.start()
        copy.wait()


def held_tile(held, r, j, index):
    take = pl.ds(pl.multiple_of(index * TILE, TILE), TILE)
    return [
        held[r, j, take, p * INNER : (p + 1) * INNER].astype(jnp.float32) for p in range(2)
    ]


def rows_part_kernel(kept, in_ref, table_hbm, out_ref, table, middle, held, sem):
    slots, masks, _, rows, _ = in_ref.shape
    slabs = rows // TILE
    fetch_table(kept, table_hbm, table, sem)
    gather_all(kept, in_ref, table, held)

    def slab(index, carry):
        mask = index // slabs
        at = pl.multiple_of((index % slabs) * TILE, TILE)

        def load(r, j):
            return held_tile(held, r, j, index)

        def store(n, values):
            for j, value in enumerate(values):
                for p in range(2):
                    out_ref[n, j, mask, p, pl.ds(at, TILE), :] = value[p].astype(jnp.bfloat16)

        inverse_part(load, store, middle, kept, OUTER // slots)
        return carry

    lax.fori_loop(0, masks * slabs, slab, 0)


def rows_part(kept, arrived, table):
    slots, masks, _, count, span = arrived.shape
    rows = row_step(count, masks)
    return pl.pallas_call(
        functools.partial(rows_part_kernel, kept),
        grid=(count // rows,),
        in_specs=[
            pl.BlockSpec((slots, masks, 2, rows, span), lambda i: (0, 0, 0, i, 0)),
            pl.BlockSpec(memory_space=pl.ANY),
        ],
        out_specs=pl.BlockSpec(
            (slots, len(kept), masks, 2, rows, INNER), lambda i: (0, 0, 0, 0, i, 0)
        ),
        out_shape=jax.ShapeDtypeStruct(
            (slots, len(kept), masks, 2, count, INNER), jnp.bfloat16
        ),
        scratch_shapes=row_scratch(slots, len(kept), masks, rows, 1)
        + [pltpu.SemaphoreType.DMA],
        name="rows_part",
        **parameters(masks * count * LENGTH * 600),
    )(arrived, table)


def rows_in_kernel(kept, blocks, code_ref, in_ref, part_ref, table_hbm, *rest):
    out_ref, table, middle, held_even, held_odd, sem = rest[-6:]
    held = (held_even, held_odd)
    slots, masks, _, rows, _ = in_ref.shape
    radix = OUTER // slots
    slabs = rows // TILE
    count = masks * slabs
    share = slots // count
    fetch_table(kept, table_hbm, table, sem)

    def slab(index, carry, first, read, write):
        mask = index // slabs
        at = pl.multiple_of((index % slabs) * TILE, TILE)
        dots = [] if write is None else [(i, j) for i in range(share) for j in range(len(kept))]
        every = slots * len(kept) // max(len(dots), 1)
        calls = []

        def load(r, j):
            if dots and len(calls) % every == 0:
                i, k = dots[len(calls) // every]
                gather_one(index * share + i, k, in_ref, table, held[write])
            calls.append(r)
            return held_tile(held[read], r, j, index)

        def store(n, values):
            early = [
                [part_ref[n, j, mask, p, pl.ds(at, TILE), :].astype(jnp.float32) for p in range(2)]
                for j in range(radix - len(kept))
            ]
            for t, value in enumerate(fourier(early + values, 1)):
                tile = n + slots * t
                span = slice(tile * INNER, (tile + 1) * INNER)
                code = code_ref[mask, pl.ds(at, TILE), span].astype(jnp.float32)
                value = rotate(value, code, -1)
                for p in range(2):
                    if first:
                        out_ref[p, pl.ds(at, TILE), span] = value[p]
                    else:
                        out_ref[p, pl.ds(at, TILE), span] += value[p]

        inverse_part(load, store, middle, kept, radix)
        return carry

    def early(write):
        gather_all(kept, in_ref, table, held[write])

    def both(read, write):
        pair = {"read": read, "write": write}
        lax.fori_loop(0, slabs, functools.partial(slab, first=True, **pair), 0)
        lax.fori_loop(slabs, count, functools.partial(slab, first=False, **pair), 0)

    def late(read):
        both(read, None)

    by_parity(pl.program_id(0), blocks, early, both, late)


def rows_in(kept, code, arrived, part, table, piece, filled):
    slots, masks, _, count, span = arrived.shape
    total = code.shape[1]
    rows = math.gcd(row_step(total, masks), *piece)
    first, blocks = piece[0] // rows, count // rows

    def now(i):
        return jnp.minimum(i, blocks - 1)

    def before(i):
        return jnp.maximum(i - 1, 0)

    return pl.pallas_call(
        functools.partial(rows_in_kernel, kept, blocks),
        grid=(blocks + 1,),
        in_specs=[
            pl.BlockSpec((masks, rows, LENGTH), lambda i: (0, first + before(i), 0)),
            pl.BlockSpec((slots, masks, 2, rows, span), lambda i: (0, 0, 0, now(i), 0)),
            pl.BlockSpec(
                (slots,) + part.shape[1:4] + (rows, INNER),
                lambda i: (0, 0, 0, 0, first + before(i), 0),
            ),
            pl.BlockSpec(memory_space=pl.ANY),
        ]
        + [pl.BlockSpec(memory_space=pl.ANY)] * len(filled),
        out_specs=pl.BlockSpec((2, rows, LENGTH), lambda i: (0, first + before(i), 0)),
        out_shape=jax.ShapeDtypeStruct((2, total, LENGTH), jnp.float32),
        input_output_aliases={4: 0} if filled else {},
        scratch_shapes=row_scratch(slots, len(kept), masks, rows, 2)
        + [pltpu.SemaphoreType.DMA],
        name="rows_in",
        **parameters(masks * count * LENGTH * 1000),
    )(code, arrived, part, table, *filled)


AXES = ("rows", "mask")
CHUNKS = 2


def exchange(blocks):
    flat = blocks.reshape((-1,) + blocks.shape[-3:])
    flat = lax.all_to_all(flat, AXES, split_axis=0, concat_axis=0, tiled=True)
    return flat.reshape(blocks.shape)


def add_over(value, devices, factor, stride):
    total = value
    for d in range(1, factor):
        pairs = []
        for i in range(devices):
            digit = i // stride % factor
            pairs.append((i, i + ((digit + d) % factor - digit) * stride))
        total = total + lax.ppermute(value, AXES, pairs)
    return total


def shards(slots, masks, image, measured, mask_ids):
    forward, backward = (jnp.asarray(table) for table in table_pair())
    _, count, width = image.shape
    devices = slots * masks
    radix = OUTER // slots
    each = radix // CHUNKS
    kept = [tuple(range(c * each, (c + 1) * each)) for c in range(CHUNKS)]
    by_slot = (slots, radix, 2 * INNER, 2 * INNER)
    out_table, in_table = backward.reshape(by_slot), forward.reshape(by_slot)
    ids = [mask_ids] + [
        lax.ppermute(mask_ids, "mask", [((m + d) % masks, m) for m in range(masks)])
        for d in range(1, masks)
    ]
    whole = [(0, count)]
    head, tail = whole, whole
    if count >= 2 * INNER:
        small = 2 * TILE
        head = [(0, small), (small, count - small)]
        tail = [(0, count - small), (count - small, small)]

    def forth(c, pieces, image, with_code):
        arrived = []
        for piece in pieces:
            sent, *code = rows_out(kept[c], ids, image, out_table, with_code, piece)
            sent, image = lax.optimization_barrier((sent, image))
            if arrived:
                sent, arrived[-1] = lax.optimization_barrier((sent, arrived[-1]))
            arrived.append(exchange(sent.reshape((-1,) + sent.shape[2:])))
        return arrived, code, image

    def back(blocks):
        arrived = exchange(blocks)
        return arrived.reshape((slots, masks) + blocks.shape[1:])

    arrived, _, image = forth(0, head, image, False)
    (leaving,), loss_early = columns(0, arrived, whole, measured, forward, backward)
    arrived, (code,), image = forth(1, whole, image, True)
    leaving_last, loss_late = columns(1, arrived, tail, measured, forward, backward)
    first = 1 << (3 * devices.bit_length() // 5)
    loss = (jnp.sum(loss_early) + jnp.sum(loss_late)).reshape(1)
    loss = add_over(loss, devices, first, 1)
    returned, loss = lax.optimization_barrier((back(leaving), loss))
    loss = add_over(loss, devices, devices // first, first)
    leaving_last, loss = lax.optimization_barrier((leaving_last, loss))
    part = rows_part(kept[0], returned, in_table)
    last = ()
    filled = ()
    for piece, blocks in zip(tail, leaving_last):
        if piece != tail[0]:
            blocks, last, part = lax.optimization_barrier((blocks, last, part))
        last = back(blocks)
        filled = (rows_in(kept[1], code, last, part, in_table, piece, filled),)
    return filled[0], loss[0] / (masks * width * width)


def solution(mesh):
    slots, masks = mesh.shape["rows"], mesh.shape["mask"]
    return jax.shard_map(
        functools.partial(shards, slots, masks),
        mesh=mesh,
        in_specs=(P(None, AXES, None), P("mask", None, "rows"), P("mask")),
        out_specs=(P(None, AXES, None), P()),
        check_vma=False,
    )
```
